32 devices in a mesh: grp: 2 (over y), row: 4 (over z), sib: 4 (over x, core).
Axes of the slice: x: 2, y: 2, z: 4, core: 2. Of those that a mesh axis runs over, the one named last changes fastest.
Arguments:
- basis_fine: float32 [32768, 512], P(('grp', 'sib', 'row')), parts along dimension 0, may hold values from -6 to 6
- dual_fine: float32 [32768, 512], P(('grp', 'sib', 'row')), parts along dimension 0, may hold values from -1 to 1
- basis_coarse: float32 [32768, 512], P(('grp', 'sib', 'row')), parts along dimension 0, may hold values from -6 to 6
- dual_coarse: float32 [32768, 512], P(('grp', 'sib', 'row')), parts along dimension 0, may hold values from -1 to 1
- right_side: float32 [32768, 128], P(('grp', 'sib', 'row')), parts along dimension 0, may hold values from -6 to 6
- pattern: int32 [256, 4], P(('grp', 'sib', 'row')), parts along dimension 0, may hold values 0 or 1
Outputs:
- coarse_basis: float32 [32768, 512], P(('grp', 'sib', 'row')), parts along dimension 0
- solution: float32 [32768, 128], P(('grp', 'sib', 'row')), parts along dimension 0
The draws below stay inside these ranges and needn't reach their ends.
There are 2 independent parts, one for each index of `grp`. The reference program is written for one: setup_inputs(seed, part) draws one part's arguments, and reference() takes and returns one part's arrays. A program takes and returns all parts, laid end to end along the dimension named above; each array names one. Nothing has to cross between parts.
Inputs may be any that keep to these rules, and one draw needn't show every extreme that they name: `pattern`: 1 where the block of basis_fine is present, 0 where it is absent.
All inputs are finite; a program needn't handle non-finite values.
Results may differ from the reference program's by a relative error of at most 0.00007.
Values sent between devices are 32-bit elements; how exact they have to be, the bound alone decides.
No kernel may reach another device: no remote copies, remote signals or barrier semaphores. Data moves between devices by JAX's collectives and lax.ppermute only.
A program may use at most 128 MiB of HBM per device.

```python
import math
import jax
import jax.numpy as jnp
import numpy as np
from jax import lax

RANK = 512
BLK = 128
NRHS = 128
ROWS_DEV = 1024
ROWS = 16384
N_ROW = 4
N_SIB = 4


def shared_field(key, tag, gain_low, gain_high, node_rows, density):
    key = jax.random.fold_in(key, tag)
    entry_key = jax.random.fold_in(key, 0)
    gain_key = jax.random.fold_in(key, 2)
    sign_key = jax.random.fold_in(key, 3)
    entries = jax.random.truncated_normal(entry_key, -6.0, 6.0, (ROWS, RANK), jnp.float32)
    entries = jnp.clip(entries, -6.0, 6.0)
    node_count = ROWS // node_rows
    node_gains = jnp.exp(jax.random.uniform(gain_key, (node_count,), jnp.float32, math.log(gain_low), math.log(gain_high)))
    pair_signs = jnp.where(jax.random.bernoulli(sign_key, 0.5, (node_count // 2,)), 1.0, -1.0).astype(jnp.float32)
    node_index = jnp.arange(node_count)
    parity = (node_index % 2).astype(jnp.float32)
    node_signs = jnp.repeat(pair_signs, 2) * (1.0 - 2.0 * parity)
    row_gains = jnp.repeat(node_signs * node_gains / (density * node_rows), node_rows)[:, None]
    return (entries, row_gains)


def draw_basis_fine(key, part):
    entries, row_gains = shared_field(key, 11, 1.0, 2.5, ROWS_DEV * N_ROW, 0.75)
    return entries


def draw_dual_fine(key, part):
    entries, row_gains = shared_field(key, 11, 1.0, 2.5, ROWS_DEV * N_ROW, 0.75)
    key = jax.random.fold_in(key, 12)
    noise = jax.random.truncated_normal(key, -6.0, 6.0, (ROWS, RANK), jnp.float32)
    return row_gains * (entries + 0.3 * noise)


def draw_basis_coarse(key, part):
    entries, row_gains = shared_field(key, 21, 1.0, 2.5, 2 * ROWS_DEV * N_ROW, 1.0)
    return entries


def draw_dual_coarse(key, part):
    entries, row_gains = shared_field(key, 21, 1.0, 2.5, 2 * ROWS_DEV * N_ROW, 1.0)
    key = jax.random.fold_in(key, 22)
    noise = jax.random.truncated_normal(key, -6.0, 6.0, (ROWS, RANK), jnp.float32)
    return row_gains * (entries + 0.3 * noise)


def set_ends(result, key, low, high):
    shape = result.shape
    index_at = [jax.random.randint(jax.random.fold_in(key, axis), (), 0, shape[axis]) for axis in range(len(shape))]
    result = result.at[tuple(index_at)].set(low)
    longest = shape.index(max(shape))
    index_at[longest] = (index_at[longest] + 1) % shape[longest]
    return result.at[tuple(index_at)].set(high)


def level_of(own_key, dims, cuts, least, top_value):
    level, own = 1.0, jax.random.fold_in(own_key, 6)
    for axis_at, parts in cuts:
        heights = jnp.exp(jax.random.uniform(jax.random.fold_in(own, axis_at), (parts,), jnp.float32, least / len(cuts), top_value / len(cuts)))
        level = level * jnp.repeat(heights, dims[axis_at] // parts).reshape([-1 if axis == axis_at else 1 for axis in range(len(dims))])
    return level


def bell_draw(own_key, dims, scale, bound, pieces=(), kind=jnp.bfloat16):
    result = jax.random.normal(own_key, dims, jnp.float32) * scale
    if len(pieces) > 0:
        result = level_of(own_key, dims, pieces, -0.22, 0.18) * result
    return jnp.clip(result, min=-bound, max=bound).astype(kind)


def setup_inputs(seed: int = 0, part: int = 0) -> dict:
    key_of = jax.random.split(jax.random.key(seed), 7)
    part_keys = jax.random.split(jax.random.fold_in(key_of[6], part), 7)
    basis_fine = draw_basis_fine(jax.random.fold_in(jax.random.fold_in(key_of[6], part), 71), part)
    dual_fine = draw_dual_fine(jax.random.fold_in(jax.random.fold_in(key_of[6], part), 71), part)
    basis_coarse = draw_basis_coarse(jax.random.fold_in(jax.random.fold_in(key_of[6], part), 71), part)
    dual_coarse = draw_dual_coarse(jax.random.fold_in(jax.random.fold_in(key_of[6], part), 71), part)
    right_side = bell_draw(part_keys[4], (ROWS, NRHS), 1.0, 6.0, ((0, 16),), jnp.float32)
    pattern = set_ends((jax.random.randint(part_keys[5], (ROWS // BLK, RANK // BLK), 0, 4) < 3).astype(jnp.int32), jax.random.fold_in(part_keys[5], 1), 0, 1)
    return dict(basis_fine=basis_fine, dual_fine=dual_fine, basis_coarse=basis_coarse, dual_coarse=dual_coarse, right_side=right_side, pattern=pattern)


HIGH = lax.Precision.HIGHEST

def product(left, right):
    return jnp.dot(left.astype(jnp.float32), right.astype(jnp.float32), precision=HIGH, preferred_element_type=jnp.float32)

def couple_solve(gram_own, gram_sib, moment_own, moment_sib):
    identity = jnp.eye(gram_own.shape[0], dtype=jnp.float32)
    coupling = identity - product(gram_sib, gram_own)
    normal = product(coupling.T, coupling)
    factor = jnp.linalg.cholesky(normal)
    target = product(coupling.T, moment_sib - product(gram_sib, moment_own))
    first = lax.linalg.triangular_solve(factor, target, left_side=True, lower=True)
    return lax.linalg.triangular_solve(factor, first, left_side=True, lower=True, transpose_a=True)

def contract(left, right):
    return jnp.einsum('knr,knc->krc', left.astype(jnp.float32), right.astype(jnp.float32), precision=HIGH, preferred_element_type=jnp.float32)

def expand(left, right):
    return jnp.einsum('knr,krc->knc', left.astype(jnp.float32), right.astype(jnp.float32), precision=HIGH, preferred_element_type=jnp.float32)

def reference(basis_fine, dual_fine, basis_coarse, dual_coarse, right_side, pattern):
    nodes = N_SIB
    node_rows = ROWS // nodes
    widths = RANK + NRHS
    mask = jnp.repeat(jnp.repeat(pattern.astype(jnp.float32), BLK, axis=0), BLK, axis=1)
    masked = (basis_fine * mask).reshape(nodes, node_rows, RANK)
    dual = dual_fine.reshape(nodes, node_rows, RANK)
    work = jnp.concatenate([basis_coarse, right_side], axis=1).reshape(nodes, node_rows, widths)
    gram = contract(dual, masked)
    moment = contract(dual, work)
    partner = np.arange(nodes) ^ 1
    coeffs = jax.vmap(couple_solve)(gram, gram[partner], moment, moment[partner])
    work = work - expand(masked, coeffs)
    work = work.reshape(nodes // 2, 2 * node_rows, widths)
    basis = work[:, :, :RANK]
    updated = work[:, :, RANK:]
    dual_top = dual_coarse.reshape(nodes // 2, 2 * node_rows, RANK)
    gram_top = contract(dual_top, basis)
    moment_top = contract(dual_top, updated)
    partner_top = np.arange(nodes // 2) ^ 1
    coeffs_top = jax.vmap(couple_solve)(gram_top, gram_top[partner_top], moment_top, moment_top[partner_top])
    solution = updated - expand(basis, coeffs_top)
    return (basis.reshape(ROWS, RANK), solution.reshape(ROWS, NRHS))
```

```python
import jax
import jax.numpy as jnp
from jax import lax
from jax.experimental import pallas as pl
from jax.experimental.pallas import tpu as pltpu
from jax.sharding import PartitionSpec as P

BLK = 128
HIGH = lax.Precision.HIGHEST
SUB, LANE = 8, 128

def block_inverse(block):
    size = block.shape[0]
    shape = (SUB, size)
    sub = lax.broadcasted_iota(jnp.int32, shape, 0)
    lane = lax.broadcasted_iota(jnp.int32, shape, 1)
    groups = size // SUB
    rows = [block[SUB * g : SUB * (g + 1), :] for g in range(groups)]
    down = lambda value, at: jnp.broadcast_to(value[at : at + 1, :], shape)
    across = lambda value, at: jnp.broadcast_to(value[:, at : at + 1], shape)
    for g in range(groups):
        first = SUB * g
        panel = rows[g]
        heads = [across(panel, first + j) for j in range(SUB)]
        for s in range(SUB):
            scale = 1.0 / down(heads[s], s)
            factor = heads[s]
            top = jnp.where(lane == first + s, scale, down(panel, s) * scale)
            rest = jnp.where(lane == first + s, 0.0, panel)
            panel = jnp.where(sub == s, top, rest - factor * top)
            for j in range(s + 1, SUB):
                head = down(heads[j], s) * scale
                heads[j] = jnp.where(sub == s, head, heads[j] - factor * head)
        rows[g] = panel
        tops = [down(panel, j) for j in range(SUB)]
        inside = (lane >= first) & (lane < first + SUB)
        for h in range(groups):
            if h != g:
                total = jnp.where(inside, 0.0, rows[h])
                for j in range(SUB):
                    total = total - across(rows[h], first + j) * tops[j]
                rows[h] = total
    return jnp.concatenate(rows, axis=0)

def dot(left, right, dims):
    return lax.dot_general(left, right, (dims, ((), ())), precision=HIGH, preferred_element_type=jnp.float32)

def inverse_kernel(own_ref, sib_ref, out_ref, c_ref, a_ref):
    rank = own_ref.shape[0]
    row = lax.broadcasted_iota(jnp.int32, (rank, rank), 0)
    col = lax.broadcasted_iota(jnp.int32, (rank, rank), 1)
    c_ref[...] = jnp.where(row == col, 1.0, 0.0) - dot(sib_ref[...], own_ref[...], ((1,), (0,)))
    a_ref[...] = dot(c_ref[...], c_ref[...], ((1,), (1,)))

    def step(j, carry):
        here = pl.ds(pl.multiple_of(j * LANE, LANE), LANE)
        inv = block_inverse(a_ref[here, here])
        a_ref[here, here] = jnp.zeros((LANE, LANE), jnp.float32)
        top = dot(inv, a_ref[here, :], ((1,), (0,)))
        side = a_ref[:, here]
        a_ref[:, here] = jnp.zeros((rank, LANE), jnp.float32)
        a_ref[here, :] = top
        a_ref[here, here] = inv
        a_ref[...] = a_ref[...] - dot(side, a_ref[here, :], ((1,), (0,)))
        return carry

    lax.fori_loop(0, rank // LANE, step, 0)
    out_ref[...] = dot(a_ref[...], c_ref[...], ((1,), (0,)))

def coupling_inverse(own, sib):
    rank = own.shape[0]
    whole = pl.BlockSpec(memory_space=pltpu.VMEM)
    return pl.pallas_call(
        inverse_kernel,
        out_shape=jax.ShapeDtypeStruct((rank, rank), jnp.float32),
        in_specs=[whole, whole], out_specs=whole,
        scratch_shapes=[pltpu.VMEM((rank, rank), jnp.float32)] * 2,
        compiler_params=pltpu.CompilerParams(vmem_limit_bytes=32 << 20),
    )(own, sib)


def swapped(value, axis, distance):
    mask = 2**distance
    pairs = [(source, source ^ mask) for source in range(lax.axis_size(axis))]
    return lax.ppermute(value, axis, pairs)


def product(left, right):
    return dot(left, right, ((1,), (0,)))


def contract(left, right):
    return dot(left, right, ((0,), (0,)))


def shards(basis_fine, dual_fine, basis_coarse, dual_coarse, right_side, pattern):
    mask = jnp.repeat(jnp.repeat(pattern.astype(jnp.float32), BLK, axis=0), BLK, axis=1)
    masked = basis_fine * mask
    gram_own = lax.psum(contract(dual_fine, masked), "row")
    work = jnp.concatenate([basis_coarse, right_side], axis=1)
    moment_own = lax.psum(contract(dual_fine, work), "row")
    gram_sib = swapped(gram_own, "sib", 0)
    inverse = coupling_inverse(gram_own, gram_sib)
    moment_sib = swapped(moment_own, "sib", 0)
    coeffs = contract(inverse, moment_sib - product(gram_sib, moment_own))
    basis = basis_coarse - product(masked, coeffs[:, : basis_fine.shape[1]])
    updated = right_side - product(masked, coeffs[:, basis_fine.shape[1] :])
    gram_half, moment_half = lax.psum(
        (contract(dual_coarse, basis), contract(dual_coarse, updated)), "row"
    )
    gram_pair, moment_pair = swapped((gram_half, moment_half), "sib", 0)
    gram_top = gram_half + gram_pair
    moment_top = moment_half + moment_pair
    gram_far, moment_far = swapped((gram_top, moment_top), "sib", 1)
    inverse_top = coupling_inverse(gram_top, gram_far)
    coeffs_top = contract(inverse_top, moment_far - product(gram_far, moment_top))
    solution = updated - product(basis, coeffs_top)
    return (basis, solution)


def solution(mesh):
    rows = P(("grp", "sib", "row"), None)
    return jax.shard_map(
        shards,
        mesh=mesh,
        in_specs=(rows,) * 6,
        out_specs=(rows, rows),
        check_vma=False,
    )
```

```python
import functools

import jax
import jax.numpy as jnp
from jax import lax
from jax.experimental import pallas as pl
from jax.experimental.pallas import tpu as pltpu
from jax.sharding import PartitionSpec as P

BLK = 128
SUB, LANE = 8, 128
PIECES = 4
HIGH = lax.Precision.HIGHEST
WHOLE = pl.BlockSpec(memory_space=pltpu.VMEM)
SCALARS = pl.BlockSpec(memory_space=pltpu.SMEM)
VMEM_LIMIT = 40 << 20


def dot(left, right, dims):
    return lax.dot_general(left, right, (dims, ((), ())), precision=HIGH, preferred_element_type=jnp.float32)


def product(left, right):
    return dot(left, right, ((1,), (0,)))


def contract(left, right):
    return dot(left, right, ((0,), (0,)))


def block_inverse(block):
    size = block.shape[0]
    shape = (SUB, size)
    sub = lax.broadcasted_iota(jnp.int32, shape, 0)
    lane = lax.broadcasted_iota(jnp.int32, shape, 1)
    groups = size // SUB
    rows = [block[SUB * g : SUB * (g + 1), :] for g in range(groups)]
    down = lambda value, at: jnp.broadcast_to(value[at : at + 1, :], shape)
    across = lambda value, at: jnp.broadcast_to(value[:, at : at + 1], shape)
    for g in range(groups):
        first = SUB * g
        panel = rows[g]
        heads = [across(panel, first + j) for j in range(SUB)]
        for s in range(SUB):
            scale = 1.0 / down(heads[s], s)
            factor = heads[s]
            top = jnp.where(lane == first + s, scale, down(panel, s) * scale)
            rest = jnp.where(lane == first + s, 0.0, panel)
            panel = jnp.where(sub == s, top, rest - factor * top)
            for j in range(s + 1, SUB):
                head = down(heads[j], s) * scale
                heads[j] = jnp.where(sub == s, head, heads[j] - factor * head)
        rows[g] = panel
        tops = [down(panel, j) for j in range(SUB)]
        inside = (lane >= first) & (lane < first + SUB)
        for h in range(groups):
            if h != g:
                total = jnp.where(inside, 0.0, rows[h])
                for j in range(SUB):
                    total = total - across(rows[h], first + j) * tops[j]
                rows[h] = total
    return jnp.concatenate(rows, axis=0)


def eliminate(a_ref, start, stop):
    rank = a_ref.shape[0]

    def step(j, carry):
        here = pl.ds(pl.multiple_of(j * LANE, LANE), LANE)
        inv = block_inverse(a_ref[here, here])
        a_ref[here, here] = jnp.zeros((LANE, LANE), jnp.float32)
        top = product(inv, a_ref[here, :])
        side = a_ref[:, here]
        a_ref[:, here] = jnp.zeros((rank, LANE), jnp.float32)
        a_ref[here, :] = top
        a_ref[here, here] = inv
        a_ref[...] = a_ref[...] - product(side, a_ref[here, :])
        return carry

    lax.fori_loop(start, stop, step, 0)


def identity_less(value):
    row = lax.broadcasted_iota(jnp.int32, value.shape, 0)
    col = lax.broadcasted_iota(jnp.int32, value.shape, 1)
    return jnp.where(row == col, 1.0, 0.0) - value


def call(kernel, inputs, outputs, scratch=(), scalars=0, flops=0, aliases=None):
    return pl.pallas_call(
        kernel,
        out_shape=[jax.ShapeDtypeStruct(shape, jnp.float32) for shape in outputs],
        in_specs=[SCALARS] * scalars + [WHOLE] * (len(inputs) - scalars),
        out_specs=[WHOLE] * len(outputs),
        scratch_shapes=[pltpu.VMEM(shape, jnp.float32) for shape in scratch],
        input_output_aliases=aliases or {},
        cost_estimate=pl.CostEstimate(flops=flops, bytes_accessed=8 << 20, transcendentals=0),
        compiler_params=pltpu.CompilerParams(vmem_limit_bytes=VMEM_LIMIT),
    )(*inputs)


def gather_rows(pieces, whole_ref):
    at = 0
    for piece in pieces:
        whole_ref[at : at + piece.shape[0], :] = piece[...]
        at += piece.shape[0]


def fine_open(own, sib, flops):
    rank = own[0].shape[1]
    count = len(own)

    def kernel(*refs):
        own_refs, sib_refs = refs[:count], refs[count : 2 * count]
        c_ref, a_ref, far_ref, own_ref = refs[2 * count :]
        gather_rows(own_refs, own_ref)
        gather_rows(sib_refs, far_ref)
        c_ref[...] = identity_less(product(far_ref[...], own_ref[...]))
        a_ref[...] = dot(c_ref[...], c_ref[...], ((1,), (1,)))

    square = (rank, rank)
    return call(kernel, [*own, *sib], [square] * 3, [square], flops=flops)


def fine_step(a, step, flops):
    def kernel(in_ref, a_ref):
        a_ref[...] = in_ref[...]
        eliminate(a_ref, step, step + 1)

    return call(kernel, [a], [a.shape], flops=flops)[0]


def fine_close(a, c, step, flops):
    def kernel(in_ref, c_ref, out_ref, a_ref):
        a_ref[...] = in_ref[...]
        eliminate(a_ref, step, step + 1)
        out_ref[...] = product(a_ref[...], c_ref[...])

    return call(kernel, [a, c], [a.shape], [a.shape], flops=flops)[0]


def fine_coeffs(inverse, gram_sib, own, sib):
    count = len(own)
    rank, width = gram_sib.shape[0], own[0].shape[1]

    def kernel(*refs):
        inv_ref, gram_ref = refs[:2]
        own_refs, sib_refs = refs[2 : 2 + count], refs[2 + count : 2 + 2 * count]
        out_ref, own_ref, far_ref = refs[2 + 2 * count :]
        gather_rows(own_refs, own_ref)
        gather_rows(sib_refs, far_ref)
        far_ref[...] = far_ref[...] - product(gram_ref[...], own_ref[...])
        out_ref[...] = contract(inv_ref[...], far_ref[...])

    wide = (rank, width)
    return call(kernel, [inverse, gram_sib, *own, *sib], [wide], [wide, wide], flops=4 * rank * rank * width * 6)[0]


def top_coeffs(core, mine, other, far_mine, far_other):
    count = len(mine)
    piece, width = mine[0].shape
    rank = 2 * count * piece
    nrhs = width - rank

    def kernel(core_ref, *refs):
        lists = [refs[count * i : count * (i + 1)] for i in range(4)]
        out_ref, own_ref, far_ref, c_ref, a_ref, t_ref = refs[4 * count :]
        half = rank // 2
        for at, (first, second), whole_ref in ((0, lists[:2], own_ref), (0, lists[2:], far_ref)):
            for side, pieces in ((core_ref[0], first), (1 - core_ref[0], second)):
                for q, part in enumerate(pieces):
                    start = pl.multiple_of(side * half + q * piece, piece)
                    whole_ref[pl.ds(start, piece), :] = part[...]
        c_ref[...] = identity_less(product(far_ref[:, :rank], own_ref[:, :rank]))
        t_ref[...] = far_ref[:, rank:] - product(far_ref[:, :rank], own_ref[:, rank:])
        a_ref[...] = dot(c_ref[...], c_ref[...], ((1,), (1,)))
        eliminate(a_ref, 0, rank // LANE)
        t_ref[...] = product(a_ref[...], t_ref[...])
        out_ref[...] = contract(c_ref[...], t_ref[...])

    square, wide = (rank, rank), (rank, width)
    return call(
        kernel,
        [core, *mine, *other, *far_mine, *far_other],
        [(rank, nrhs)],
        [wide, wide, square, square, (rank, nrhs)],
        scalars=1,
        flops=1 << 32,
    )[0]


def swapped(value, axis, distance):
    mask = 2**distance
    pairs = [(source, source ^ mask) for source in range(lax.axis_size(axis))]
    return lax.ppermute(value, axis, pairs)


def after(value, *others):
    return lax.optimization_barrier((value, *others))[0]


def hop_count(axis):
    return 2 * (lax.axis_size(axis) // 2) - 1


def hop_pairs(axis, hop):
    size = lax.axis_size(axis)
    half = size // 2
    if hop == half - 1:
        return [(half - 1, half), (half, half - 1)]
    if hop < half - 1:
        return [(hop, hop + 1), (size - 1 - hop, size - 2 - hop)]
    t = 2 * half - 2 - hop
    return [(t + 1, t), (size - 2 - t, size - 1 - t)]


def leave(value, axis, hop):
    return lax.ppermute(value, axis, hop_pairs(axis, hop))


def arrive(value, arrived, axis, hop):
    size = lax.axis_size(axis)
    if hop < size // 2:
        return value + arrived
    here = lax.axis_index(axis)
    t = 2 * (size // 2) - 2 - hop
    return jnp.where((here == t) | (here == size - 1 - t), arrived, value)


class Line:
    def __init__(self, pieces, axis):
        self.values, self.axis = list(pieces), axis
        self.flying = [None] * len(self.values)
        self.slot = 0
        self.hops = hop_count(axis)

    def advance(self, token=None):
        settled = []
        for i in range(len(self.values)):
            hop = self.slot - i
            if 1 <= hop <= self.hops:
                value = self.values[i] if token is None else after(self.values[i], token)
                self.values[i] = arrive(value, self.flying[i], self.axis, hop - 1)
                settled.append(self.values[i])
                if hop < self.hops:
                    self.flying[i] = leave(self.values[i], self.axis, hop)
        for i in range(len(self.values)):
            if self.slot == max(0, i - 1):
                if token is not None:
                    self.values[i] = after(self.values[i], token)
                self.flying[i] = leave(self.values[i], self.axis, 0)
        self.slot += 1
        return settled

    def finish(self):
        while self.slot < len(self.values) + self.hops:
            self.advance()
        return self.values


def line_sums(values, axis):
    result = []
    for value in values:
        for hop in range(hop_count(axis)):
            value = arrive(value, leave(value, axis, hop), axis, hop)
        result.append(value)
    return result


def column_pieces(array, count):
    width = array.shape[1] // count
    return [array[:, width * i : width * (i + 1)] for i in range(count)]


def shards(basis_fine, dual_fine, basis_coarse, dual_coarse, right_side, pattern):
    rank = basis_fine.shape[1]
    step_flops = 8 << 30
    mask = jnp.repeat(jnp.repeat(pattern.astype(jnp.float32), BLK, axis=0), BLK, axis=1)
    masked = basis_fine * mask
    duals = column_pieces(dual_fine, PIECES)
    work = jnp.concatenate([basis_coarse, right_side], axis=1)
    gram = [contract(dual, masked) for dual in duals]
    moment = Line([contract(dual, work) for dual in duals], "row")
    hops = hop_count("row")
    for hop in range(hops):
        gram = [arrive(piece, leave(piece, "row", hop), "row", hop) for piece in gram]
        if hop < 2:
            settled = moment.advance(gram[-1])
    gram_sib = [swapped(piece, "sib", 0) for piece in gram]
    gram[0] = after(gram[0], *settled)
    coupling, normal, gram_sib = fine_open(gram, gram_sib, step_flops)
    for step in range(rank // LANE):
        normal = after(normal, *moment.advance(normal))
        if step < rank // LANE - 1:
            normal = fine_step(normal, step, step_flops)
        else:
            inverse = fine_close(normal, coupling, step, step_flops)
    moment_own = moment.finish()
    moment_sib = [swapped(piece, "sib", 0) for piece in moment_own]
    coeffs = fine_coeffs(inverse, gram_sib, moment_own, moment_sib)
    basis = basis_coarse - product(masked, coeffs[:, :rank])
    updated = right_side - product(masked, coeffs[:, rank:])

    core = lax.axis_index("sib") % 2
    half = rank // 2
    both = jnp.concatenate([basis, updated], axis=1)
    keep = lax.dynamic_slice_in_dim(dual_coarse, core * half, half, 1)
    send = lax.dynamic_slice_in_dim(dual_coarse, (1 - core) * half, half, 1)
    arrived = swapped(contract(send, both), "sib", 0)
    part = contract(keep, both) + arrived
    piece = half // PIECES
    parts = lax.optimization_barrier([part[piece * i : piece * (i + 1)] for i in range(PIECES)])
    mine = line_sums(parts, "row")
    far_mine = [swapped(value, "sib", 1) for value in mine]
    other = [swapped(value, "sib", 0) for value in mine]
    far_other = [swapped(value, "sib", 0) for value in far_mine]
    coeffs_top = top_coeffs(core[None], mine, other, far_mine, far_other)
    solution = updated - product(basis, coeffs_top)
    return (basis, solution)


def solution(mesh):
    rows = P(("grp", "sib", "row"), None)
    return jax.shard_map(
        shards,
        mesh=mesh,
        in_specs=(rows,) * 6,
        out_specs=(rows, rows),
        check_vma=False,
    )
```

```python
import jax
import jax.numpy as jnp
from jax import lax
from jax.experimental import pallas as pl
from jax.experimental.pallas import tpu as pltpu
from jax.sharding import PartitionSpec as P

BLK = 128
SUB, LANE = 8, 128
PIECES = 4
HIGH = lax.Precision.HIGHEST
WHOLE = pl.BlockSpec(memory_space=pltpu.VMEM)
SCALARS = pl.BlockSpec(memory_space=pltpu.SMEM)
VMEM_LIMIT = 40 << 20


def dot(left, right, dims):
    return lax.dot_general(left, right, (dims, ((), ())), precision=HIGH, preferred_element_type=jnp.float32)


def product(left, right):
    return dot(left, right, ((1,), (0,)))


def contract(left, right):
    return dot(left, right, ((0,), (0,)))


def block_inverse(block):
    size = block.shape[0]
    shape = (SUB, size)
    sub = lax.broadcasted_iota(jnp.int32, shape, 0)
    lane = lax.broadcasted_iota(jnp.int32, shape, 1)
    groups = size // SUB
    rows = [block[SUB * g : SUB * (g + 1), :] for g in range(groups)]
    down = lambda value, at: jnp.broadcast_to(value[at : at + 1, :], shape)
    across = lambda value, at: jnp.broadcast_to(value[:, at : at + 1], shape)
    for g in range(groups):
        first = SUB * g
        panel = rows[g]
        heads = [across(panel, first + j) for j in range(SUB)]
        for s in range(0, SUB, 2):
            pair = heads[s], heads[s + 1]
            mid = down(pair[0], s + 1)
            low, high = down(pair[0], s), down(pair[1], s + 1)
            scale = 1.0 / (low * high - mid * mid)
            ends, cross = (high * scale, low * scale), -mid * scale
            solve = lambda first_row, second_row: (
                ends[0] * first_row + cross * second_row,
                cross * first_row + ends[1] * second_row,
            )
            place = lambda value, tops: jnp.where(
                sub == s,
                tops[0],
                jnp.where(sub == s + 1, tops[1], value - pair[0] * tops[0] - pair[1] * tops[1]),
            )
            here = (lane == first + s) | (lane == first + s + 1)
            tops = solve(down(panel, s), down(panel, s + 1))
            tops = (
                jnp.where(here, jnp.where(lane == first + s, ends[0], cross), tops[0]),
                jnp.where(here, jnp.where(lane == first + s, cross, ends[1]), tops[1]),
            )
            panel = place(jnp.where(here, 0.0, panel), tops)
            for j in range(s + 2, SUB):
                heads[j] = place(heads[j], solve(down(heads[j], s), down(heads[j], s + 1)))
        rows[g] = panel
        tops = [down(panel, j) for j in range(SUB)]
        inside = (lane >= first) & (lane < first + SUB)
        for h in range(groups):
            if h != g:
                total = jnp.where(inside, 0.0, rows[h])
                for j in range(SUB):
                    total = total - across(rows[h], first + j) * tops[j]
                rows[h] = total
    return jnp.concatenate(rows, axis=0)


def eliminate(a_ref, start, stop):
    rank = a_ref.shape[0]

    def step(j, carry):
        here = pl.ds(pl.multiple_of(j * LANE, LANE), LANE)
        inv = block_inverse(a_ref[here, here])
        a_ref[here, here] = jnp.zeros((LANE, LANE), jnp.float32)
        top = product(inv, a_ref[here, :])
        side = a_ref[:, here]
        a_ref[:, here] = jnp.zeros((rank, LANE), jnp.float32)
        a_ref[here, :] = top
        a_ref[here, here] = inv
        a_ref[...] = a_ref[...] - product(side, a_ref[here, :])
        return carry

    lax.fori_loop(start, stop, step, 0)


def identity_less(value):
    row = lax.broadcasted_iota(jnp.int32, value.shape, 0)
    col = lax.broadcasted_iota(jnp.int32, value.shape, 1)
    return jnp.where(row == col, 1.0, 0.0) - value


def call(kernel, inputs, outputs, scratch=(), scalars=0, flops=0, aliases=None):
    return pl.pallas_call(
        kernel,
        out_shape=[jax.ShapeDtypeStruct(shape, jnp.float32) for shape in outputs],
        in_specs=[SCALARS] * scalars + [WHOLE] * (len(inputs) - scalars),
        out_specs=[WHOLE] * len(outputs),
        scratch_shapes=[pltpu.VMEM(shape, jnp.float32) for shape in scratch],
        input_output_aliases=aliases or {},
        cost_estimate=pl.CostEstimate(flops=flops, bytes_accessed=8 << 20, transcendentals=0),
        compiler_params=pltpu.CompilerParams(vmem_limit_bytes=VMEM_LIMIT),
    )(*inputs)


def gather_rows(pieces, whole_ref):
    at = 0
    for piece in pieces:
        whole_ref[at : at + piece.shape[0], :] = piece[...]
        at += piece.shape[0]


def fine_open(own, sib, flops):
    rank = own[0].shape[1]
    count = len(own)

    def kernel(*refs):
        own_refs, sib_refs = refs[:count], refs[count : 2 * count]
        c_ref, a_ref, far_ref, own_ref = refs[2 * count :]
        gather_rows(own_refs, own_ref)
        gather_rows(sib_refs, far_ref)
        c_ref[...] = identity_less(product(far_ref[...], own_ref[...]))
        a_ref[...] = dot(c_ref[...], c_ref[...], ((1,), (1,)))

    square = (rank, rank)
    return call(kernel, [*own, *sib], [square] * 3, [square], flops=flops)


def fine_close(a, c, flops):
    def kernel(in_ref, c_ref, out_ref, a_ref):
        a_ref[...] = in_ref[...]
        eliminate(a_ref, 0, a_ref.shape[0] // LANE)
        out_ref[...] = product(a_ref[...], c_ref[...])

    return call(kernel, [a, c], [a.shape], [a.shape], flops=flops)[0]


def split(value):
    high = value.astype(jnp.bfloat16)
    return high, (value - high.astype(jnp.float32)).astype(jnp.bfloat16)


def dot3(left, right, dims):
    part = lambda a, b: lax.dot_general(a, b, (dims, ((), ())), preferred_element_type=jnp.float32)
    return part(left[0], right[0]) + (part(left[0], right[1]) + part(left[1], right[0]))


def blocks_masked(pattern_ref, basis, at):
    rows = []
    for i in range(basis.shape[0] // BLK):
        here = basis[BLK * i : BLK * (i + 1), :]
        row = [
            here[:, BLK * j : BLK * (j + 1)] * pattern_ref[at + i, j].astype(jnp.float32)
            for j in range(basis.shape[1] // BLK)
        ]
        rows.append(jnp.concatenate(row, axis=1))
    return jnp.concatenate(rows, axis=0)


def fine_gram(pattern, basis, dual):
    rows, rank = basis.shape
    piece = rank // PIECES

    def kernel(pattern_ref, basis_ref, dual_ref, *out_refs):
        masked = blocks_masked(pattern_ref, basis_ref[...], 0)
        for i, out_ref in enumerate(out_refs):
            out_ref[...] = contract(dual_ref[:, piece * i : piece * (i + 1)], masked)

    return call(kernel, [pattern, basis, dual], [(piece, rank)] * PIECES, scalars=1, flops=12 * rows * rank * rank)


def fine_update(pattern, inverse, gram_sib, own, sib, basis, coarse, right):
    rank, nrhs = gram_sib.shape[0], right.shape[1]
    rows = basis.shape[0]
    tile = 2 * BLK

    def kernel(pattern_ref, inv_ref, gram_ref, *refs):
        own_refs, sib_refs = refs[:2], refs[2:4]
        basis_ref, coarse_ref, right_ref, new_ref, updated_ref = refs[4:]
        for own_ref, sib_ref, old_ref, out_ref in (
            (own_refs[0], sib_refs[0], coarse_ref, new_ref),
            (own_refs[1], sib_refs[1], right_ref, updated_ref),
        ):
            target = sib_ref[...] - product(gram_ref[...], own_ref[...])
            coeffs = split(contract(inv_ref[...], target))
            for t in range(rows // tile):
                here = slice(tile * t, tile * (t + 1))
                masked = split(blocks_masked(pattern_ref, basis_ref[here, :], t * (tile // BLK)))
                out_ref[here, :] = old_ref[here, :] - dot3(masked, coeffs, ((1,), (0,)))

    return call(
        kernel,
        [pattern, inverse, gram_sib, *own, *sib, basis, coarse, right],
        [(rows, rank), (rows, nrhs)],
        scalars=1,
        flops=6 * 2 * (rank + rows) * rank * (rank + nrhs),
    )


def coarse_part(which, dual, basis, updated):
    rows, rank = basis.shape
    nrhs = updated.shape[1]
    half = rank // 2

    def kernel(which_ref, dual_ref, basis_ref, updated_ref, out_ref):
        start = pl.multiple_of(which_ref[0] * half, half)
        left = split(dual_ref[:, pl.ds(start, half)])
        out_ref[:, :rank] = dot3(left, split(basis_ref[...]), ((0,), (0,)))
        out_ref[:, rank:] = dot3(left, split(updated_ref[...]), ((0,), (0,)))

    return call(
        kernel,
        [which, dual, basis, updated],
        [(half, rank + nrhs)],
        scalars=1,
        flops=6 * rows * half * (rank + nrhs),
    )[0]


def top_half(core, mine, other, far_mine, far_other):
    count = len(mine)
    piece, width = mine[0].shape
    rank = 2 * count * piece
    nrhs = width - rank
    half = rank // 2

    def kernel(core_ref, *refs):
        lists = [refs[count * i : count * (i + 1)] for i in range(4)]
        out_ref, own_ref, far_ref, c_ref, a_ref, t_ref = refs[4 * count :]
        for first, second, whole_ref in ((*lists[:2], own_ref), (*lists[2:], far_ref)):
            for side, pieces in ((core_ref[0], first), (1 - core_ref[0], second)):
                for q, part in enumerate(pieces):
                    start = pl.multiple_of(side * half + q * piece, piece)
                    whole_ref[pl.ds(start, piece), :] = part[...]
        c_ref[...] = identity_less(product(far_ref[:, :rank], own_ref[:, :rank]))
        t_ref[...] = far_ref[:, rank:] - product(far_ref[:, :rank], own_ref[:, rank:])
        a_ref[...] = dot(c_ref[...], c_ref[...], ((1,), (1,)))
        eliminate(a_ref, 0, rank // LANE)
        t_ref[...] = product(a_ref[...], t_ref[...])
        here = pl.ds(pl.multiple_of(core_ref[0] * half, half), half)
        out_ref[...] = contract(c_ref[:, here], t_ref[...])

    square, wide = (rank, rank), (rank, width)
    return call(
        kernel,
        [core, *mine, *other, *far_mine, *far_other],
        [(half, nrhs)],
        [wide, wide, square, square, (rank, nrhs)],
        scalars=1,
        flops=1 << 34,
    )[0]


def final_update(core, mine, other, basis, updated):
    rows, rank = basis.shape
    half, nrhs = mine.shape

    def kernel(core_ref, mine_ref, other_ref, basis_ref, updated_ref, out_ref, coeffs_ref):
        for side, part in ((core_ref[0], mine_ref), (1 - core_ref[0], other_ref)):
            coeffs_ref[pl.ds(pl.multiple_of(side * half, half), half), :] = part[...]
        out_ref[...] = updated_ref[...] - dot3(split(basis_ref[...]), split(coeffs_ref[...]), ((1,), (0,)))

    return call(
        kernel,
        [core, mine, other, basis, updated],
        [(rows, nrhs)],
        [(rank, nrhs)],
        scalars=1,
        flops=6 * rows * rank * nrhs,
    )[0]


def swapped(value, axis, distance):
    mask = 2**distance
    pairs = [(source, source ^ mask) for source in range(lax.axis_size(axis))]
    return lax.ppermute(value, axis, pairs)


def after(value, *others):
    return lax.optimization_barrier((value, *others))[0]


def hop_count(axis):
    return 2 * (lax.axis_size(axis) // 2) - 1


def hop_pairs(axis, hop):
    size = lax.axis_size(axis)
    half = size // 2
    if hop == half - 1:
        return [(half - 1, half), (half, half - 1)]
    if hop < half - 1:
        return [(hop, hop + 1), (size - 1 - hop, size - 2 - hop)]
    t = 2 * half - 2 - hop
    return [(t + 1, t), (size - 2 - t, size - 1 - t)]


def leave(value, axis, hop):
    return lax.ppermute(value, axis, hop_pairs(axis, hop))


def arrive(value, arrived, axis, hop):
    size = lax.axis_size(axis)
    if hop < size // 2:
        return value + arrived
    here = lax.axis_index(axis)
    t = 2 * (size // 2) - 2 - hop
    return jnp.where((here == t) | (here == size - 1 - t), arrived, value)


def shards(basis_fine, dual_fine, basis_coarse, dual_coarse, right_side, pattern):
    rank = basis_fine.shape[1]
    hops = hop_count("row")
    middle = hops // 2 + 1
    core = lax.axis_index("sib") % 2
    mine, other = core[None], (1 - core)[None]

    gram = fine_gram(pattern, basis_fine, dual_fine)
    moment = [
        lax.dot_general(
            dual_fine, right, (((0,), (0,)), ((), ())), precision=lax.Precision.HIGH,
            preferred_element_type=jnp.float32,
        )
        for right in (basis_coarse, right_side)
    ]
    for hop in range(hops):
        gram = [arrive(piece, leave(piece, "row", hop), "row", hop) for piece in gram]
        if hop == 0:
            *moment, _ = lax.optimization_barrier((*moment, gram[-1]))
            moment = lax.psum(moment, "row")
    gram_sib = [swapped(piece, "sib", 0) for piece in gram]
    coupling, normal, gram_sib = fine_open(gram, gram_sib, 1 << 30)
    inverse = fine_close(normal, coupling, 1 << 34)
    *moment, inverse = lax.optimization_barrier((*moment, inverse))
    moment_sib = [swapped(piece, "sib", 0) for piece in moment]
    basis, updated = fine_update(
        pattern, inverse, gram_sib, moment, moment_sib, basis_fine, basis_coarse, right_side
    )

    arrived = swapped(coarse_part(other, dual_coarse, basis, updated), "sib", 0)
    part = coarse_part(mine, dual_coarse, basis, updated) + arrived
    piece = rank // 2 // PIECES
    parts = lax.optimization_barrier([part[piece * i : piece * (i + 1)] for i in range(PIECES)])
    for hop in range(middle):
        parts = [arrive(value, leave(value, "row", hop), "row", hop) for value in parts]
    far = [swapped(value, "sib", 1) for value in parts]
    parts_other = [swapped(value, "sib", 0) for value in parts]
    far_other = [swapped(value, "sib", 0) for value in far]
    half = top_half(mine, parts, parts_other, far, far_other)
    for hop in range(middle, hops):
        half = arrive(half, leave(half, "row", hop), "row", hop)
    solution = final_update(mine, half, swapped(half, "sib", 0), basis, updated)
    return (basis, solution)


def solution(mesh):
    rows = P(("grp", "sib", "row"), None)
    return jax.shard_map(
        shards,
        mesh=mesh,
        in_specs=(rows,) * 6,
        out_specs=(rows, rows),
        check_vma=False,
    )
```

```python
import jax
import jax.numpy as jnp
from jax import lax
from jax.experimental import pallas as pl
from jax.experimental.pallas import tpu as pltpu
from jax.sharding import PartitionSpec as P

BLK = 128
SUB, LANE, PANEL = 8, 128, 32
PIECES = 4
TILE = 256
HIGH = lax.Precision.HIGHEST
WHOLE = pl.BlockSpec(memory_space=pltpu.VMEM)
SCALARS = pl.BlockSpec(memory_space=pltpu.SMEM)
VMEM_LIMIT = 40 << 20


def dot(left, right, dims):
    return lax.dot_general(left, right, (dims, ((), ())), precision=HIGH, preferred_element_type=jnp.float32)


def product(left, right):
    return dot(left, right, ((1,), (0,)))


def contract(left, right):
    return dot(left, right, ((0,), (0,)))


def block_inverse(block):
    size = block.shape[0]
    shape = (SUB, size)
    sub = lax.broadcasted_iota(jnp.int32, shape, 0)
    lane = lax.broadcasted_iota(jnp.int32, shape, 1)
    groups, tall = size // SUB, PANEL // SUB
    rows = [block[SUB * g : SUB * (g + 1), :] for g in range(groups)]
    down = lambda value, at: jnp.broadcast_to(value[at : at + 1, :], shape)
    across = lambda value, at: jnp.broadcast_to(value[:, at : at + 1], shape)
    for start in range(0, groups, tall):
        within = range(start, start + tall)
        for g in within:
            first = SUB * g
            panel = rows[g]
            heads = [across(panel, first + j) for j in range(SUB)]
            for s in range(0, SUB, 2):
                pair = heads[s], heads[s + 1]
                mid = down(pair[0], s + 1)
                low, high = down(pair[0], s), down(pair[1], s + 1)
                scale = 1.0 / (low * high - mid * mid)
                ends, cross = (high * scale, low * scale), -mid * scale
                solve = lambda first_row, second_row: (
                    ends[0] * first_row + cross * second_row,
                    cross * first_row + ends[1] * second_row,
                )
                place = lambda value, tops: jnp.where(
                    sub == s,
                    tops[0],
                    jnp.where(sub == s + 1, tops[1], value - pair[0] * tops[0] - pair[1] * tops[1]),
                )
                here = (lane == first + s) | (lane == first + s + 1)
                tops = solve(down(panel, s), down(panel, s + 1))
                tops = (
                    jnp.where(here, jnp.where(lane == first + s, ends[0], cross), tops[0]),
                    jnp.where(here, jnp.where(lane == first + s, cross, ends[1]), tops[1]),
                )
                panel = place(jnp.where(here, 0.0, panel), tops)
                for j in range(s + 2, SUB):
                    heads[j] = place(heads[j], solve(down(heads[j], s), down(heads[j], s + 1)))
            rows[g] = panel
            tops = [down(panel, j) for j in range(SUB)]
            inside = (lane >= first) & (lane < first + SUB)
            for h in within:
                if h != g:
                    terms = [across(rows[h], first + j) * tops[j] for j in range(SUB)]
                    while len(terms) > 1:
                        terms = [terms[i] + terms[i + 1] for i in range(0, len(terms), 2)]
                    rows[h] = jnp.where(inside, 0.0, rows[h]) - terms[0]
        inside = (lane >= SUB * start) & (lane < SUB * (start + tall))
        zero = jnp.zeros(shape, jnp.float32)
        side = [zero if h in within else jnp.where(inside, rows[h], 0.0) for h in range(groups)]
        top = [rows[h] if h in within else zero for h in range(groups)]
        less = product(jnp.concatenate(side, axis=0), jnp.concatenate(top, axis=0))
        for h in range(groups):
            if h not in within:
                rows[h] = jnp.where(inside, 0.0, rows[h]) - less[SUB * h : SUB * (h + 1), :]
    return jnp.concatenate(rows, axis=0)


def eliminate(a_ref, t_ref):
    rank = a_ref.shape[0]
    blocks = rank // LANE
    at = lambda j: slice(LANE * j, LANE * (j + 1))
    for j in range(blocks):
        rest = slice(LANE * (j + 1), rank)
        inv = block_inverse(a_ref[at(j), at(j)])
        others = [i for i in range(j + 1, blocks)] + [i for i in range(j)]
        if j < blocks - 1:
            top = product(inv, a_ref[at(j), rest])
            a_ref[at(j), rest] = top
            for i in others:
                a_ref[at(i), rest] = a_ref[at(i), rest] - product(a_ref[at(i), at(j)], top)
        top = product(inv, t_ref[at(j), :])
        t_ref[at(j), :] = top
        for i in others:
            t_ref[at(i), :] = t_ref[at(i), :] - product(a_ref[at(i), at(j)], top)


def identity_less(value):
    row = lax.broadcasted_iota(jnp.int32, value.shape, 0)
    col = lax.broadcasted_iota(jnp.int32, value.shape, 1)
    return jnp.where(row == col, 1.0, 0.0) - value


def call(kernel, inputs, outputs, scratch=(), scalars=0, flops=0, tiled=(), tiled_out=()):
    tiles = inputs[tiled[0]].shape[0] // TILE if tiled else 1
    by_rows = lambda shape: pl.BlockSpec((TILE, shape[1]), lambda t: (t, 0))
    whole = lambda shape: pl.BlockSpec(shape, lambda t: (0,) * len(shape))
    return pl.pallas_call(
        kernel,
        grid=(tiles,) if tiled else (),
        out_shape=[jax.ShapeDtypeStruct(shape, jnp.float32) for shape in outputs],
        in_specs=[
            SCALARS if i < scalars else by_rows(x.shape) if i in tiled else whole(x.shape) if tiled else WHOLE
            for i, x in enumerate(inputs)
        ],
        out_specs=[
            by_rows(shape) if i in tiled_out else whole(shape) if tiled else WHOLE
            for i, shape in enumerate(outputs)
        ],
        scratch_shapes=[
            pltpu.VMEM(shape, jnp.float32) if isinstance(shape, tuple) else shape for shape in scratch
        ],
        cost_estimate=pl.CostEstimate(flops=flops, bytes_accessed=8 << 20, transcendentals=0),
        compiler_params=pltpu.CompilerParams(vmem_limit_bytes=VMEM_LIMIT),
    )(*inputs)


def gather_rows(pieces, whole_ref):
    at = 0
    for piece in pieces:
        whole_ref[at : at + piece.shape[0], :] = piece[...]
        at += piece.shape[0]


def fine_inverse(own, sib, flops):
    rank = own[0].shape[1]
    count = len(own)

    def kernel(*refs):
        own_refs, sib_refs = refs[:count], refs[count : 2 * count]
        t_ref, far_ref, a_ref, own_ref = refs[2 * count :]
        gather_rows(own_refs, own_ref)
        gather_rows(sib_refs, far_ref)
        t_ref[...] = identity_less(product(far_ref[...], own_ref[...]))
        a_ref[...] = dot(t_ref[...], t_ref[...], ((1,), (1,)))
        eliminate(a_ref, t_ref)

    square = (rank, rank)
    return call(kernel, [*own, *sib], [square] * 2, [square] * 2, flops=flops)


def split(value):
    high = value.astype(jnp.bfloat16)
    return high, (value - high.astype(jnp.float32)).astype(jnp.bfloat16)


def dot3(left, right, dims):
    part = lambda a, b: lax.dot_general(a, b, (dims, ((), ())), preferred_element_type=jnp.float32)
    return part(left[0], right[0]) + (part(left[0], right[1]) + part(left[1], right[0]))


def blocks_masked(pattern_ref, basis, at):
    rows = []
    for i in range(basis.shape[0] // BLK):
        here = basis[BLK * i : BLK * (i + 1), :]
        row = [
            here[:, BLK * j : BLK * (j + 1)] * pattern_ref[at + i, j].astype(jnp.float32)
            for j in range(basis.shape[1] // BLK)
        ]
        rows.append(jnp.concatenate(row, axis=1))
    return jnp.concatenate(rows, axis=0)


def fine_gram(pattern, basis, dual):
    rows, rank = basis.shape
    piece = rank // PIECES

    def kernel(pattern_ref, basis_ref, dual_ref, *refs):
        out_refs, sum_ref = refs[:-1], refs[-1]
        t = pl.program_id(0)
        part = contract(dual_ref[...], blocks_masked(pattern_ref, basis_ref[...], t * (TILE // BLK)))
        sum_ref[...] = jnp.where(t == 0, part, sum_ref[...] + part)

        @pl.when(t == pl.num_programs(0) - 1)
        def _():
            for i, out_ref in enumerate(out_refs):
                out_ref[...] = sum_ref[piece * i : piece * (i + 1), :]

    return call(
        kernel,
        [pattern, basis, dual],
        [(piece, rank)] * PIECES,
        [(rank, rank)],
        scalars=1,
        flops=12 * rows * rank * rank,
        tiled=(1, 2),
    )


def fine_moment(dual, coarse, right):
    rows, rank = dual.shape

    def kernel(dual_ref, coarse_ref, right_ref, *out_refs):
        t = pl.program_id(0)
        left = split(dual_ref[...])
        for right_hand, out_ref in zip((coarse_ref, right_ref), out_refs):
            part = dot3(left, split(right_hand[...]), ((0,), (0,)))
            out_ref[...] = jnp.where(t == 0, part, out_ref[...] + part)

    return call(
        kernel,
        [dual, coarse, right],
        [(rank, coarse.shape[1]), (rank, right.shape[1])],
        flops=6 * rows * rank * (coarse.shape[1] + right.shape[1]),
        tiled=(0, 1, 2),
    )


def fine_update(which, pattern, inverse, gram_sib, own, sib, basis, coarse, right, dual):
    rank, nrhs = gram_sib.shape[0], right.shape[1]
    rows = basis.shape[0]
    half, width = rank // 2, rank + nrhs

    def kernel(which_ref, pattern_ref, inv_ref, gram_ref, *refs):
        own_refs, sib_refs = refs[:2], refs[2:4]
        basis_ref, coarse_ref, right_ref, dual_ref = refs[4:8]
        new_ref, updated_ref, keep_ref, send_ref, high_ref, low_ref = refs[8:]
        t = pl.program_id(0)
        columns = slice(0, rank), slice(rank, width)

        @pl.when(t == 0)
        def _():
            for own_ref, sib_ref, here in zip(own_refs, sib_refs, columns):
                target = sib_ref[...] - product(gram_ref[...], own_ref[...])
                high_ref[:, here], low_ref[:, here] = split(contract(inv_ref[...], target))

        masked = split(blocks_masked(pattern_ref, basis_ref[...], t * (TILE // BLK)))
        kept = pl.ds(pl.multiple_of(which_ref[0] * half, half), half)
        sent = pl.ds(pl.multiple_of((1 - which_ref[0]) * half, half), half)
        duals = split(dual_ref[:, kept]), split(dual_ref[:, sent])
        for old_ref, out_ref, here in zip((coarse_ref, right_ref), (new_ref, updated_ref), columns):
            new = old_ref[...] - dot3(masked, (high_ref[:, here], low_ref[:, here]), ((1,), (0,)))
            out_ref[...] = new
            new = split(new)
            for left, sum_ref in zip(duals, (keep_ref, send_ref)):
                part = dot3(left, new, ((0,), (0,)))
                sum_ref[:, here] = jnp.where(t == 0, part, sum_ref[:, here] + part)

    return call(
        kernel,
        [which, pattern, inverse, gram_sib, *own, *sib, basis, coarse, right, dual],
        [(rows, rank), (rows, nrhs), (half, width), (half, width)],
        [pltpu.VMEM((rank, width), jnp.bfloat16)] * 2,
        scalars=2,
        flops=12 * (rank + rows) * rank * width,
        tiled=(8, 9, 10, 11),
        tiled_out=(0, 1),
    )


def top_half(core, mine, other, far_mine, far_other):
    count = len(mine)
    half, width = sum(piece.shape[0] for piece in mine), mine[0].shape[1]
    rank = 2 * half
    nrhs = width - rank

    def kernel(core_ref, *refs):
        lists = [refs[count * i : count * (i + 1)] for i in range(4)]
        out_ref, own_ref, far_ref, c_ref, a_ref, t_ref = refs[4 * count :]
        for first, second, whole_ref in ((*lists[:2], own_ref), (*lists[2:], far_ref)):
            for side, pieces in ((core_ref[0], first), (1 - core_ref[0], second)):
                at = 0
                for part in pieces:
                    start = pl.multiple_of(side * half + at, SUB)
                    whole_ref[pl.ds(start, part.shape[0]), :] = part[...]
                    at += part.shape[0]
        c_ref[...] = identity_less(product(far_ref[:, :rank], own_ref[:, :rank]))
        t_ref[...] = far_ref[:, rank:] - product(far_ref[:, :rank], own_ref[:, rank:])
        a_ref[...] = dot(c_ref[...], c_ref[...], ((1,), (1,)))
        eliminate(a_ref, t_ref)
        here = pl.ds(pl.multiple_of(core_ref[0] * half, half), half)
        out_ref[...] = contract(c_ref[:, here], t_ref[...])

    square, wide = (rank, rank), (rank, width)
    return call(
        kernel,
        [core, *mine, *other, *far_mine, *far_other],
        [(half, nrhs)],
        [wide, wide, square, square, (rank, nrhs)],
        scalars=1,
        flops=1 << 34,
    )[0]


def final_update(core, mine, other, basis, updated):
    rows, rank = basis.shape
    half, nrhs = mine.shape

    def kernel(core_ref, mine_ref, other_ref, basis_ref, updated_ref, out_ref, coeffs_ref):
        @pl.when(pl.program_id(0) == 0)
        def _():
            for side, part in ((core_ref[0], mine_ref), (1 - core_ref[0], other_ref)):
                coeffs_ref[pl.ds(pl.multiple_of(side * half, half), half), :] = part[...]

        out_ref[...] = updated_ref[...] - dot3(split(basis_ref[...]), split(coeffs_ref[...]), ((1,), (0,)))

    return call(
        kernel,
        [core, mine, other, basis, updated],
        [(rows, nrhs)],
        [(rank, nrhs)],
        scalars=1,
        flops=6 * rows * rank * nrhs,
        tiled=(3, 4),
        tiled_out=(0,),
    )[0]


def swapped(value, axis, distance):
    mask = 2**distance
    pairs = [(source, source ^ mask) for source in range(lax.axis_size(axis))]
    return lax.ppermute(value, axis, pairs)


def after(value, *others):
    return lax.optimization_barrier((value, *others))[0]


def hop_count(axis):
    return 2 * (lax.axis_size(axis) // 2) - 1


def hop_pairs(axis, hop):
    size = lax.axis_size(axis)
    half = size // 2
    if hop == half - 1:
        return [(half - 1, half), (half, half - 1)]
    if hop < half - 1:
        return [(hop, hop + 1), (size - 1 - hop, size - 2 - hop)]
    t = 2 * half - 2 - hop
    return [(t + 1, t), (size - 2 - t, size - 1 - t)]


def leave(value, axis, hop):
    return lax.ppermute(value, axis, hop_pairs(axis, hop))


def arrive(value, arrived, axis, hop):
    size = lax.axis_size(axis)
    if hop < size // 2:
        return value + arrived
    here = lax.axis_index(axis)
    t = 2 * (size // 2) - 2 - hop
    return jnp.where((here == t) | (here == size - 1 - t), arrived, value)


def line_hops(values, axis, first, last, lag=None):
    values = list(values)
    for hop in range(first, last):
        moved = []
        for i, value in enumerate(values):
            if lag and i >= lag and hop == hop_count(axis) // 2:
                value = after(value, moved[i - lag])
            moved.append(arrive(value, leave(value, axis, hop), axis, hop))
        values = moved
    return values


def shards(basis_fine, dual_fine, basis_coarse, dual_coarse, right_side, pattern):
    rank = basis_fine.shape[1]
    half = rank // 2
    hops = hop_count("row")
    middle = hops // 2 + 1
    core = (lax.axis_index("sib") % 2)[None]

    gram = fine_gram(pattern, basis_fine, dual_fine)
    moment = fine_moment(after(dual_fine, gram[0]), basis_coarse, right_side)
    leaving = [leave(piece, "row", 0) for piece in gram]
    gram = lax.optimization_barrier((*gram, *moment))[: len(gram)]
    gram = [arrive(piece, arrived, "row", 0) for piece, arrived in zip(gram, leaving)]
    *moment, _ = lax.optimization_barrier((*moment, gram[1]))
    moment = lax.psum(moment, "row")
    gram = line_hops(gram, "row", 1, hops, lag=2)
    gram_sib = [swapped(piece, "sib", 0) for piece in gram]
    inverse, gram_sib = fine_inverse(gram, gram_sib, 1 << 28)
    *moment, inverse = lax.optimization_barrier((*moment, inverse))
    moment_sib = [swapped(piece, "sib", 0) for piece in moment]
    basis, updated, keep, send = fine_update(
        core, pattern, inverse, gram_sib, moment, moment_sib, basis_fine, basis_coarse, right_side, dual_coarse
    )

    part = keep + swapped(send, "sib", 0)
    cuts = [0, half * 3 // 8, half * 3 // 4, half]
    parts = lax.optimization_barrier([part[low:high] for low, high in zip(cuts, cuts[1:])])
    parts = line_hops(parts, "row", 0, middle)
    far = [swapped(value, "sib", 1) for value in parts]
    parts_other = [swapped(value, "sib", 0) for value in parts]
    far_other = [swapped(value, "sib", 0) for value in far]
    result = top_half(core, parts, parts_other, far, far_other)
    result = line_hops([result], "row", middle, hops)[0]
    solution = final_update(core, result, swapped(result, "sib", 0), basis, updated)
    return (basis, solution)


def solution(mesh):
    rows = P(("grp", "sib", "row"), None)
    return jax.shard_map(
        shards,
        mesh=mesh,
        in_specs=(rows,) * 6,
        out_specs=(rows, rows),
        check_vma=False,
    )
```

```python
import jax
import jax.numpy as jnp
from jax import lax
from jax.experimental import pallas as pl
from jax.experimental.pallas import tpu as pltpu
from jax.sharding import PartitionSpec as P

BLK = 128
SUB, LANE, PANEL = 8, 128, 32
PIECES = 4
TILE = 256
HIGH = lax.Precision.HIGHEST
WHOLE = pl.BlockSpec(memory_space=pltpu.VMEM)
FAR = pl.BlockSpec(memory_space=pltpu.HBM)
SCALARS = pl.BlockSpec(memory_space=pltpu.SMEM)
VMEM_LIMIT = 40 << 20


def dot(left, right, dims):
    return lax.dot_general(left, right, (dims, ((), ())), precision=HIGH, preferred_element_type=jnp.float32)


def product(left, right):
    return dot(left, right, ((1,), (0,)))


def contract(left, right):
    return dot(left, right, ((0,), (0,)))


def block_inverse(block):
    size = block.shape[0]
    shape = (SUB, size)
    sub = lax.broadcasted_iota(jnp.int32, shape, 0)
    lane = lax.broadcasted_iota(jnp.int32, shape, 1)
    groups, tall = size // SUB, PANEL // SUB
    rows = [block[SUB * g : SUB * (g + 1), :] for g in range(groups)]
    down = lambda value, at: jnp.broadcast_to(value[at : at + 1, :], shape)
    across = lambda value, at: jnp.broadcast_to(value[:, at : at + 1], shape)
    for start in range(0, groups, tall):
        within = range(start, start + tall)
        for g in within:
            first = SUB * g
            panel = rows[g]
            heads = [across(panel, first + j) for j in range(SUB)]
            for s in range(0, SUB, 2):
                pair = heads[s], heads[s + 1]
                mid = down(pair[0], s + 1)
                low, high = down(pair[0], s), down(pair[1], s + 1)
                scale = 1.0 / (low * high - mid * mid)
                ends, cross = (high * scale, low * scale), -mid * scale
                solve = lambda first_row, second_row: (
                    ends[0] * first_row + cross * second_row,
                    cross * first_row + ends[1] * second_row,
                )
                place = lambda value, tops: jnp.where(
                    sub == s,
                    tops[0],
                    jnp.where(sub == s + 1, tops[1], value - pair[0] * tops[0] - pair[1] * tops[1]),
                )
                here = (lane == first + s) | (lane == first + s + 1)
                tops = solve(down(panel, s), down(panel, s + 1))
                tops = (
                    jnp.where(here, jnp.where(lane == first + s, ends[0], cross), tops[0]),
                    jnp.where(here, jnp.where(lane == first + s, cross, ends[1]), tops[1]),
                )
                panel = place(jnp.where(here, 0.0, panel), tops)
                for j in range(s + 2, SUB):
                    heads[j] = place(heads[j], solve(down(heads[j], s), down(heads[j], s + 1)))
            rows[g] = panel
            tops = [down(panel, j) for j in range(SUB)]
            inside = (lane >= first) & (lane < first + SUB)
            for h in within:
                if h != g:
                    terms = [across(rows[h], first + j) * tops[j] for j in range(SUB)]
                    while len(terms) > 1:
                        terms = [terms[i] + terms[i + 1] for i in range(0, len(terms), 2)]
                    rows[h] = jnp.where(inside, 0.0, rows[h]) - terms[0]
        inside = (lane >= SUB * start) & (lane < SUB * (start + tall))
        zero = jnp.zeros(shape, jnp.float32)
        side = [zero if h in within else jnp.where(inside, rows[h], 0.0) for h in range(groups)]
        top = [rows[h] if h in within else zero for h in range(groups)]
        less = product(jnp.concatenate(side, axis=0), jnp.concatenate(top, axis=0))
        for h in range(groups):
            if h not in within:
                rows[h] = jnp.where(inside, 0.0, rows[h]) - less[SUB * h : SUB * (h + 1), :]
    return jnp.concatenate(rows, axis=0)


def eliminate(a_ref, t_ref, steps):
    rank = a_ref.shape[0]
    blocks = rank // LANE
    at = lambda j: slice(LANE * j, LANE * (j + 1))
    for j in steps:
        rest = slice(LANE * (j + 1), rank)
        inv = block_inverse(a_ref[at(j), at(j)])
        others = [i for i in range(j + 1, blocks)] + [i for i in range(j)]
        if j < blocks - 1:
            top = product(inv, a_ref[at(j), rest])
            a_ref[at(j), rest] = top
            for i in others:
                a_ref[at(i), rest] = a_ref[at(i), rest] - product(a_ref[at(i), at(j)], top)
        top = product(inv, t_ref[at(j), :])
        t_ref[at(j), :] = top
        for i in others:
            t_ref[at(i), :] = t_ref[at(i), :] - product(a_ref[at(i), at(j)], top)


def identity_less(value):
    row = lax.broadcasted_iota(jnp.int32, value.shape, 0)
    col = lax.broadcasted_iota(jnp.int32, value.shape, 1)
    return jnp.where(row == col, 1.0, 0.0) - value


def call(kernel, inputs, outputs, scratch=(), scalars=0, flops=0, far_in=(), far_out=()):
    return pl.pallas_call(
        kernel,
        out_shape=[jax.ShapeDtypeStruct(shape, jnp.float32) for shape in outputs],
        in_specs=[SCALARS if i < scalars else FAR if i in far_in else WHOLE for i in range(len(inputs))],
        out_specs=[FAR if i in far_out else WHOLE for i in range(len(outputs))],
        scratch_shapes=[
            pltpu.VMEM(shape, jnp.float32) if isinstance(shape, tuple) else shape for shape in scratch
        ],
        cost_estimate=pl.CostEstimate(flops=flops, bytes_accessed=8 << 20, transcendentals=0),
        compiler_params=pltpu.CompilerParams(vmem_limit_bytes=VMEM_LIMIT),
    )(*inputs)


def row_tiles(rows):
    return [slice(TILE * t, TILE * (t + 1)) for t in range(rows // TILE)]


def stream(far_refs, near_refs, sems):
    tiles = row_tiles(far_refs[0].shape[0])
    copies = [
        [pltpu.make_async_copy(far.at[here, :], near.at[here, :], sems.at[i, t])
         for i, (far, near) in enumerate(zip(far_refs, near_refs))]
        for t, here in enumerate(tiles)
    ]
    for tile in copies:
        for copy in tile:
            copy.start()

    def wait(t):
        for copy in copies[t]:
            copy.wait()

    return wait


def gather_rows(pieces, whole_ref):
    at = 0
    for piece in pieces:
        whole_ref[at : at + piece.shape[0], :] = piece[...]
        at += piece.shape[0]


def fine_open(own, sib, steps, flops):
    rank = own[0].shape[1]
    count = len(own)

    def kernel(*refs):
        own_refs, sib_refs = refs[:count], refs[count : 2 * count]
        a_ref, t_ref, far_ref, own_ref = refs[2 * count :]
        gather_rows(own_refs, own_ref)
        gather_rows(sib_refs, far_ref)
        t_ref[...] = identity_less(product(far_ref[...], own_ref[...]))
        a_ref[...] = dot(t_ref[...], t_ref[...], ((1,), (1,)))
        eliminate(a_ref, t_ref, steps)

    square = (rank, rank)
    return call(kernel, [*own, *sib], [square] * 3, [square], flops=flops)


def fine_steps(a, t, steps, flops):
    def kernel(a_in, t_in, a_ref, t_ref):
        a_ref[...] = a_in[...]
        t_ref[...] = t_in[...]
        eliminate(a_ref, t_ref, steps)

    return call(kernel, [a, t], [a.shape, t.shape], flops=flops)


def fine_close(a, t, steps, arrays, flops):
    count = len(arrays)

    def kernel(a_in, t_in, *refs):
        far_refs, out_ref, near_refs = refs[:count], refs[count], refs[count + 1 : 2 * count + 1]
        a_ref, t_ref, sems = refs[2 * count + 1 :]
        copies = [
            pltpu.make_async_copy(far, near, sems.at[i]) for i, (far, near) in enumerate(zip(far_refs, near_refs))
        ]
        for copy in copies:
            copy.start()
        a_ref[...] = a_in[...]
        t_ref[...] = t_in[...]
        eliminate(a_ref, t_ref, steps)
        out_ref[...] = t_ref[...].T
        for copy in copies:
            copy.wait()

    return call(
        kernel,
        [a, t, *arrays],
        [t.shape, *(array.shape for array in arrays)],
        [a.shape, t.shape, pltpu.SemaphoreType.DMA((count,))],
        flops=flops,
        far_in=range(2, 2 + count),
    )


def split(value):
    high = value.astype(jnp.bfloat16)
    return high, (value - high.astype(jnp.float32)).astype(jnp.bfloat16)


def dot3(left, right, dims):
    part = lambda a, b: lax.dot_general(a, b, (dims, ((), ())), preferred_element_type=jnp.float32)
    return part(left[0], right[0]) + (part(left[0], right[1]) + part(left[1], right[0]))


def blocks_masked(pattern_ref, basis, at):
    rows = []
    for i in range(basis.shape[0] // BLK):
        here = basis[BLK * i : BLK * (i + 1), :]
        row = [
            here[:, BLK * j : BLK * (j + 1)] * pattern_ref[at + i, j].astype(jnp.float32)
            for j in range(basis.shape[1] // BLK)
        ]
        rows.append(jnp.concatenate(row, axis=1))
    return jnp.concatenate(rows, axis=0)


def fine_gram(pattern, basis, dual):
    rows, rank = basis.shape
    piece = rank // PIECES
    tiles = row_tiles(rows)

    def kernel(pattern_ref, basis_far, dual_far, *refs):
        out_refs, (basis_ref, dual_ref, sum_ref, sems) = refs[:-4], refs[-4:]
        wait = stream((basis_far, dual_far), (basis_ref, dual_ref), sems)
        for t, here in enumerate(tiles):
            wait(t)
            masked = blocks_masked(pattern_ref, basis_ref[here, :], t * (TILE // BLK))
            part = contract(dual_ref[here, :], masked)
            sum_ref[...] = part if t == 0 else sum_ref[...] + part
        for i, out_ref in enumerate(out_refs):
            out_ref[...] = sum_ref[piece * i : piece * (i + 1), :]

    return call(
        kernel,
        [pattern, basis, dual],
        [(piece, rank)] * PIECES,
        [basis.shape, dual.shape, (rank, rank), pltpu.SemaphoreType.DMA((2, len(tiles)))],
        scalars=1,
        flops=12 * rows * rank * rank,
        far_in=(1, 2),
    )


def fine_moment(dual, coarse, right, cuts):
    rows, rank = dual.shape
    width = rank + right.shape[1]
    tiles = row_tiles(rows)

    def kernel(dual_far, coarse_far, right_far, *refs):
        out_refs, (dual_ref, coarse_ref, right_ref, sum_ref, sems) = refs[:-5], refs[-5:]
        wait = stream((dual_far, coarse_far, right_far), (dual_ref, coarse_ref, right_ref), sems)
        for t, here in enumerate(tiles):
            wait(t)
            left = split(dual_ref[here, :])
            for hand, columns in ((coarse_ref, slice(0, rank)), (right_ref, slice(rank, width))):
                part = dot3(left, split(hand[here, :]), ((0,), (0,)))
                sum_ref[:, columns] = part if t == 0 else sum_ref[:, columns] + part
        for low, high, out_ref in zip(cuts, cuts[1:], out_refs):
            out_ref[...] = sum_ref[low:high, :]

    return call(
        kernel,
        [dual, coarse, right],
        [(high - low, width) for low, high in zip(cuts, cuts[1:])],
        [dual.shape, coarse.shape, right.shape, (rank, width), pltpu.SemaphoreType.DMA((3, len(tiles)))],
        flops=6 * rows * rank * width,
        far_in=(0, 1, 2),
    )


def fine_update(core, pattern, inverse, gram_sib, own, sib, basis, old, dual, columns, at, flops):
    rows, rank = basis.shape
    width = columns.stop - columns.start
    half = rank // 2
    count = len(own)

    def kernel(core_ref, pattern_ref, inv_ref, gram_ref, *refs):
        own_refs, sib_refs = refs[:count], refs[count : 2 * count]
        basis_ref, old_ref, dual_ref, new_ref, keep_ref, send_ref, own_ref, far_ref = refs[2 * count :]
        gather_rows([ref.at[:, columns] for ref in own_refs], own_ref)
        gather_rows([ref.at[:, columns] for ref in sib_refs], far_ref)
        target = far_ref[...] - product(gram_ref[...], own_ref[...])
        coeffs = split(product(inv_ref[...], target))
        kept = pl.ds(pl.multiple_of(core_ref[0] * half, half), half)
        sent = pl.ds(pl.multiple_of((1 - core_ref[0]) * half, half), half)
        for t, here in enumerate(row_tiles(rows)):
            masked = split(blocks_masked(pattern_ref, basis_ref[here, :], t * (TILE // BLK)))
            new = old_ref[here, at : at + width] - dot3(masked, coeffs, ((1,), (0,)))
            new_ref[here, :] = new
            new = split(new)
            for side, sum_ref in ((sent, send_ref), (kept, keep_ref)):
                part = dot3(split(dual_ref[here, side]), new, ((0,), (0,)))
                sum_ref[...] = part if t == 0 else sum_ref[...] + part

    return call(
        kernel,
        [core, pattern, inverse, gram_sib, *own, *sib, basis, old, dual],
        [(rows, width), (half, width), (half, width)],
        [(rank, width)] * 2,
        scalars=2,
        flops=flops,
    )


def top_half(core, mine, other, far_mine, far_other, basis):
    count = len(mine)
    half, width = mine[0].shape[0], sum(piece.shape[1] for piece in mine)
    rank = 2 * half
    nrhs = width - rank
    rows = basis[0].shape[0]

    def kernel(core_ref, *refs):
        lists = [refs[count * i : count * (i + 1)] for i in range(4)]
        basis_refs = refs[4 * count : 4 * count + len(basis)]
        out_ref, whole_basis, own_ref, far_ref, c_ref, a_ref, t_ref, sems = refs[4 * count + len(basis) :]
        copies, at = [], 0
        for i, part in enumerate(basis_refs):
            there = whole_basis.at[:, at : at + part.shape[1]]
            copies.append(pltpu.make_async_copy(part, there, sems.at[i]))
            copies[-1].start()
            at += part.shape[1]
        for first, second, whole_ref in ((*lists[:2], own_ref), (*lists[2:], far_ref)):
            for side, pieces in ((core_ref[0], first), (1 - core_ref[0], second)):
                here, at = pl.ds(pl.multiple_of(side * half, half), half), 0
                for part in pieces:
                    whole_ref[here, at : at + part.shape[1]] = part[...]
                    at += part.shape[1]
        c_ref[...] = identity_less(product(far_ref[:, :rank], own_ref[:, :rank]))
        t_ref[...] = far_ref[:, rank:] - product(far_ref[:, :rank], own_ref[:, rank:])
        a_ref[...] = dot(c_ref[...], c_ref[...], ((1,), (1,)))
        eliminate(a_ref, t_ref, range(rank // LANE))
        here = pl.ds(pl.multiple_of(core_ref[0] * half, half), half)
        out_ref[...] = contract(c_ref[:, here], t_ref[...])
        for copy in copies:
            copy.wait()

    square, wide = (rank, rank), (rank, width)
    return call(
        kernel,
        [core, *mine, *other, *far_mine, *far_other, *basis],
        [(half, nrhs), (rows, rank)],
        [wide, wide, square, square, (rank, nrhs), pltpu.SemaphoreType.DMA((len(basis),))],
        scalars=1,
        flops=1 << 34,
        far_out=(1,),
    )


def final_update(core, mine, other, basis, updated):
    half, nrhs = mine.shape
    rows = updated.shape[0]
    tiles = row_tiles(rows)

    def kernel(core_ref, mine_ref, other_ref, *refs):
        basis_refs, (updated_ref, out_far, coeffs_ref, out_ref, sems) = refs[:-5], refs[-5:]
        for side, part in ((core_ref[0], mine_ref), (1 - core_ref[0], other_ref)):
            coeffs_ref[pl.ds(pl.multiple_of(side * half, half), half), :] = part[...]
        copies = []
        for t, here in enumerate(tiles):
            total, at = updated_ref[here, :], 0
            for part in basis_refs:
                coeffs = split(coeffs_ref[at : at + part.shape[1], :])
                total = total - dot3(split(part[here, :]), coeffs, ((1,), (0,)))
                at += part.shape[1]
            out_ref[here, :] = total
            copies.append(pltpu.make_async_copy(out_ref.at[here, :], out_far.at[here, :], sems.at[t]))
            copies[-1].start()
        for copy in copies:
            copy.wait()

    return call(
        kernel,
        [core, mine, other, *basis, updated],
        [(rows, nrhs)],
        [(2 * half, nrhs), (rows, nrhs), pltpu.SemaphoreType.DMA((len(tiles),))],
        scalars=1,
        flops=12 * rows * half * nrhs,
        far_out=(0,),
    )[0]


def swapped(value, axis, distance):
    mask = 2**distance
    pairs = [(source, source ^ mask) for source in range(lax.axis_size(axis))]
    return lax.ppermute(value, axis, pairs)


def after(value, *others):
    return lax.optimization_barrier((value, *others))[0]


def hop_count(axis):
    return 2 * (lax.axis_size(axis) // 2) - 1


def hop_pairs(axis, hop):
    size = lax.axis_size(axis)
    half = size // 2
    if hop == half - 1:
        return [(half - 1, half), (half, half - 1)]
    if hop < half - 1:
        return [(hop, hop + 1), (size - 1 - hop, size - 2 - hop)]
    t = 2 * half - 2 - hop
    return [(t + 1, t), (size - 2 - t, size - 1 - t)]


def leave(value, axis, hop):
    return lax.ppermute(value, axis, hop_pairs(axis, hop))


def arrive(value, arrived, axis, hop):
    size = lax.axis_size(axis)
    if hop < size // 2:
        return value + arrived
    here = lax.axis_index(axis)
    t = 2 * (size // 2) - 2 - hop
    return jnp.where((here == t) | (here == size - 1 - t), arrived, value)


def line_hops(values, axis, first, last, lag=None):
    values = list(values)
    for hop in range(first, last):
        moved = []
        for i, value in enumerate(values):
            if lag and i >= lag and hop == hop_count(axis) // 2:
                value = after(value, moved[i - lag])
            moved.append(arrive(value, leave(value, axis, hop), axis, hop))
        values = moved
    return values


def cross(value, hop):
    return arrive(value, leave(value, "row", hop), "row", hop)


def shards(basis_fine, dual_fine, basis_coarse, dual_coarse, right_side, pattern):
    rank, nrhs = basis_fine.shape[1], right_side.shape[1]
    half = rank // 2
    hops = hop_count("row")
    middle = hops // 2 + 1
    core = (lax.axis_index("sib") % 2)[None]

    gram = fine_gram(pattern, basis_fine, dual_fine)
    moment = fine_moment(after(dual_fine, gram[0]), basis_coarse, right_side, [0, 176, 352, rank])
    leaving = [leave(piece, "row", 0) for piece in gram]
    gram = lax.optimization_barrier((*gram, *moment))[: len(gram)]
    gram = [arrive(piece, arrived, "row", 0) for piece, arrived in zip(gram, leaving)]
    first, second, third = moment
    for hop in range(middle - 1):
        first = cross(after(first, gram[-1]) if hop == 0 else first, hop)
    for hop in range(middle - 1):
        second = cross(after(second, first) if hop == 0 else second, hop)
    flying = leave(after(third, second), "row", 0)
    gram = line_hops(gram, "row", 1, hops, lag=2)
    gram_sib = [swapped(piece, "sib", 0) for piece in gram]
    *gram, first, second = lax.optimization_barrier((*gram, first, second))
    first_flying = leave(first, "row", middle - 1)
    second_flying = leave(second, "row", middle - 1)
    normal, solved, gram_sib = fine_open(gram, gram_sib, range(1), 1 << 24)

    first, second, third, normal = lax.optimization_barrier((first, second, third, normal))
    first = arrive(first, first_flying, "row", middle - 1)
    third = arrive(third, flying, "row", 0)
    for hop in range(1, middle - 1):
        third = cross(third, hop)
    second = arrive(second, second_flying, "row", middle - 1)
    normal, first, second, third = lax.optimization_barrier((normal, first, second, third))
    flying = leave(third, "row", middle - 1)
    first_flying = leave(first, "row", middle)
    second_flying = leave(second, "row", middle)
    normal, solved = fine_steps(normal, solved, range(1, 2), 1 << 24)

    third, normal = lax.optimization_barrier((third, normal))
    third = arrive(third, flying, "row", middle - 1)
    third, normal = lax.optimization_barrier((third, normal))
    flying = leave(third, "row", middle)
    normal, solved = fine_steps(normal, solved, range(2, 3), 1 << 24)

    first, second, normal = lax.optimization_barrier((first, second, normal))
    first = arrive(first, first_flying, "row", middle)
    second = arrive(second, second_flying, "row", middle)
    inverse, basis_near, dual_near, coarse_near, right_near = fine_close(
        normal, solved, range(3, rank // LANE), [basis_fine, dual_coarse, basis_coarse, right_side], 1 << 24
    )
    third, inverse = lax.optimization_barrier((third, inverse))
    third = arrive(third, flying, "row", middle)
    moment = [first, second, third]
    for hop in range(middle + 1, hops):
        moment = [cross(value, hop) for value in moment]
    moment_sib = [swapped(piece, "sib", 0) for piece in moment]

    new, parts = [], []
    for low, high in ((0, half), (half, rank), (rank, rank + nrhs)):
        old, at = (coarse_near, low) if low < rank else (right_near, 0)
        if new:
            old = after(old, new[-1])
        chunk, keep, send = fine_update(
            core, pattern, inverse, gram_sib, moment, moment_sib, basis_near, old, dual_near,
            slice(low, high), at, 1 << 32,
        )
        new.append(chunk)
        parts.append(keep + swapped(send, "sib", 0))
    parts = line_hops(parts, "row", 0, middle)
    far = [swapped(value, "sib", 1) for value in parts]
    parts_other = [swapped(value, "sib", 0) for value in parts]
    far_other = [swapped(value, "sib", 0) for value in far]
    *basis, updated = new
    result, whole_basis = top_half(core, parts, parts_other, far, far_other, basis)
    result = line_hops([result], "row", middle, hops)[0]
    solution = final_update(core, result, swapped(result, "sib", 0), basis, updated)
    return (whole_basis, solution)


def solution(mesh):
    rows = P(("grp", "sib", "row"), None)
    return jax.shard_map(
        shards,
        mesh=mesh,
        in_specs=(rows,) * 6,
        out_specs=(rows, rows),
        check_vma=False,
    )
```

```python
import jax
import jax.numpy as jnp
from jax import lax
from jax.experimental import pallas as pl
from jax.experimental.pallas import tpu as pltpu
from jax.sharding import PartitionSpec as P

BLK = 128
SUB, LANE, PANEL = 8, 128, 32
PIECES = 4
TILE = 256
HIGH = lax.Precision.HIGHEST
WHOLE = pl.BlockSpec(memory_space=pltpu.VMEM)
FAR = pl.BlockSpec(memory_space=pltpu.HBM)
SCALARS = pl.BlockSpec(memory_space=pltpu.SMEM)
VMEM_LIMIT = 20 << 20
STREAM_LIMIT = 62 << 20


def dot(left, right, dims):
    return lax.dot_general(left, right, (dims, ((), ())), precision=HIGH, preferred_element_type=jnp.float32)


def product(left, right):
    return dot(left, right, ((1,), (0,)))


def contract(left, right):
    return dot(left, right, ((0,), (0,)))


def block_inverse(block):
    size = block.shape[0]
    shape = (SUB, size)
    sub = lax.broadcasted_iota(jnp.int32, shape, 0)
    lane = lax.broadcasted_iota(jnp.int32, shape, 1)
    groups, tall = size // SUB, PANEL // SUB
    rows = [block[SUB * g : SUB * (g + 1), :] for g in range(groups)]
    down = lambda value, at: jnp.broadcast_to(value[at : at + 1, :], shape)
    across = lambda value, at: jnp.broadcast_to(value[:, at : at + 1], shape)
    for start in range(0, groups, tall):
        within = range(start, start + tall)
        for g in within:
            first = SUB * g
            panel = rows[g]
            heads = [across(panel, first + j) for j in range(SUB)]
            for s in range(0, SUB, 2):
                pair = heads[s], heads[s + 1]
                mid = down(pair[0], s + 1)
                low, high = down(pair[0], s), down(pair[1], s + 1)
                scale = 1.0 / (low * high - mid * mid)
                ends, cross = (high * scale, low * scale), -mid * scale
                solve = lambda first_row, second_row: (
                    ends[0] * first_row + cross * second_row,
                    cross * first_row + ends[1] * second_row,
                )
                place = lambda value, tops: jnp.where(
                    sub == s,
                    tops[0],
                    jnp.where(sub == s + 1, tops[1], value - pair[0] * tops[0] - pair[1] * tops[1]),
                )
                here = (lane == first + s) | (lane == first + s + 1)
                tops = solve(down(panel, s), down(panel, s + 1))
                tops = (
                    jnp.where(here, jnp.where(lane == first + s, ends[0], cross), tops[0]),
                    jnp.where(here, jnp.where(lane == first + s, cross, ends[1]), tops[1]),
                )
                panel = place(jnp.where(here, 0.0, panel), tops)
                for j in range(s + 2, SUB):
                    heads[j] = place(heads[j], solve(down(heads[j], s), down(heads[j], s + 1)))
            rows[g] = panel
            tops = [down(panel, j) for j in range(SUB)]
            inside = (lane >= first) & (lane < first + SUB)
            for h in within:
                if h != g:
                    terms = [across(rows[h], first + j) * tops[j] for j in range(SUB)]
                    while len(terms) > 1:
                        terms = [terms[i] + terms[i + 1] for i in range(0, len(terms), 2)]
                    rows[h] = jnp.where(inside, 0.0, rows[h]) - terms[0]
        inside = (lane >= SUB * start) & (lane < SUB * (start + tall))
        zero = jnp.zeros(shape, jnp.float32)
        side = [zero if h in within else jnp.where(inside, rows[h], 0.0) for h in range(groups)]
        top = [rows[h] if h in within else zero for h in range(groups)]
        less = product(jnp.concatenate(side, axis=0), jnp.concatenate(top, axis=0))
        for h in range(groups):
            if h not in within:
                rows[h] = jnp.where(inside, 0.0, rows[h]) - less[SUB * h : SUB * (h + 1), :]
    return jnp.concatenate(rows, axis=0)


def eliminate(a_ref, t_ref, steps):
    rank = a_ref.shape[0]
    blocks = rank // LANE
    at = lambda j: slice(LANE * j, LANE * (j + 1))
    for j in steps:
        rest = slice(LANE * (j + 1), rank)
        inv = block_inverse(a_ref[at(j), at(j)])
        others = [i for i in range(j + 1, blocks)] + [i for i in range(j)]
        if j < blocks - 1:
            top = product(inv, a_ref[at(j), rest])
            a_ref[at(j), rest] = top
            for i in others:
                a_ref[at(i), rest] = a_ref[at(i), rest] - product(a_ref[at(i), at(j)], top)
        top = product(inv, t_ref[at(j), :])
        t_ref[at(j), :] = top
        for i in others:
            t_ref[at(i), :] = t_ref[at(i), :] - product(a_ref[at(i), at(j)], top)


def identity_less(value):
    row = lax.broadcasted_iota(jnp.int32, value.shape, 0)
    col = lax.broadcasted_iota(jnp.int32, value.shape, 1)
    return jnp.where(row == col, 1.0, 0.0) - value


def call(kernel, inputs, outputs, scratch=(), scalars=0, flops=0, far_in=(), far_out=(), limit=VMEM_LIMIT):
    return pl.pallas_call(
        kernel,
        out_shape=[
            jax.ShapeDtypeStruct(shape, jnp.float32) if isinstance(shape, tuple) else shape for shape in outputs
        ],
        in_specs=[SCALARS if i < scalars else FAR if i in far_in else WHOLE for i in range(len(inputs))],
        out_specs=[FAR if i in far_out else WHOLE for i in range(len(outputs))],
        scratch_shapes=[
            pltpu.VMEM(shape, jnp.float32) if isinstance(shape, tuple) else shape for shape in scratch
        ],
        cost_estimate=pl.CostEstimate(flops=flops, bytes_accessed=8 << 20, transcendentals=0),
        compiler_params=pltpu.CompilerParams(vmem_limit_bytes=limit),
    )(*inputs)


def row_tiles(rows):
    return [slice(TILE * t, TILE * (t + 1)) for t in range(rows // TILE)]


def stream(far_refs, near_refs, sems):
    tiles = row_tiles(far_refs[0].shape[0])
    copies = [
        [pltpu.make_async_copy(far.at[here, :], near.at[here, :], sems.at[i, t])
         for i, (far, near) in enumerate(zip(far_refs, near_refs))]
        for t, here in enumerate(tiles)
    ]
    for tile in copies:
        for copy in tile:
            copy.start()

    def wait(t):
        for copy in copies[t]:
            copy.wait()

    return wait


def gather_rows(pieces, whole_ref):
    at = 0
    for piece in pieces:
        whole_ref[at : at + piece.shape[0], :] = piece[...]
        at += piece.shape[0]


def fine_open(own, sib, steps, flops):
    rank = own[0].shape[1]
    count = len(own)

    def kernel(*refs):
        own_refs, sib_refs = refs[:count], refs[count : 2 * count]
        a_ref, t_ref, far_ref, own_ref = refs[2 * count :]
        gather_rows(own_refs, own_ref)
        gather_rows(sib_refs, far_ref)
        t_ref[...] = identity_less(product(far_ref[...], own_ref[...]))
        a_ref[...] = dot(t_ref[...], t_ref[...], ((1,), (1,)))
        eliminate(a_ref, t_ref, steps)

    square = (rank, rank)
    return call(kernel, [*own, *sib], [square] * 3, [square], flops=flops)


def fine_steps(a, t, steps, flops):
    def kernel(a_in, t_in, a_ref, t_ref):
        a_ref[...] = a_in[...]
        t_ref[...] = t_in[...]
        eliminate(a_ref, t_ref, steps)

    return call(kernel, [a, t], [a.shape, t.shape], flops=flops)


def fine_close(a, t, steps, arrays, flops):
    count = len(arrays)

    def kernel(a_in, t_in, *refs):
        far_refs, out_ref, near_refs = refs[:count], refs[count], refs[count + 1 : 2 * count + 1]
        a_ref, t_ref, sems = refs[2 * count + 1 :]
        copies = [
            pltpu.make_async_copy(far, near, sems.at[i]) for i, (far, near) in enumerate(zip(far_refs, near_refs))
        ]
        for copy in copies:
            copy.start()
        a_ref[...] = a_in[...]
        t_ref[...] = t_in[...]
        eliminate(a_ref, t_ref, steps)
        out_ref[...] = t_ref[...].T
        for copy in copies:
            copy.wait()

    return call(
        kernel,
        [a, t, *arrays],
        [t.shape, *(array.shape for array in arrays)],
        [a.shape, t.shape, pltpu.SemaphoreType.DMA((count,))],
        flops=flops,
        far_in=range(2, 2 + count),
    )


def split(value):
    high = value.astype(jnp.bfloat16)
    return high, (value - high.astype(jnp.float32)).astype(jnp.bfloat16)


def dot3(left, right, dims):
    part = lambda a, b: lax.dot_general(a, b, (dims, ((), ())), preferred_element_type=jnp.float32)
    return part(left[0], right[0]) + (part(left[0], right[1]) + part(left[1], right[0]))


def blocks_masked(pattern_ref, basis, at):
    rows = []
    for i in range(basis.shape[0] // BLK):
        here = basis[BLK * i : BLK * (i + 1), :]
        row = [
            here[:, BLK * j : BLK * (j + 1)] * pattern_ref[at + i, j].astype(jnp.float32)
            for j in range(basis.shape[1] // BLK)
        ]
        rows.append(jnp.concatenate(row, axis=1))
    return jnp.concatenate(rows, axis=0)


def fine_gram(pattern, basis, dual):
    rows, rank = basis.shape
    piece = rank // PIECES
    tiles = row_tiles(rows)

    def kernel(pattern_ref, basis_far, dual_far, *refs):
        out_refs, (basis_ref, dual_ref, sum_ref, sems) = refs[:-4], refs[-4:]
        wait = stream((basis_far, dual_far), (basis_ref, dual_ref), sems)
        for t, here in enumerate(tiles):
            wait(t)
            masked = blocks_masked(pattern_ref, basis_ref[here, :], t * (TILE // BLK))
            part = contract(dual_ref[here, :], masked)
            sum_ref[...] = part if t == 0 else sum_ref[...] + part
        for i, out_ref in enumerate(out_refs):
            out_ref[...] = sum_ref[piece * i : piece * (i + 1), :]

    return call(
        kernel,
        [pattern, basis, dual],
        [(piece, rank)] * PIECES,
        [basis.shape, dual.shape, (rank, rank), pltpu.SemaphoreType.DMA((2, len(tiles)))],
        scalars=1,
        flops=12 * rows * rank * rank,
        far_in=(1, 2),
        limit=STREAM_LIMIT,
    )


def fine_moment(dual, coarse, right, cuts):
    rows, rank = dual.shape
    width = rank + right.shape[1]
    tiles = row_tiles(rows)

    def kernel(dual_far, coarse_far, right_far, *refs):
        out_refs, (dual_ref, coarse_ref, right_ref, sum_ref, sems) = refs[:-5], refs[-5:]
        wait = stream((dual_far, coarse_far, right_far), (dual_ref, coarse_ref, right_ref), sems)
        for t, here in enumerate(tiles):
            wait(t)
            left = split(dual_ref[here, :])
            for hand, columns in ((coarse_ref, slice(0, rank)), (right_ref, slice(rank, width))):
                part = dot3(left, split(hand[here, :]), ((0,), (0,)))
                sum_ref[:, columns] = part if t == 0 else sum_ref[:, columns] + part
        for low, high, out_ref in zip(cuts, cuts[1:], out_refs):
            out_ref[...] = sum_ref[low:high, :]

    return call(
        kernel,
        [dual, coarse, right],
        [(high - low, width) for low, high in zip(cuts, cuts[1:])],
        [dual.shape, coarse.shape, right.shape, (rank, width), pltpu.SemaphoreType.DMA((3, len(tiles)))],
        flops=6 * rows * rank * width,
        far_in=(0, 1, 2),
        limit=STREAM_LIMIT,
    )


def halves(shape):
    return [jax.ShapeDtypeStruct(shape, jnp.bfloat16)] * 2


def split_masked(pattern, basis):
    def kernel(pattern_ref, basis_ref, high_ref, low_ref):
        for t, here in enumerate(row_tiles(basis.shape[0])):
            masked = blocks_masked(pattern_ref, basis_ref[here, :], t * (TILE // BLK))
            high_ref[here, :], low_ref[here, :] = split(masked)

    return call(kernel, [pattern, basis], halves(basis.shape), scalars=1, flops=1 << 24)


def split_transposed(dual):
    def kernel(dual_ref, high_ref, low_ref):
        for here in row_tiles(dual.shape[0]):
            high_ref[:, here], low_ref[:, here] = split(dual_ref[here, :].T)

    return call(kernel, [dual], halves(dual.shape[::-1]), flops=1 << 24)


def fine_update(core, inverse, gram_sib, own, sib, masked, old, dual, columns, at, flops):
    rows, rank = masked[0].shape
    width = columns.stop - columns.start
    half = rank // 2
    count = len(own)

    def kernel(core_ref, inv_ref, gram_ref, *refs):
        own_refs, sib_refs = refs[:count], refs[count : 2 * count]
        masked_refs, dual_refs = refs[2 * count : 2 * count + 2], refs[2 * count + 2 : 2 * count + 4]
        old_ref, new_ref, keep_ref, send_ref, own_ref, far_ref = refs[2 * count + 4 :]
        gather_rows([ref.at[:, columns] for ref in own_refs], own_ref)
        gather_rows([ref.at[:, columns] for ref in sib_refs], far_ref)
        target = far_ref[...] - product(gram_ref[...], own_ref[...])
        coeffs = split(product(inv_ref[...], target))
        for here in row_tiles(rows):
            tile = [ref[here, :] for ref in masked_refs]
            new_ref[here, :] = old_ref[here, at : at + width] - dot3(tile, coeffs, ((1,), (0,)))
        new = split(new_ref[...])
        for side, sum_ref in ((1 - core_ref[0], send_ref), (core_ref[0], keep_ref)):
            here = pl.ds(pl.multiple_of(side * half, half), half)
            sum_ref[...] = dot3([ref[here, :] for ref in dual_refs], new, ((1,), (0,)))

    return call(
        kernel,
        [core, inverse, gram_sib, *own, *sib, *masked, *dual, old],
        [(rows, width), (half, width), (half, width)],
        [(rank, width)] * 2,
        scalars=1,
        flops=flops,
    )


def top_half(core, mine, other, far_mine, far_other, basis):
    count = len(mine)
    half, width = mine[0].shape[0], sum(piece.shape[1] for piece in mine)
    rank = 2 * half
    nrhs = width - rank
    rows = basis[0].shape[0]

    def kernel(core_ref, *refs):
        lists = [refs[count * i : count * (i + 1)] for i in range(4)]
        basis_refs = refs[4 * count : 4 * count + len(basis)]
        out_ref, whole_basis, own_ref, far_ref, c_ref, a_ref, t_ref, sems = refs[4 * count + len(basis) :]
        copies, at = [], 0
        for i, part in enumerate(basis_refs):
            there = whole_basis.at[:, at : at + part.shape[1]]
            copies.append(pltpu.make_async_copy(part, there, sems.at[i]))
            copies[-1].start()
            at += part.shape[1]
        for first, second, whole_ref in ((*lists[:2], own_ref), (*lists[2:], far_ref)):
            for side, pieces in ((core_ref[0], first), (1 - core_ref[0], second)):
                here, at = pl.ds(pl.multiple_of(side * half, half), half), 0
                for part in pieces:
                    whole_ref[here, at : at + part.shape[1]] = part[...]
                    at += part.shape[1]
        c_ref[...] = identity_less(product(far_ref[:, :rank], own_ref[:, :rank]))
        t_ref[...] = far_ref[:, rank:] - product(far_ref[:, :rank], own_ref[:, rank:])
        a_ref[...] = dot(c_ref[...], c_ref[...], ((1,), (1,)))
        eliminate(a_ref, t_ref, range(rank // LANE))
        here = pl.ds(pl.multiple_of(core_ref[0] * half, half), half)
        out_ref[...] = contract(c_ref[:, here], t_ref[...])
        for copy in copies:
            copy.wait()

    square, wide = (rank, rank), (rank, width)
    return call(
        kernel,
        [core, *mine, *other, *far_mine, *far_other, *basis],
        [(half, nrhs), (rows, rank)],
        [wide, wide, square, square, (rank, nrhs), pltpu.SemaphoreType.DMA((len(basis),))],
        scalars=1,
        flops=1 << 34,
        far_out=(1,),
    )


def final_update(core, mine, other, basis, updated):
    half, nrhs = mine.shape
    rows = updated.shape[0]
    tiles = row_tiles(rows)

    def kernel(core_ref, mine_ref, other_ref, *refs):
        basis_refs, (updated_ref, out_far, coeffs_ref, out_ref, sems) = refs[:-5], refs[-5:]
        for side, part in ((core_ref[0], mine_ref), (1 - core_ref[0], other_ref)):
            coeffs_ref[pl.ds(pl.multiple_of(side * half, half), half), :] = part[...]
        copies = []
        for t, here in enumerate(tiles):
            total, at = updated_ref[here, :], 0
            for part in basis_refs:
                coeffs = split(coeffs_ref[at : at + part.shape[1], :])
                total = total - dot3(split(part[here, :]), coeffs, ((1,), (0,)))
                at += part.shape[1]
            out_ref[here, :] = total
            copies.append(pltpu.make_async_copy(out_ref.at[here, :], out_far.at[here, :], sems.at[t]))
            copies[-1].start()
        for copy in copies:
            copy.wait()

    return call(
        kernel,
        [core, mine, other, *basis, updated],
        [(rows, nrhs)],
        [(2 * half, nrhs), (rows, nrhs), pltpu.SemaphoreType.DMA((len(tiles),))],
        scalars=1,
        flops=12 * rows * half * nrhs,
        far_out=(0,),
    )[0]


def swapped(value, axis, distance):
    mask = 2**distance
    pairs = [(source, source ^ mask) for source in range(lax.axis_size(axis))]
    return lax.ppermute(value, axis, pairs)


def after(value, *others):
    return lax.optimization_barrier((value, *others))[0]


def hop_count(axis):
    return 2 * (lax.axis_size(axis) // 2) - 1


def hop_pairs(axis, hop):
    size = lax.axis_size(axis)
    half = size // 2
    if hop == half - 1:
        return [(half - 1, half), (half, half - 1)]
    if hop < half - 1:
        return [(hop, hop + 1), (size - 1 - hop, size - 2 - hop)]
    t = 2 * half - 2 - hop
    return [(t + 1, t), (size - 2 - t, size - 1 - t)]


def leave(value, axis, hop):
    return lax.ppermute(value, axis, hop_pairs(axis, hop))


def arrive(value, arrived, axis, hop):
    size = lax.axis_size(axis)
    if hop < size // 2:
        return value + arrived
    here = lax.axis_index(axis)
    t = 2 * (size // 2) - 2 - hop
    return jnp.where((here == t) | (here == size - 1 - t), arrived, value)


def line_hops(values, axis, first, last, lag=None):
    values = list(values)
    for hop in range(first, last):
        moved = []
        for i, value in enumerate(values):
            if lag and i >= lag and hop == hop_count(axis) // 2:
                value = after(value, moved[i - lag])
            moved.append(arrive(value, leave(value, axis, hop), axis, hop))
        values = moved
    return values


def cross(value, hop):
    return arrive(value, leave(value, "row", hop), "row", hop)


def shards(basis_fine, dual_fine, basis_coarse, dual_coarse, right_side, pattern):
    rank, nrhs = basis_fine.shape[1], right_side.shape[1]
    half = rank // 2
    hops = hop_count("row")
    middle = hops // 2 + 1
    core = (lax.axis_index("sib") % 2)[None]

    gram = fine_gram(pattern, basis_fine, dual_fine)
    moment = fine_moment(after(dual_fine, gram[0]), basis_coarse, right_side, [0, half, rank])
    leaving = [leave(piece, "row", 0) for piece in gram]
    gram = lax.optimization_barrier((*gram, *moment))[: len(gram)]
    gram = [arrive(piece, arrived, "row", 0) for piece, arrived in zip(gram, leaving)]
    gram = line_hops(gram, "row", 1, middle, lag=2)
    masked = split_masked(pattern, after(basis_fine, gram[0]))
    dual = split_transposed(after(dual_coarse, gram[1]))
    first, second = moment
    first = after(first, gram[1])
    for hop in range(middle - 1):
        first = cross(first, hop)
    gram = line_hops(gram, "row", middle, hops)
    gram_sib = [swapped(piece, "sib", 0) for piece in gram]
    second = after(second, first)
    first_flying, second_flying = leave(first, "row", middle - 1), leave(second, "row", 0)
    *gram, first, high, low, dual_high, dual_low = lax.optimization_barrier((*gram, first, *masked, *dual))
    masked, dual = (high, low), (dual_high, dual_low)
    normal, solved, gram_sib = fine_open(gram, gram_sib, range(1), 1 << 24)

    first, second, normal = lax.optimization_barrier((first, second, normal))
    second = arrive(second, second_flying, "row", 0)
    for hop in range(1, middle - 1):
        second = cross(second, hop)
    first = arrive(first, first_flying, "row", middle - 1)
    normal, first, second = lax.optimization_barrier((normal, first, second))
    second_flying, first_flying = leave(second, "row", middle - 1), leave(first, "row", middle)
    normal, solved = fine_steps(normal, solved, range(1, 3), 1 << 24)

    first, second, normal = lax.optimization_barrier((first, second, normal))
    second = arrive(second, second_flying, "row", middle - 1)
    second, normal = lax.optimization_barrier((second, normal))
    second_flying = leave(second, "row", middle)
    inverse, coarse_near, right_near = fine_close(
        normal, solved, range(3, rank // LANE), [basis_coarse, right_side], 1 << 24
    )
    first, second, inverse = lax.optimization_barrier((first, second, inverse))
    first = arrive(first, first_flying, "row", middle)
    second = arrive(second, second_flying, "row", middle)
    moment = [first, second]
    for hop in range(middle + 1, hops):
        moment = [cross(value, hop) for value in moment]
    moment_sib = [swapped(piece, "sib", 0) for piece in moment]

    new, parts = [], []
    for low, high in ((0, half), (half, rank), (rank, rank + nrhs)):
        old, at = (coarse_near, low) if low < rank else (right_near, 0)
        if new:
            old = after(old, new[-1])
        chunk, keep, send = fine_update(
            core, inverse, gram_sib, moment, moment_sib, masked, old, dual, slice(low, high), at, 1 << 30
        )
        new.append(chunk)
        parts.append(keep + swapped(send, "sib", 0))
    leaving = [leave(value, "row", 0) for value in parts]
    for i, arrived in enumerate(leaving):
        parts[i] = arrive(after(parts[i], parts[0]) if i else parts[i], arrived, "row", 0)
    parts[1] = after(parts[1], parts[2])
    parts = line_hops(parts, "row", 1, middle)
    far = [swapped(value, "sib", 1) for value in parts]
    parts_other = [swapped(value, "sib", 0) for value in parts]
    far_other = [swapped(value, "sib", 0) for value in far]
    *basis, updated = new
    result, whole_basis = top_half(core, parts, parts_other, far, far_other, basis)
    result = line_hops([result], "row", middle, hops)[0]
    solution = final_update(core, result, swapped(result, "sib", 0), basis, updated)
    return (whole_basis, solution)


def solution(mesh):
    rows = P(("grp", "sib", "row"), None)
    return jax.shard_map(
        shards,
        mesh=mesh,
        in_specs=(rows,) * 6,
        out_specs=(rows, rows),
        check_vma=False,
    )
```

```python
import jax
import jax.numpy as jnp
from jax import lax
from jax.experimental import pallas as pl
from jax.experimental.pallas import tpu as pltpu
from jax.sharding import PartitionSpec as P

BLK = 128
SUB, LANE, PANEL = 8, 128, 32
PIECES = 4
TILE = 256
HIGH = lax.Precision.HIGHEST
WHOLE = pl.BlockSpec(memory_space=pltpu.VMEM)
FAR = pl.BlockSpec(memory_space=pltpu.HBM)
SCALARS = pl.BlockSpec(memory_space=pltpu.SMEM)
VMEM_LIMIT = 20 << 20
STREAM_LIMIT = 62 << 20


def dot(left, right, dims):
    return lax.dot_general(left, right, (dims, ((), ())), precision=HIGH, preferred_element_type=jnp.float32)


def product(left, right):
    return dot(left, right, ((1,), (0,)))


def contract(left, right):
    return dot(left, right, ((0,), (0,)))


def block_inverse(block):
    size = block.shape[0]
    shape = (SUB, size)
    sub = lax.broadcasted_iota(jnp.int32, shape, 0)
    lane = lax.broadcasted_iota(jnp.int32, shape, 1)
    groups, tall = size // SUB, PANEL // SUB
    rows = [block[SUB * g : SUB * (g + 1), :] for g in range(groups)]
    down = lambda value, at: jnp.broadcast_to(value[at : at + 1, :], shape)
    across = lambda value, at: jnp.broadcast_to(value[:, at : at + 1], shape)
    for start in range(0, groups, tall):
        within = range(start, start + tall)
        for g in within:
            first = SUB * g
            panel = rows[g]
            heads = [across(panel, first + j) for j in range(SUB)]
            for s in range(0, SUB, 2):
                pair = heads[s], heads[s + 1]
                mid = down(pair[0], s + 1)
                low, high = down(pair[0], s), down(pair[1], s + 1)
                scale = 1.0 / (low * high - mid * mid)
                ends, cross = (high * scale, low * scale), -mid * scale
                solve = lambda first_row, second_row: (
                    ends[0] * first_row + cross * second_row,
                    cross * first_row + ends[1] * second_row,
                )
                place = lambda value, tops: jnp.where(
                    sub == s,
                    tops[0],
                    jnp.where(sub == s + 1, tops[1], value - pair[0] * tops[0] - pair[1] * tops[1]),
                )
                here = (lane == first + s) | (lane == first + s + 1)
                tops = solve(down(panel, s), down(panel, s + 1))
                tops = (
                    jnp.where(here, jnp.where(lane == first + s, ends[0], cross), tops[0]),
                    jnp.where(here, jnp.where(lane == first + s, cross, ends[1]), tops[1]),
                )
                panel = place(jnp.where(here, 0.0, panel), tops)
                for j in range(s + 2, SUB):
                    heads[j] = place(heads[j], solve(down(heads[j], s), down(heads[j], s + 1)))
            rows[g] = panel
            tops = [down(panel, j) for j in range(SUB)]
            inside = (lane >= first) & (lane < first + SUB)
            for h in within:
                if h != g:
                    terms = [across(rows[h], first + j) * tops[j] for j in range(SUB)]
                    while len(terms) > 1:
                        terms = [terms[i] + terms[i + 1] for i in range(0, len(terms), 2)]
                    rows[h] = jnp.where(inside, 0.0, rows[h]) - terms[0]
        inside = (lane >= SUB * start) & (lane < SUB * (start + tall))
        zero = jnp.zeros(shape, jnp.float32)
        side = [zero if h in within else jnp.where(inside, rows[h], 0.0) for h in range(groups)]
        top = [rows[h] if h in within else zero for h in range(groups)]
        less = product(jnp.concatenate(side, axis=0), jnp.concatenate(top, axis=0))
        for h in range(groups):
            if h not in within:
                rows[h] = jnp.where(inside, 0.0, rows[h]) - less[SUB * h : SUB * (h + 1), :]
    return jnp.concatenate(rows, axis=0)


def eliminate(a_ref, t_ref, steps):
    rank = a_ref.shape[0]
    blocks = rank // LANE
    at = lambda j: slice(LANE * j, LANE * (j + 1))
    for j in steps:
        rest = slice(LANE * (j + 1), rank)
        inv = block_inverse(a_ref[at(j), at(j)])
        others = [i for i in range(j + 1, blocks)] + [i for i in range(j)]
        if j < blocks - 1:
            top = product(inv, a_ref[at(j), rest])
            a_ref[at(j), rest] = top
            for i in others:
                a_ref[at(i), rest] = a_ref[at(i), rest] - product(a_ref[at(i), at(j)], top)
        top = product(inv, t_ref[at(j), :])
        t_ref[at(j), :] = top
        for i in others:
            t_ref[at(i), :] = t_ref[at(i), :] - product(a_ref[at(i), at(j)], top)


def identity_less(value):
    row = lax.broadcasted_iota(jnp.int32, value.shape, 0)
    col = lax.broadcasted_iota(jnp.int32, value.shape, 1)
    return jnp.where(row == col, 1.0, 0.0) - value


def call(kernel, inputs, outputs, scratch=(), scalars=0, flops=0, far_in=(), far_out=(), limit=VMEM_LIMIT):
    return pl.pallas_call(
        kernel,
        out_shape=[
            jax.ShapeDtypeStruct(shape, jnp.float32) if isinstance(shape, tuple) else shape for shape in outputs
        ],
        in_specs=[SCALARS if i < scalars else FAR if i in far_in else WHOLE for i in range(len(inputs))],
        out_specs=[FAR if i in far_out else WHOLE for i in range(len(outputs))],
        scratch_shapes=[
            pltpu.VMEM(shape, jnp.float32) if isinstance(shape, tuple) else shape for shape in scratch
        ],
        cost_estimate=pl.CostEstimate(flops=flops, bytes_accessed=8 << 20, transcendentals=0),
        compiler_params=pltpu.CompilerParams(vmem_limit_bytes=limit),
    )(*inputs)


def row_tiles(rows):
    return [slice(TILE * t, TILE * (t + 1)) for t in range(rows // TILE)]


def stream(far_refs, near_refs, sems):
    tiles = row_tiles(far_refs[0].shape[0])
    copies = [
        [pltpu.make_async_copy(far.at[here, :], near.at[here, :], sems.at[i, t])
         for i, (far, near) in enumerate(zip(far_refs, near_refs))]
        for t, here in enumerate(tiles)
    ]
    for tile in copies:
        for copy in tile:
            copy.start()

    def wait(t):
        for copy in copies[t]:
            copy.wait()

    return wait


def gather_rows(pieces, whole_ref):
    at = 0
    for piece in pieces:
        whole_ref[at : at + piece.shape[0], :] = piece[...]
        at += piece.shape[0]


def fine_open(own, sib, steps, flops):
    rank = own[0].shape[1]
    count = len(own)

    def kernel(*refs):
        own_refs, sib_refs = refs[:count], refs[count : 2 * count]
        a_ref, t_ref, far_ref, own_ref = refs[2 * count :]
        gather_rows(own_refs, own_ref)
        gather_rows(sib_refs, far_ref)
        t_ref[...] = identity_less(product(far_ref[...], own_ref[...]))
        a_ref[...] = dot(t_ref[...], t_ref[...], ((1,), (1,)))
        eliminate(a_ref, t_ref, steps)

    square = (rank, rank)
    return call(kernel, [*own, *sib], [square] * 3, [square], flops=flops)


def fine_steps(a, t, gram, steps, flops):
    def kernel(a_in, t_in, gram_in, a_ref, t_ref, gram_ref):
        a_ref[...] = a_in[...]
        t_ref[...] = t_in[...]
        gram_ref[...] = gram_in[...]
        eliminate(a_ref, t_ref, steps)

    return call(kernel, [a, t, gram], [a.shape, t.shape, gram.shape], flops=flops)


def fine_close(pattern, a, t, gram, steps, arrays, flops):
    rank = a.shape[0]
    rows, nrhs = arrays[3].shape
    tiles = row_tiles(rows)

    def kernel(pattern_ref, a_in, t_in, gram_in, *refs):
        far_refs, (out_ref, gram_ref, high_ref, low_ref, sum_ref) = refs[:4], refs[4:9]
        near_refs, (part_ref, a_ref, t_ref, sems) = refs[9:13], refs[13:]
        basis_ref, dual_ref, coarse_ref, right_ref = near_refs
        wait = stream(far_refs, near_refs, sems)
        gram_ref[...] = gram_in[...]
        a_ref[...] = a_in[...]
        t_ref[...] = t_in[...]
        eliminate(a_ref, t_ref, steps)
        for k, here in enumerate(tiles):
            wait(k)
            dual = split(dual_ref[here, :].T)
            masked = blocks_masked(pattern_ref, basis_ref[here, :], k * (TILE // BLK))
            for hand, to_ref, columns in (
                (masked, part_ref, slice(0, rank)),
                (coarse_ref[here, :], sum_ref, slice(0, rank)),
                (right_ref[here, :], sum_ref, slice(rank, rank + nrhs)),
            ):
                part = dot3(dual, split(hand), ((1,), (0,)))
                to_ref[:, columns] = part if k == 0 else to_ref[:, columns] + part
        high_ref[...], low_ref[...] = split(part_ref[...])
        out_ref[...] = t_ref[...].T

    return call(
        kernel,
        [pattern, a, t, gram, *arrays],
        [t.shape, gram.shape, *halves(a.shape), (rank, rank + nrhs)],
        [*(array.shape for array in arrays), *[a.shape] * 3, pltpu.SemaphoreType.DMA((4, len(tiles)))],
        scalars=1,
        flops=flops,
        far_in=range(4, 8),
    )


def halves(shape):
    return [jax.ShapeDtypeStruct(shape, jnp.bfloat16)] * 2


def split(value):
    high = value.astype(jnp.bfloat16)
    return high, (value - high.astype(jnp.float32)).astype(jnp.bfloat16)


def dot3(left, right, dims):
    part = lambda a, b: lax.dot_general(a, b, (dims, ((), ())), preferred_element_type=jnp.float32)
    return part(left[0], right[0]) + (part(left[0], right[1]) + part(left[1], right[0]))


def blocks_masked(pattern_ref, basis, at):
    rows = []
    for i in range(basis.shape[0] // BLK):
        here = basis[BLK * i : BLK * (i + 1), :]
        row = [
            here[:, BLK * j : BLK * (j + 1)] * pattern_ref[at + i, j].astype(jnp.float32)
            for j in range(basis.shape[1] // BLK)
        ]
        rows.append(jnp.concatenate(row, axis=1))
    return jnp.concatenate(rows, axis=0)


def fine_gram(pattern, basis, dual):
    rows, rank = basis.shape
    piece = rank // PIECES
    tiles = row_tiles(rows)

    def kernel(pattern_ref, basis_far, dual_far, *refs):
        out_refs, (basis_ref, dual_ref, sum_ref, sems) = refs[:-4], refs[-4:]
        wait = stream((basis_far, dual_far), (basis_ref, dual_ref), sems)
        for t, here in enumerate(tiles):
            wait(t)
            masked = blocks_masked(pattern_ref, basis_ref[here, :], t * (TILE // BLK))
            part = contract(dual_ref[here, :], masked)
            sum_ref[...] = part if t == 0 else sum_ref[...] + part
        for i, out_ref in enumerate(out_refs):
            out_ref[...] = sum_ref[piece * i : piece * (i + 1), :]

    return call(
        kernel,
        [pattern, basis, dual],
        [(piece, rank)] * PIECES,
        [basis.shape, dual.shape, (rank, rank), pltpu.SemaphoreType.DMA((2, len(tiles)))],
        scalars=1,
        flops=12 * rows * rank * rank,
        far_in=(1, 2),
        limit=STREAM_LIMIT,
    )


def fine_moment(dual, coarse, right, cuts):
    rows, rank = dual.shape
    width = rank + right.shape[1]
    tiles = row_tiles(rows)

    def kernel(dual_far, coarse_far, right_far, *refs):
        out_refs, (dual_ref, coarse_ref, right_ref, sum_ref, sems) = refs[:-5], refs[-5:]
        wait = stream((dual_far, coarse_far, right_far), (dual_ref, coarse_ref, right_ref), sems)
        for t, here in enumerate(tiles):
            wait(t)
            left = split(dual_ref[here, :])
            for hand, columns in ((coarse_ref, slice(0, rank)), (right_ref, slice(rank, width))):
                part = dot3(left, split(hand[here, :]), ((0,), (0,)))
                sum_ref[:, columns] = part if t == 0 else sum_ref[:, columns] + part
        for low, high, out_ref in zip(cuts, cuts[1:], out_refs):
            out_ref[...] = sum_ref[low:high, :]

    return call(
        kernel,
        [dual, coarse, right],
        [(high - low, width) for low, high in zip(cuts, cuts[1:])],
        [dual.shape, coarse.shape, right.shape, (rank, width), pltpu.SemaphoreType.DMA((3, len(tiles)))],
        flops=6 * rows * rank * width,
        far_in=(0, 1, 2),
        limit=STREAM_LIMIT,
    )


def coarse_parts(core, inverse, gram, own, sib, part, total, columns, flops):
    rank = gram.shape[0]
    half = rank // 2
    count = len(own)
    low, high = columns[0].start, columns[-1].stop
    width = high - low

    def kernel(core_ref, inv_ref, gram_ref, *refs):
        own_refs, sib_refs = refs[:count], refs[count : 2 * count]
        part_refs, total_ref = refs[2 * count : 2 * count + 2], refs[2 * count + 2]
        high_ref, low_ref = refs[2 * count + 3 : 2 * count + 5]
        keep_refs = refs[2 * count + 5 : 2 * count + 5 + len(columns)]
        send_refs = refs[2 * count + 5 + len(columns) : 2 * count + 5 + 2 * len(columns)]
        own_ref, far_ref = refs[2 * count + 5 + 2 * len(columns) :]
        gather_rows([ref.at[:, low:high] for ref in own_refs], own_ref)
        gather_rows([ref.at[:, low:high] for ref in sib_refs], far_ref)
        target = far_ref[...] - dot3(split(gram_ref[...]), split(own_ref[...]), ((1,), (0,)))
        coeffs = split(product(inv_ref[...], target))
        high_ref[...], low_ref[...] = coeffs
        for side, out_refs in ((1 - core_ref[0], send_refs), (core_ref[0], keep_refs)):
            here = pl.ds(pl.multiple_of(side * half, half), half)
            less = dot3([ref[here, :] for ref in part_refs], coeffs, ((1,), (0,)))
            for at, out_ref in zip(columns, out_refs):
                out_ref[...] = total_ref[here, at] - less[:, at.start - low : at.stop - low]

    pieces = [(half, at.stop - at.start) for at in columns]
    outs = call(
        kernel,
        [core, inverse, gram, *own, *sib, *part, total],
        [*halves((rank, width)), *pieces, *pieces],
        [(rank, width)] * 2,
        scalars=1,
        flops=flops,
    )
    return list(outs[:2]), outs[2 : 2 + len(columns)], outs[2 + len(columns) :]


def fine_update(pattern, basis, coarse, right, coeffs, flops):
    rows, rank = basis.shape
    nrhs = right.shape[1]

    def kernel(pattern_ref, basis_ref, coarse_ref, right_ref, *refs):
        coeff_refs, (new_ref, updated_ref) = refs[:-2], refs[-2:]
        for t, here in enumerate(row_tiles(rows)):
            masked = split(blocks_masked(pattern_ref, basis_ref[here, :], t * (TILE // BLK)))
            at = 0
            for high_ref, low_ref in zip(coeff_refs[::2], coeff_refs[1::2]):
                less = dot3(masked, (high_ref[...], low_ref[...]), ((1,), (0,)))
                for i in range(0, less.shape[1], BLK):
                    old_ref, to_ref, start = (
                        (coarse_ref, new_ref, at + i) if at + i < rank else (right_ref, updated_ref, at + i - rank)
                    )
                    to = slice(start, start + BLK)
                    to_ref[here, to] = old_ref[here, to] - less[:, i : i + BLK]
                at += less.shape[1]

    return call(
        kernel,
        [pattern, basis, coarse, right, *[half for pair in coeffs for half in pair]],
        [(rows, rank), (rows, nrhs)],
        scalars=1,
        flops=flops,
    )


def top_half(core, mine, other, far_mine, far_other, basis):
    count = len(mine)
    half, width = mine[0].shape[0], sum(piece.shape[1] for piece in mine)
    rank = 2 * half
    nrhs = width - rank
    rows = basis[0].shape[0]

    def kernel(core_ref, *refs):
        lists = [refs[count * i : count * (i + 1)] for i in range(4)]
        basis_refs = refs[4 * count : 4 * count + len(basis)]
        out_ref, whole_basis, own_ref, far_ref, c_ref, a_ref, t_ref, sems = refs[4 * count + len(basis) :]
        copies, at = [], 0
        for i, part in enumerate(basis_refs):
            there = whole_basis.at[:, at : at + part.shape[1]]
            copies.append(pltpu.make_async_copy(part, there, sems.at[i]))
            copies[-1].start()
            at += part.shape[1]
        for first, second, whole_ref in ((*lists[:2], own_ref), (*lists[2:], far_ref)):
            for side, pieces in ((core_ref[0], first), (1 - core_ref[0], second)):
                here, at = pl.ds(pl.multiple_of(side * half, half), half), 0
                for part in pieces:
                    whole_ref[here, at : at + part.shape[1]] = part[...]
                    at += part.shape[1]
        c_ref[...] = identity_less(product(far_ref[:, :rank], own_ref[:, :rank]))
        t_ref[...] = far_ref[:, rank:] - product(far_ref[:, :rank], own_ref[:, rank:])
        a_ref[...] = dot(c_ref[...], c_ref[...], ((1,), (1,)))
        eliminate(a_ref, t_ref, range(rank // LANE))
        here = pl.ds(pl.multiple_of(core_ref[0] * half, half), half)
        out_ref[...] = contract(c_ref[:, here], t_ref[...])
        for copy in copies:
            copy.wait()

    square, wide = (rank, rank), (rank, width)
    return call(
        kernel,
        [core, *mine, *other, *far_mine, *far_other, *basis],
        [(half, nrhs), (rows, rank)],
        [wide, wide, square, square, (rank, nrhs), pltpu.SemaphoreType.DMA((len(basis),))],
        scalars=1,
        flops=1 << 34,
        far_out=(1,),
    )


def final_update(core, mine, other, basis, updated):
    half, nrhs = mine.shape
    rows = updated.shape[0]
    tiles = row_tiles(rows)

    def kernel(core_ref, mine_ref, other_ref, *refs):
        basis_refs, (updated_ref, out_far, coeffs_ref, out_ref, sems) = refs[:-5], refs[-5:]
        for side, part in ((core_ref[0], mine_ref), (1 - core_ref[0], other_ref)):
            coeffs_ref[pl.ds(pl.multiple_of(side * half, half), half), :] = part[...]
        copies = []
        for t, here in enumerate(tiles):
            total, at = updated_ref[here, :], 0
            for part in basis_refs:
                coeffs = split(coeffs_ref[at : at + part.shape[1], :])
                total = total - dot3(split(part[here, :]), coeffs, ((1,), (0,)))
                at += part.shape[1]
            out_ref[here, :] = total
            copies.append(pltpu.make_async_copy(out_ref.at[here, :], out_far.at[here, :], sems.at[t]))
            copies[-1].start()
        for copy in copies:
            copy.wait()

    return call(
        kernel,
        [core, mine, other, *basis, updated],
        [(rows, nrhs)],
        [(2 * half, nrhs), (rows, nrhs), pltpu.SemaphoreType.DMA((len(tiles),))],
        scalars=1,
        flops=12 * rows * half * nrhs,
        far_out=(0,),
    )[0]


def swapped(value, axis, distance):
    mask = 2**distance
    pairs = [(source, source ^ mask) for source in range(lax.axis_size(axis))]
    return lax.ppermute(value, axis, pairs)


def after(value, *others):
    return lax.optimization_barrier((value, *others))[0]


def hop_count(axis):
    return 2 * (lax.axis_size(axis) // 2) - 1


def hop_pairs(axis, hop):
    size = lax.axis_size(axis)
    half = size // 2
    if hop == half - 1:
        return [(half - 1, half), (half, half - 1)]
    if hop < half - 1:
        return [(hop, hop + 1), (size - 1 - hop, size - 2 - hop)]
    t = 2 * half - 2 - hop
    return [(t + 1, t), (size - 2 - t, size - 1 - t)]


def leave(value, axis, hop):
    return lax.ppermute(value, axis, hop_pairs(axis, hop))


def arrive(value, arrived, axis, hop):
    size = lax.axis_size(axis)
    if hop < size // 2:
        return value + arrived
    here = lax.axis_index(axis)
    t = 2 * (size // 2) - 2 - hop
    return jnp.where((here == t) | (here == size - 1 - t), arrived, value)


def line_hops(values, axis, first, last, lag=None):
    values = list(values)
    for hop in range(first, last):
        moved = []
        for i, value in enumerate(values):
            if lag and i >= lag and hop == hop_count(axis) // 2:
                value = after(value, moved[i - lag])
            moved.append(arrive(value, leave(value, axis, hop), axis, hop))
        values = moved
    return values


def cross(value, hop):
    return arrive(value, leave(value, "row", hop), "row", hop)


def shards(basis_fine, dual_fine, basis_coarse, dual_coarse, right_side, pattern):
    rank, nrhs = basis_fine.shape[1], right_side.shape[1]
    half = rank // 2
    hops = hop_count("row")
    middle = hops // 2 + 1
    core = (lax.axis_index("sib") % 2)[None]

    gram = fine_gram(pattern, basis_fine, dual_fine)
    moment = fine_moment(after(dual_fine, gram[0]), basis_coarse, right_side, [0, half, rank])
    leaving = [leave(piece, "row", 0) for piece in gram]
    gram = lax.optimization_barrier((*gram, *moment))[: len(gram)]
    gram = [arrive(piece, arrived, "row", 0) for piece, arrived in zip(gram, leaving)]
    gram = line_hops(gram, "row", 1, middle, lag=2)
    first, second = moment
    first = after(first, gram[1])
    for hop in range(middle - 1):
        first = cross(first, hop)
    gram = line_hops(gram, "row", middle, hops)
    gram_sib = [swapped(piece, "sib", 0) for piece in gram]
    second = after(second, first)
    first_flying, second_flying = leave(first, "row", middle - 1), leave(second, "row", 0)
    *gram, first = lax.optimization_barrier((*gram, first))
    normal, solved, gram_sib = fine_open(gram, gram_sib, range(1), 1 << 24)

    first, second, normal = lax.optimization_barrier((first, second, normal))
    second = arrive(second, second_flying, "row", 0)
    for hop in range(1, middle - 1):
        second = cross(second, hop)
    first = arrive(first, first_flying, "row", middle - 1)
    normal, first, second = lax.optimization_barrier((normal, first, second))
    second_flying, first_flying = leave(second, "row", middle - 1), leave(first, "row", middle)
    normal, solved, gram_sib = fine_steps(normal, solved, gram_sib, range(1, 3), 1 << 24)

    first, second, normal = lax.optimization_barrier((first, second, normal))
    second = arrive(second, second_flying, "row", middle - 1)
    second, normal = lax.optimization_barrier((second, normal))
    second_flying = leave(second, "row", middle)
    inverse, gram_sib, *part, total = fine_close(
        pattern, normal, solved, gram_sib, range(3, rank // LANE),
        [basis_fine, dual_coarse, basis_coarse, right_side], 1 << 24,
    )
    first, second, inverse = lax.optimization_barrier((first, second, inverse))
    first = arrive(first, first_flying, "row", middle)
    second = arrive(second, second_flying, "row", middle)
    moment = [first, second]
    for hop in range(middle + 1, hops):
        moment = [cross(value, hop) for value in moment]
    moment_sib = [swapped(piece, "sib", 0) for piece in moment]

    coeffs, parts = [], []
    for columns in ([slice(0, half)], [slice(half, rank), slice(rank, rank + nrhs)]):
        if coeffs:
            total = after(total, coeffs[0][0])
        pair, keep, send = coarse_parts(
            core, inverse, gram_sib, moment, moment_sib, part, total, columns, 1 << 28
        )
        coeffs.append(pair)
        parts += [own + swapped(other, "sib", 0) for own, other in zip(keep, send)]
    parts = line_hops(parts, "row", 0, middle)
    coeffs[0][0] = after(coeffs[0][0], *parts)
    new, updated = fine_update(pattern, basis_fine, basis_coarse, right_side, coeffs, 1 << 32)
    far = [after(swapped(value, "sib", 1), new) for value in parts]
    parts_other = [swapped(value, "sib", 0) for value in parts]
    far_other = [swapped(value, "sib", 0) for value in far]
    basis = [new]
    result, whole_basis = top_half(core, parts, parts_other, far, far_other, basis)
    result = line_hops([result], "row", middle, hops)[0]
    solution = final_update(core, result, swapped(result, "sib", 0), basis, updated)
    return (whole_basis, solution)


def solution(mesh):
    rows = P(("grp", "sib", "row"), None)
    return jax.shard_map(
        shards,
        mesh=mesh,
        in_specs=(rows,) * 6,
        out_specs=(rows, rows),
        check_vma=False,
    )
```

```python
import jax
import jax.numpy as jnp
from jax import lax
from jax.experimental import pallas as pl
from jax.experimental.pallas import tpu as pltpu
from jax.sharding import PartitionSpec as P

BLK = 128
SUB, LANE, PANEL = 8, 128, 32
PIECES = 3
TILE = 256
HIGH = lax.Precision.HIGHEST
WHOLE = pl.BlockSpec(memory_space=pltpu.VMEM)
FAR = pl.BlockSpec(memory_space=pltpu.HBM)
SCALARS = pl.BlockSpec(memory_space=pltpu.SMEM)
VMEM_LIMIT = 20 << 20
STREAM_LIMIT = 62 << 20


def dot(left, right, dims):
    return lax.dot_general(left, right, (dims, ((), ())), precision=HIGH, preferred_element_type=jnp.float32)


def product(left, right):
    return dot(left, right, ((1,), (0,)))


def contract(left, right):
    return dot(left, right, ((0,), (0,)))


def inverse_of(value):
    guess = pl.reciprocal(value, approx=True)
    guess = guess * (2.0 - value * guess)
    return guess * (2.0 - value * guess)


def block_inverse(block):
    size = block.shape[0]
    shape = (SUB, size)
    sub = lax.broadcasted_iota(jnp.int32, shape, 0)
    lane = lax.broadcasted_iota(jnp.int32, shape, 1)
    groups, tall = size // SUB, PANEL // SUB
    rows = [block[SUB * g : SUB * (g + 1), :] for g in range(groups)]
    down = lambda value, at: jnp.broadcast_to(value[at : at + 1, :], shape)
    across = lambda value, at: jnp.broadcast_to(value[:, at : at + 1], shape)
    for start in range(0, groups, tall):
        within = range(start, start + tall)
        for g in within:
            first = SUB * g
            panel = rows[g]
            heads = [across(panel, first + j) for j in range(SUB)]
            for s in range(0, SUB, 2):
                pair = heads[s], heads[s + 1]
                mid = down(pair[0], s + 1)
                low, high = down(pair[0], s), down(pair[1], s + 1)
                scale = inverse_of(low * high - mid * mid)
                ends, cross = (high * scale, low * scale), -mid * scale
                solve = lambda first_row, second_row: (
                    ends[0] * first_row + cross * second_row,
                    cross * first_row + ends[1] * second_row,
                )
                place = lambda value, tops: jnp.where(
                    sub == s,
                    tops[0],
                    jnp.where(sub == s + 1, tops[1], value - pair[0] * tops[0] - pair[1] * tops[1]),
                )
                here = (lane == first + s) | (lane == first + s + 1)
                tops = solve(down(panel, s), down(panel, s + 1))
                tops = (
                    jnp.where(here, jnp.where(lane == first + s, ends[0], cross), tops[0]),
                    jnp.where(here, jnp.where(lane == first + s, cross, ends[1]), tops[1]),
                )
                panel = place(jnp.where(here, 0.0, panel), tops)
                for j in range(s + 2, SUB):
                    heads[j] = place(heads[j], solve(down(heads[j], s), down(heads[j], s + 1)))
            rows[g] = panel
            tops = [down(panel, j) for j in range(SUB)]
            inside = (lane >= first) & (lane < first + SUB)
            for h in within:
                if h != g:
                    terms = [across(rows[h], first + j) * tops[j] for j in range(SUB)]
                    while len(terms) > 1:
                        terms = [terms[i] + terms[i + 1] for i in range(0, len(terms), 2)]
                    rows[h] = jnp.where(inside, 0.0, rows[h]) - terms[0]
        inside = (lane >= SUB * start) & (lane < SUB * (start + tall))
        zero = jnp.zeros(shape, jnp.float32)
        side = [zero if h in within else jnp.where(inside, rows[h], 0.0) for h in range(groups)]
        top = [rows[h] if h in within else zero for h in range(groups)]
        less = product(jnp.concatenate(side, axis=0), jnp.concatenate(top, axis=0))
        for h in range(groups):
            if h not in within:
                rows[h] = jnp.where(inside, 0.0, rows[h]) - less[SUB * h : SUB * (h + 1), :]
    return jnp.concatenate(rows, axis=0)


def eliminate(a_ref, t_ref, steps):
    rank = a_ref.shape[0]
    blocks = rank // LANE
    at = lambda j: slice(LANE * j, LANE * (j + 1))
    for j in steps:
        rest = slice(LANE * (j + 1), rank)
        inv = block_inverse(a_ref[at(j), at(j)])
        others = [i for i in range(j + 1, blocks)] + [i for i in range(j)]
        if j < blocks - 1:
            top = product(inv, a_ref[at(j), rest])
            a_ref[at(j), rest] = top
            for i in others:
                a_ref[at(i), rest] = a_ref[at(i), rest] - product(a_ref[at(i), at(j)], top)
        top = product(inv, t_ref[at(j), :])
        t_ref[at(j), :] = top
        for i in others:
            t_ref[at(i), :] = t_ref[at(i), :] - product(a_ref[at(i), at(j)], top)


def unit_rows(value):
    scale = lax.rsqrt(jnp.sum(value * value, axis=1, keepdims=True))
    return value * scale, jnp.broadcast_to(scale, (value.shape[0], LANE))


def identity_less(value):
    row = lax.broadcasted_iota(jnp.int32, value.shape, 0)
    col = lax.broadcasted_iota(jnp.int32, value.shape, 1)
    return jnp.where(row == col, 1.0, 0.0) - value


def call(kernel, inputs, outputs, scratch=(), scalars=0, flops=0, far_in=(), far_out=(), limit=VMEM_LIMIT):
    return pl.pallas_call(
        kernel,
        out_shape=[
            jax.ShapeDtypeStruct(shape, jnp.float32) if isinstance(shape, tuple) else shape for shape in outputs
        ],
        in_specs=[SCALARS if i < scalars else FAR if i in far_in else WHOLE for i in range(len(inputs))],
        out_specs=[FAR if i in far_out else WHOLE for i in range(len(outputs))],
        scratch_shapes=[
            pltpu.VMEM(shape, jnp.float32) if isinstance(shape, tuple) else shape for shape in scratch
        ],
        cost_estimate=pl.CostEstimate(flops=flops, bytes_accessed=8 << 20, transcendentals=0),
        compiler_params=pltpu.CompilerParams(vmem_limit_bytes=limit),
    )(*inputs)


def cuts(rows, count):
    step = -(-rows // count // 16) * 16 if rows % (16 * count) else rows // count
    return [slice(low, min(low + step, rows)) for low in range(0, rows, step)]


def row_tiles(rows):
    return [slice(TILE * t, TILE * (t + 1)) for t in range(rows // TILE)]


def stream(far_refs, near_refs, sems):
    tiles = row_tiles(far_refs[0].shape[0])
    copies = [
        [pltpu.make_async_copy(far.at[here, :], near.at[here, :], sems.at[i, t])
         for i, (far, near) in enumerate(zip(far_refs, near_refs))]
        for t, here in enumerate(tiles)
    ]
    for tile in copies:
        for copy in tile:
            copy.start()

    def wait(t):
        for copy in copies[t]:
            copy.wait()

    return wait


def gather_rows(pieces, whole_ref):
    at = 0
    for piece in pieces:
        whole_ref[at : at + piece.shape[0], :] = piece[...]
        at += piece.shape[0]


def fine_open(own, sib, steps, flops):
    rank = own[0].shape[1]
    count = len(own)

    def kernel(*refs):
        own_refs, sib_refs = refs[:count], refs[count : 2 * count]
        a_ref, t_ref, scale_ref, far_ref, own_ref = refs[2 * count :]
        gather_rows(own_refs, own_ref)
        gather_rows(sib_refs, far_ref)
        t_ref[...], scale_ref[...] = unit_rows(identity_less(product(far_ref[...], own_ref[...])))
        a_ref[...] = dot(t_ref[...], t_ref[...], ((1,), (1,)))
        eliminate(a_ref, t_ref, steps)

    square = (rank, rank)
    return call(kernel, [*own, *sib], [square, square, (rank, LANE), square], [square], flops=flops)


def fine_steps(a, t, scale, gram, steps, flops):
    def kernel(a_in, t_in, scale_in, gram_in, a_ref, t_ref, scale_ref, gram_ref):
        a_ref[...] = a_in[...]
        t_ref[...] = t_in[...]
        scale_ref[...] = scale_in[...]
        gram_ref[...] = gram_in[...]
        eliminate(a_ref, t_ref, steps)

    arrays = [a, t, scale, gram]
    return call(kernel, arrays, [array.shape for array in arrays], flops=flops)


def fine_close(pattern, a, t, scale, gram, steps, arrays, flops):
    rank = a.shape[0]
    rows, nrhs = arrays[3].shape
    tiles = row_tiles(rows)

    def kernel(pattern_ref, a_in, t_in, scale_in, gram_in, *refs):
        far_refs, (out_ref, gram_ref, high_ref, low_ref, sum_ref) = refs[:4], refs[4:9]
        near_refs, (part_ref, a_ref, t_ref, sems) = refs[9:13], refs[13:]
        basis_ref, dual_ref, coarse_ref, right_ref = near_refs
        wait = stream(far_refs, near_refs, sems)
        gram_ref[...] = gram_in[...]
        a_ref[...] = a_in[...]
        t_ref[...] = t_in[...]
        eliminate(a_ref, t_ref, steps)
        for k, here in enumerate(tiles):
            wait(k)
            dual = split(dual_ref[here, :].T)
            masked = blocks_masked(pattern_ref, basis_ref[here, :], k * (TILE // BLK))
            for hand, to_ref, columns in (
                (masked, part_ref, slice(0, rank)),
                (coarse_ref[here, :], sum_ref, slice(0, rank)),
                (right_ref[here, :], sum_ref, slice(rank, rank + nrhs)),
            ):
                part = dot3(dual, split(hand), ((1,), (0,)))
                to_ref[:, columns] = part if k == 0 else to_ref[:, columns] + part
        high_ref[...], low_ref[...] = split(part_ref[...])
        for here in row_tiles(rank):
            for at in range(0, rank, LANE):
                to = slice(at, at + LANE)
                out_ref[to, here] = (t_ref[here, to] * scale_in[here, :]).T

    return call(
        kernel,
        [pattern, a, t, scale, gram, *arrays],
        [t.shape, gram.shape, *halves(a.shape), (rank, rank + nrhs)],
        [*(array.shape for array in arrays), *[a.shape] * 3, pltpu.SemaphoreType.DMA((4, len(tiles)))],
        scalars=1,
        flops=flops,
        far_in=range(5, 9),
    )


def halves(shape):
    return [jax.ShapeDtypeStruct(shape, jnp.bfloat16)] * 2


def split(value):
    high = value.astype(jnp.bfloat16)
    return high, (value - high.astype(jnp.float32)).astype(jnp.bfloat16)


def dot3(left, right, dims):
    part = lambda a, b: lax.dot_general(a, b, (dims, ((), ())), preferred_element_type=jnp.float32)
    return part(left[0], right[0]) + (part(left[0], right[1]) + part(left[1], right[0]))


def blocks_masked(pattern_ref, basis, at):
    rows = []
    for i in range(basis.shape[0] // BLK):
        here = basis[BLK * i : BLK * (i + 1), :]
        row = [
            here[:, BLK * j : BLK * (j + 1)] * pattern_ref[at + i, j].astype(jnp.float32)
            for j in range(basis.shape[1] // BLK)
        ]
        rows.append(jnp.concatenate(row, axis=1))
    return jnp.concatenate(rows, axis=0)


def fine_gram(pattern, basis, dual):
    rows, rank = basis.shape
    pieces = cuts(rank, PIECES)
    tiles = row_tiles(rows)

    def kernel(pattern_ref, basis_far, dual_far, *refs):
        out_refs, (basis_ref, dual_ref, sum_ref, sems) = refs[:-4], refs[-4:]
        wait = stream((basis_far, dual_far), (basis_ref, dual_ref), sems)
        for t, here in enumerate(tiles):
            wait(t)
            masked = blocks_masked(pattern_ref, basis_ref[here, :], t * (TILE // BLK))
            part = contract(dual_ref[here, :], masked)
            sum_ref[...] = part if t == 0 else sum_ref[...] + part
        for piece, out_ref in zip(pieces, out_refs):
            out_ref[...] = sum_ref[piece, :]

    return call(
        kernel,
        [pattern, basis, dual],
        [(piece.stop - piece.start, rank) for piece in pieces],
        [basis.shape, dual.shape, (rank, rank), pltpu.SemaphoreType.DMA((2, len(tiles)))],
        scalars=1,
        flops=12 * rows * rank * rank,
        far_in=(1, 2),
        limit=STREAM_LIMIT,
    )


def fine_moment(dual, coarse, right, cuts):
    rows, rank = dual.shape
    width = rank + right.shape[1]
    tiles = row_tiles(rows)

    def kernel(dual_far, coarse_far, right_far, *refs):
        out_refs, (dual_ref, coarse_ref, right_ref, sum_ref, sems) = refs[:-5], refs[-5:]
        wait = stream((dual_far, coarse_far, right_far), (dual_ref, coarse_ref, right_ref), sems)
        for t, here in enumerate(tiles):
            wait(t)
            left = split(dual_ref[here, :])
            for hand, columns in ((coarse_ref, slice(0, rank)), (right_ref, slice(rank, width))):
                part = dot3(left, split(hand[here, :]), ((0,), (0,)))
                sum_ref[:, columns] = part if t == 0 else sum_ref[:, columns] + part
        for low, high, out_ref in zip(cuts, cuts[1:], out_refs):
            out_ref[...] = sum_ref[low:high, :]

    return call(
        kernel,
        [dual, coarse, right],
        [(high - low, width) for low, high in zip(cuts, cuts[1:])],
        [dual.shape, coarse.shape, right.shape, (rank, width), pltpu.SemaphoreType.DMA((3, len(tiles)))],
        flops=6 * rows * rank * width,
        far_in=(0, 1, 2),
        limit=STREAM_LIMIT,
    )


def coarse_sent(core, inverse, gram, own, sib, part, total, flops):
    rank = gram.shape[0]
    half, width = rank // 2, total.shape[1]
    count = len(own)

    def kernel(core_ref, *refs):
        own_refs, sib_refs, fars = refs[:count], refs[count : 2 * count], refs[2 * count : 2 * count + 5]
        high_ref, low_ref, send_ref, own_ref, far_ref = refs[2 * count + 5 : 2 * count + 10]
        nears, sems = refs[2 * count + 10 : -1], refs[-1]
        gram_ref, inv_ref, part_high, part_low, total_ref = nears
        sent = pl.ds(pl.multiple_of((1 - core_ref[0]) * half, half), half)
        copies = [
            pltpu.make_async_copy(far if i < 2 else far.at[sent, :], near, sems.at[i])
            for i, (far, near) in enumerate(zip(fars, nears))
        ]
        for copy in copies:
            copy.start()
        gather_rows(own_refs, own_ref)
        gather_rows(sib_refs, far_ref)
        copies[0].wait()
        target = far_ref[...] - dot3(split(gram_ref[...]), split(own_ref[...]), ((1,), (0,)))
        copies[1].wait()
        coeffs = split(product(inv_ref[...], target))
        high_ref[...], low_ref[...] = coeffs
        for copy in copies[2:]:
            copy.wait()
        send_ref[...] = total_ref[...] - dot3((part_high[...], part_low[...]), coeffs, ((1,), (0,)))

    half_part = pltpu.VMEM((half, rank), jnp.bfloat16)
    return call(
        kernel,
        [core, *own, *sib, gram, inverse, *part, total],
        [*halves((rank, width)), (half, width)],
        [(rank, width)] * 2
        + [gram.shape, inverse.shape, half_part, half_part, (half, width), pltpu.SemaphoreType.DMA((5,))],
        scalars=1,
        flops=flops,
        far_in=range(1 + 2 * count, 6 + 2 * count),
    )


def coarse_kept(core, coeffs, part, total, flops):
    rank, width = total.shape
    half = rank // 2

    def kernel(core_ref, high_ref, low_ref, *refs):
        fars, keep_ref, nears, sems = refs[:3], refs[3], refs[4:7], refs[7]
        kept = pl.ds(pl.multiple_of(core_ref[0] * half, half), half)
        copies = [
            pltpu.make_async_copy(far.at[kept, :], near, sems.at[i]) for i, (far, near) in enumerate(zip(fars, nears))
        ]
        for copy in copies:
            copy.start()
        for copy in copies:
            copy.wait()
        coeffs = high_ref[...], low_ref[...]
        keep_ref[...] = nears[2][...] - dot3((nears[0][...], nears[1][...]), coeffs, ((1,), (0,)))

    half_part = pltpu.VMEM((half, rank), jnp.bfloat16)
    return call(
        kernel,
        [core, *coeffs, *part, total],
        [(half, width)],
        [half_part, half_part, (half, width), pltpu.SemaphoreType.DMA((3,))],
        scalars=1,
        flops=flops,
        far_in=(3, 4, 5),
    )[0]


def fine_update(pattern, basis, coarse, right, coeffs, flops):
    rows, rank = basis.shape
    nrhs = right.shape[1]

    def kernel(pattern_ref, basis_ref, coarse_ref, right_ref, *refs):
        coeff_refs, (new_ref, updated_ref) = refs[:-2], refs[-2:]
        for t, here in enumerate(row_tiles(rows)):
            masked = split(blocks_masked(pattern_ref, basis_ref[here, :], t * (TILE // BLK)))
            at = 0
            for high_ref, low_ref in zip(coeff_refs[::2], coeff_refs[1::2]):
                less = dot3(masked, (high_ref[...], low_ref[...]), ((1,), (0,)))
                for i in range(0, less.shape[1], BLK):
                    old_ref, to_ref, start = (
                        (coarse_ref, new_ref, at + i) if at + i < rank else (right_ref, updated_ref, at + i - rank)
                    )
                    to = slice(start, start + BLK)
                    to_ref[here, to] = old_ref[here, to] - less[:, i : i + BLK]
                at += less.shape[1]

    return call(
        kernel,
        [pattern, basis, coarse, right, *[half for pair in coeffs for half in pair]],
        [(rows, rank), (rows, nrhs)],
        scalars=1,
        flops=flops,
    )


def top_half(core, mine, other, far_mine, far_other, basis):
    count = len(mine)
    half, width = sum(piece.shape[0] for piece in mine), mine[0].shape[1]
    rank = 2 * half
    nrhs = width - rank
    rows = basis[0].shape[0]

    def kernel(core_ref, *refs):
        lists = [refs[count * i : count * (i + 1)] for i in range(4)]
        basis_refs = refs[4 * count : 4 * count + len(basis)]
        out_ref, whole_basis, own_ref, far_ref, c_ref, a_ref, t_ref, sems = refs[4 * count + len(basis) :]
        copies, at = [], 0
        for i, part in enumerate(basis_refs):
            there = whole_basis.at[:, at : at + part.shape[1]]
            copies.append(pltpu.make_async_copy(part, there, sems.at[i]))
            copies[-1].start()
            at += part.shape[1]
        for first, second, whole_ref in ((*lists[:2], own_ref), (*lists[2:], far_ref)):
            for side, pieces in ((core_ref[0], first), (1 - core_ref[0], second)):
                at = 0
                for part in pieces:
                    rows_here = pl.ds(pl.multiple_of(side * half + at, SUB), part.shape[0])
                    whole_ref[rows_here, :] = part[...]
                    at += part.shape[0]
        c_ref[...], scale = unit_rows(identity_less(product(far_ref[:, :rank], own_ref[:, :rank])))
        t_ref[...] = scale[:, :nrhs] * (far_ref[:, rank:] - product(far_ref[:, :rank], own_ref[:, rank:]))
        a_ref[...] = dot(c_ref[...], c_ref[...], ((1,), (1,)))
        eliminate(a_ref, t_ref, range(rank // LANE))
        here = pl.ds(pl.multiple_of(core_ref[0] * half, half), half)
        out_ref[...] = contract(c_ref[:, here], t_ref[...])
        for copy in copies:
            copy.wait()

    square, wide = (rank, rank), (rank, width)
    return call(
        kernel,
        [core, *mine, *other, *far_mine, *far_other, *basis],
        [(half, nrhs), (rows, rank)],
        [wide, wide, square, square, (rank, nrhs), pltpu.SemaphoreType.DMA((len(basis),))],
        scalars=1,
        flops=1 << 34,
        far_out=(1,),
    )


def final_update(core, mine, other, basis, updated):
    half, nrhs = mine.shape
    rows = updated.shape[0]
    tiles = row_tiles(rows)

    def kernel(core_ref, mine_ref, other_ref, *refs):
        basis_refs, (updated_ref, out_far, coeffs_ref, out_ref, sems) = refs[:-5], refs[-5:]
        for side, part in ((core_ref[0], mine_ref), (1 - core_ref[0], other_ref)):
            coeffs_ref[pl.ds(pl.multiple_of(side * half, half), half), :] = part[...]
        copies = []
        for t, here in enumerate(tiles):
            total, at = updated_ref[here, :], 0
            for part in basis_refs:
                coeffs = split(coeffs_ref[at : at + part.shape[1], :])
                total = total - dot3(split(part[here, :]), coeffs, ((1,), (0,)))
                at += part.shape[1]
            out_ref[here, :] = total
            copies.append(pltpu.make_async_copy(out_ref.at[here, :], out_far.at[here, :], sems.at[t]))
            copies[-1].start()
        for copy in copies:
            copy.wait()

    return call(
        kernel,
        [core, mine, other, *basis, updated],
        [(rows, nrhs)],
        [(2 * half, nrhs), (rows, nrhs), pltpu.SemaphoreType.DMA((len(tiles),))],
        scalars=1,
        flops=12 * rows * half * nrhs,
        far_out=(0,),
    )[0]


def swapped(value, axis, distance):
    mask = 2**distance
    pairs = [(source, source ^ mask) for source in range(lax.axis_size(axis))]
    return lax.ppermute(value, axis, pairs)


def after(value, *others):
    return lax.optimization_barrier((value, *others))[0]


def hop_count(axis):
    return 2 * (lax.axis_size(axis) // 2) - 1


def hop_pairs(axis, hop):
    size = lax.axis_size(axis)
    half = size // 2
    if hop == half - 1:
        return [(half - 1, half), (half, half - 1)]
    if hop < half - 1:
        return [(hop, hop + 1), (size - 1 - hop, size - 2 - hop)]
    t = 2 * half - 2 - hop
    return [(t + 1, t), (size - 2 - t, size - 1 - t)]


def leave(value, axis, hop):
    return lax.ppermute(value, axis, hop_pairs(axis, hop))


def arrive(value, arrived, axis, hop):
    size = lax.axis_size(axis)
    if hop < size // 2:
        return value + arrived
    here = lax.axis_index(axis)
    t = 2 * (size // 2) - 2 - hop
    return jnp.where((here == t) | (here == size - 1 - t), arrived, value)


def line_hops(values, axis, first, last, lag=None):
    values = list(values)
    for hop in range(first, last):
        moved = []
        for i, value in enumerate(values):
            if lag and i >= lag and hop == hop_count(axis) // 2:
                value = after(value, moved[i - lag])
            moved.append(arrive(value, leave(value, axis, hop), axis, hop))
        values = moved
    return values


def cross(value, hop):
    return arrive(value, leave(value, "row", hop), "row", hop)


def shards(basis_fine, dual_fine, basis_coarse, dual_coarse, right_side, pattern):
    rank, nrhs = basis_fine.shape[1], right_side.shape[1]
    half = rank // 2
    hops = hop_count("row")
    middle = hops // 2 + 1
    core = (lax.axis_index("sib") % 2)[None]

    gram = fine_gram(pattern, basis_fine, dual_fine)
    moment = fine_moment(after(dual_fine, gram[0]), basis_coarse, right_side, [0, half, rank])
    leaving = [leave(piece, "row", 0) for piece in gram]
    gram = lax.optimization_barrier((*gram, *moment))[: len(gram)]
    gram = [arrive(piece, arrived, "row", 0) for piece, arrived in zip(gram, leaving)]
    gram = line_hops(gram, "row", 1, middle)
    first, second = moment
    first = after(first, gram[1])
    for hop in range(middle - 1):
        first = cross(first, hop)
    gram = line_hops(gram, "row", middle, hops)
    gram_sib = [swapped(piece, "sib", 0) for piece in gram]
    second = after(second, first)
    first_flying, second_flying = leave(first, "row", middle - 1), leave(second, "row", 0)
    *gram, first = lax.optimization_barrier((*gram, first))
    normal, solved, scale, gram_sib = fine_open(gram, gram_sib, range(1), 1 << 24)

    first, second, normal = lax.optimization_barrier((first, second, normal))
    second = arrive(second, second_flying, "row", 0)
    for hop in range(1, middle - 1):
        second = cross(second, hop)
    first = arrive(first, first_flying, "row", middle - 1)
    normal, first, second = lax.optimization_barrier((normal, first, second))
    second_flying, first_flying = leave(second, "row", middle - 1), leave(first, "row", middle)
    normal, solved, scale, gram_sib = fine_steps(normal, solved, scale, gram_sib, range(1, 3), 1 << 24)

    first, second, normal = lax.optimization_barrier((first, second, normal))
    second = arrive(second, second_flying, "row", middle - 1)
    second, normal = lax.optimization_barrier((second, normal))
    second_flying = leave(second, "row", middle)
    inverse, gram_sib, *part, total = fine_close(
        pattern, normal, solved, scale, gram_sib, range(3, rank // LANE),
        [basis_fine, dual_coarse, basis_coarse, right_side], 1 << 24,
    )
    first, second, inverse = lax.optimization_barrier((first, second, inverse))
    first = arrive(first, first_flying, "row", middle)
    second = arrive(second, second_flying, "row", middle)
    moment = [first, second]
    for hop in range(middle + 1, hops):
        moment = [cross(value, hop) for value in moment]
    moment_sib = [swapped(piece, "sib", 0) for piece in moment]

    *coeffs, send = coarse_sent(core, inverse, gram_sib, moment, moment_sib, part, total, 1 << 28)
    keep = coarse_kept(core, coeffs, part, total, 1 << 24)
    whole = keep + swapped(send, "sib", 0)
    parts = lax.optimization_barrier([whole[piece, :] for piece in cuts(half, PIECES)])
    parts = line_hops(parts, "row", 0, middle, lag=2)
    coeffs[0] = after(coeffs[0], *parts)
    coeffs = [coeffs]
    new, updated = fine_update(pattern, basis_fine, basis_coarse, right_side, coeffs, 1 << 32)
    far = [after(swapped(value, "sib", 1), new) for value in parts]
    parts_other = [swapped(value, "sib", 0) for value in parts]
    far_other = [swapped(value, "sib", 0) for value in far]
    basis = [new]
    result, whole_basis = top_half(core, parts, parts_other, far, far_other, basis)
    result = line_hops([result], "row", middle, hops)[0]
    solution = final_update(core, result, swapped(result, "sib", 0), basis, updated)
    return (whole_basis, solution)


def solution(mesh):
    rows = P(("grp", "sib", "row"), None)
    return jax.shard_map(
        shards,
        mesh=mesh,
        in_specs=(rows,) * 6,
        out_specs=(rows, rows),
        check_vma=False,
    )
```

```python
import jax
import jax.numpy as jnp
from jax import lax
from jax.experimental import pallas as pl
from jax.experimental.pallas import tpu as pltpu
from jax.sharding import PartitionSpec as P

BLK = 128
SUB, LANE, PANEL = 8, 128, 32
PIECES = 3
TILE = 256
HIGH = lax.Precision.HIGHEST
WHOLE = pl.BlockSpec(memory_space=pltpu.VMEM)
FAR = pl.BlockSpec(memory_space=pltpu.HBM)
SCALARS = pl.BlockSpec(memory_space=pltpu.SMEM)
VMEM_LIMIT = 20 << 20
STREAM_LIMIT = 62 << 20


def dot(left, right, dims):
    return lax.dot_general(left, right, (dims, ((), ())), precision=HIGH, preferred_element_type=jnp.float32)


def product(left, right):
    return dot(left, right, ((1,), (0,)))


def contract(left, right):
    return dot(left, right, ((0,), (0,)))


def inverse_of(value):
    guess = pl.reciprocal(value, approx=True)
    guess = guess * (2.0 - value * guess)
    return guess * (2.0 - value * guess)


def sub_panel(panel, first, down, across, lane):
    rows = [down(panel, i) for i in range(SUB)]
    entry = {(i, j): across(rows[i], first + j) for i in range(SUB) for j in range(i + 1)}
    inside = (lane >= first) & (lane < first + SUB)
    rows = [jnp.where(inside, jnp.where(lane == first + i, 1.0, 0.0), row) for i, row in enumerate(rows)]
    lower, ends = {}, {}
    for s in range(0, SUB, 2):
        low, mid, high = entry[s, s], entry[s + 1, s], entry[s + 1, s + 1]
        scale = inverse_of(low * high - mid * mid)
        ends[s] = high * scale, -mid * scale, low * scale
        for i in range(s + 2, SUB):
            first_part, second_part = entry[i, s], entry[i, s + 1]
            lower[i, s] = first_part * ends[s][0] + second_part * ends[s][1]
            lower[i, s + 1] = first_part * ends[s][1] + second_part * ends[s][2]
        for i in range(s + 2, SUB):
            for j in range(s + 2, i + 1):
                entry[i, j] = entry[i, j] - (lower[i, s] * entry[j, s] + lower[i, s + 1] * entry[j, s + 1])
        for i in range(s + 2, SUB):
            rows[i] = rows[i] - (lower[i, s] * rows[s] + lower[i, s + 1] * rows[s + 1])
    for s in reversed(range(0, SUB, 2)):
        one, two = rows[s], rows[s + 1]
        rows[s] = ends[s][0] * one + ends[s][1] * two
        rows[s + 1] = ends[s][1] * one + ends[s][2] * two
        for at in (s, s + 1):
            for i in range(s + 2, SUB, 2):
                rows[at] = rows[at] - (lower[i, at] * rows[i] + lower[i + 1, at] * rows[i + 1])
    return rows


def block_inverse(block):
    size = block.shape[0]
    shape = (SUB, size)
    sub = lax.broadcasted_iota(jnp.int32, shape, 0)
    lane = lax.broadcasted_iota(jnp.int32, shape, 1)
    groups, tall = size // SUB, PANEL // SUB
    rows = [block[SUB * g : SUB * (g + 1), :] for g in range(groups)]
    down = lambda value, at: jnp.broadcast_to(value[at : at + 1, :], shape)
    across = lambda value, at: jnp.broadcast_to(value[:, at : at + 1], shape)
    for start in range(0, groups, tall):
        within = range(start, start + tall)
        for g in within:
            first = SUB * g
            tops = sub_panel(rows[g], first, down, across, lane)
            panel = tops[0]
            for i in range(1, SUB):
                panel = jnp.where(sub == i, tops[i], panel)
            rows[g] = panel
            inside = (lane >= first) & (lane < first + SUB)
            for h in within:
                if h != g:
                    terms = [across(rows[h], first + j) * tops[j] for j in range(SUB)]
                    while len(terms) > 1:
                        terms = [terms[i] + terms[i + 1] for i in range(0, len(terms), 2)]
                    rows[h] = jnp.where(inside, 0.0, rows[h]) - terms[0]
        inside = (lane >= SUB * start) & (lane < SUB * (start + tall))
        zero = jnp.zeros(shape, jnp.float32)
        side = [zero if h in within else jnp.where(inside, rows[h], 0.0) for h in range(groups)]
        top = [rows[h] if h in within else zero for h in range(groups)]
        less = product(jnp.concatenate(side, axis=0), jnp.concatenate(top, axis=0))
        for h in range(groups):
            if h not in within:
                rows[h] = jnp.where(inside, 0.0, rows[h]) - less[SUB * h : SUB * (h + 1), :]
    return jnp.concatenate(rows, axis=0)


def eliminate(a_ref, t_ref, steps):
    rank = a_ref.shape[0]
    blocks = rank // LANE
    at = lambda j: slice(LANE * j, LANE * (j + 1))
    for j in steps:
        rest = slice(LANE * (j + 1), rank)
        inv = block_inverse(a_ref[at(j), at(j)])
        others = [i for i in range(j + 1, blocks)] + [i for i in range(j)]
        if j < blocks - 1:
            top = product(inv, a_ref[at(j), rest])
            a_ref[at(j), rest] = top
            for i in others:
                a_ref[at(i), rest] = a_ref[at(i), rest] - product(a_ref[at(i), at(j)], top)
        top = product(inv, t_ref[at(j), :])
        t_ref[at(j), :] = top
        for i in others:
            t_ref[at(i), :] = t_ref[at(i), :] - product(a_ref[at(i), at(j)], top)


def unit_rows(value):
    scale = lax.rsqrt(jnp.sum(value * value, axis=1, keepdims=True))
    return value * scale, jnp.broadcast_to(scale, (value.shape[0], LANE))


def identity_less(value):
    row = lax.broadcasted_iota(jnp.int32, value.shape, 0)
    col = lax.broadcasted_iota(jnp.int32, value.shape, 1)
    return jnp.where(row == col, 1.0, 0.0) - value


def call(kernel, inputs, outputs, scratch=(), scalars=0, flops=0, far_in=(), far_out=(), limit=VMEM_LIMIT):
    return pl.pallas_call(
        kernel,
        out_shape=[
            jax.ShapeDtypeStruct(shape, jnp.float32) if isinstance(shape, tuple) else shape for shape in outputs
        ],
        in_specs=[SCALARS if i < scalars else FAR if i in far_in else WHOLE for i in range(len(inputs))],
        out_specs=[FAR if i in far_out else WHOLE for i in range(len(outputs))],
        scratch_shapes=[
            pltpu.VMEM(shape, jnp.float32) if isinstance(shape, tuple) else shape for shape in scratch
        ],
        cost_estimate=pl.CostEstimate(flops=flops, bytes_accessed=8 << 20, transcendentals=0),
        compiler_params=pltpu.CompilerParams(vmem_limit_bytes=limit),
    )(*inputs)


def cuts(rows, count):
    step = -(-rows // count // 16) * 16 if rows % (16 * count) else rows // count
    return [slice(low, min(low + step, rows)) for low in range(0, rows, step)]


def row_tiles(rows):
    return [slice(TILE * t, TILE * (t + 1)) for t in range(rows // TILE)]


def stream(far_refs, near_refs, sems):
    tiles = row_tiles(far_refs[0].shape[0])
    copies = [
        [pltpu.make_async_copy(far.at[here, :], near.at[here, :], sems.at[i, t])
         for i, (far, near) in enumerate(zip(far_refs, near_refs))]
        for t, here in enumerate(tiles)
    ]
    for tile in copies:
        for copy in tile:
            copy.start()

    def wait(t):
        for copy in copies[t]:
            copy.wait()

    return wait


def gather_rows(pieces, whole_ref):
    at = 0
    for piece in pieces:
        whole_ref[at : at + piece.shape[0], :] = piece[...]
        at += piece.shape[0]


def fine_open(own, sib, steps, flops):
    rank = own[0].shape[1]
    count = len(own)

    def kernel(*refs):
        own_refs, sib_refs = refs[:count], refs[count : 2 * count]
        a_ref, t_ref, scale_ref, far_ref, own_ref = refs[2 * count :]
        gather_rows(own_refs, own_ref)
        gather_rows(sib_refs, far_ref)
        t_ref[...], scale_ref[...] = unit_rows(identity_less(product(far_ref[...], own_ref[...])))
        a_ref[...] = dot(t_ref[...], t_ref[...], ((1,), (1,)))
        eliminate(a_ref, t_ref, steps)

    square = (rank, rank)
    return call(kernel, [*own, *sib], [square, square, (rank, LANE), square], [square], flops=flops)


def fine_steps(a, t, scale, gram, steps, flops):
    def kernel(a_in, t_in, scale_in, gram_in, a_ref, t_ref, scale_ref, gram_ref):
        a_ref[...] = a_in[...]
        t_ref[...] = t_in[...]
        scale_ref[...] = scale_in[...]
        gram_ref[...] = gram_in[...]
        eliminate(a_ref, t_ref, steps)

    arrays = [a, t, scale, gram]
    return call(kernel, arrays, [array.shape for array in arrays], flops=flops)


def fine_close(pattern, a, t, scale, gram, steps, arrays, flops):
    rank = a.shape[0]
    rows, nrhs = arrays[3].shape
    tiles = row_tiles(rows)

    def kernel(pattern_ref, a_in, t_in, scale_in, gram_in, *refs):
        far_refs, far_outs, near_refs = refs[:4], refs[4:9], refs[9:13]
        part_ref, a_ref, t_ref, sems, out_ref, high_ref, low_ref, sum_ref, out_sems = refs[13:]
        copies = [
            pltpu.make_async_copy(near, far, out_sems.at[i])
            for i, (near, far) in enumerate(zip((out_ref, gram_in, high_ref, low_ref, sum_ref), far_outs))
        ]
        copies[1].start()
        basis_ref, dual_ref, coarse_ref, right_ref = near_refs
        wait = stream(far_refs, near_refs, sems)
        a_ref[...] = a_in[...]
        t_ref[...] = t_in[...]
        eliminate(a_ref, t_ref, steps)
        for k, here in enumerate(tiles):
            wait(k)
            dual = split(dual_ref[here, :].T)
            masked = blocks_masked(pattern_ref, basis_ref[here, :], k * (TILE // BLK))
            for hand, to_ref, columns in (
                (masked, part_ref, slice(0, rank)),
                (coarse_ref[here, :], sum_ref, slice(0, rank)),
                (right_ref[here, :], sum_ref, slice(rank, rank + nrhs)),
            ):
                part = dot3(dual, split(hand), ((1,), (0,)))
                to_ref[:, columns] = part if k == 0 else to_ref[:, columns] + part
        high_ref[...], low_ref[...] = split(part_ref[...])
        for copy in copies[2:]:
            copy.start()
        for here in row_tiles(rank):
            for at in range(0, rank, LANE):
                to = slice(at, at + LANE)
                out_ref[to, here] = (t_ref[here, to] * scale_in[here, :]).T
        copies[0].start()
        for copy in copies:
            copy.wait()

    return call(
        kernel,
        [pattern, a, t, scale, gram, *arrays],
        [t.shape, gram.shape, *halves(a.shape), (rank, rank + nrhs)],
        [*(array.shape for array in arrays), *[a.shape] * 3, pltpu.SemaphoreType.DMA((4, len(tiles))), t.shape]
        + [pltpu.VMEM(a.shape, jnp.bfloat16)] * 2
        + [(rank, rank + nrhs), pltpu.SemaphoreType.DMA((5,))],
        scalars=1,
        flops=flops,
        far_in=range(5, 9),
        far_out=range(5),
    )


def halves(shape):
    return [jax.ShapeDtypeStruct(shape, jnp.bfloat16)] * 2


def split(value):
    high = value.astype(jnp.bfloat16)
    return high, (value - high.astype(jnp.float32)).astype(jnp.bfloat16)


def dot3(left, right, dims):
    part = lambda a, b: lax.dot_general(a, b, (dims, ((), ())), preferred_element_type=jnp.float32)
    return part(left[0], right[0]) + (part(left[0], right[1]) + part(left[1], right[0]))


def blocks_masked(pattern_ref, basis, at):
    rows = []
    for i in range(basis.shape[0] // BLK):
        here = basis[BLK * i : BLK * (i + 1), :]
        row = [
            here[:, BLK * j : BLK * (j + 1)] * pattern_ref[at + i, j].astype(jnp.float32)
            for j in range(basis.shape[1] // BLK)
        ]
        rows.append(jnp.concatenate(row, axis=1))
    return jnp.concatenate(rows, axis=0)


def fine_gram(pattern, basis, dual):
    rows, rank = basis.shape
    pieces = cuts(rank, PIECES)
    tiles = row_tiles(rows)

    def kernel(pattern_ref, basis_far, dual_far, *refs):
        out_refs, (basis_ref, dual_ref, sum_ref, sems) = refs[:-4], refs[-4:]
        wait = stream((basis_far, dual_far), (basis_ref, dual_ref), sems)
        for t, here in enumerate(tiles):
            wait(t)
            masked = blocks_masked(pattern_ref, basis_ref[here, :], t * (TILE // BLK))
            part = contract(dual_ref[here, :], masked)
            sum_ref[...] = part if t == 0 else sum_ref[...] + part
        for piece, out_ref in zip(pieces, out_refs):
            out_ref[...] = sum_ref[piece, :]

    return call(
        kernel,
        [pattern, basis, dual],
        [(piece.stop - piece.start, rank) for piece in pieces],
        [basis.shape, dual.shape, (rank, rank), pltpu.SemaphoreType.DMA((2, len(tiles)))],
        scalars=1,
        flops=12 * rows * rank * rank,
        far_in=(1, 2),
        limit=STREAM_LIMIT,
    )


def fine_moment(dual, coarse, right, cuts):
    rows, rank = dual.shape
    width = rank + right.shape[1]
    tiles = row_tiles(rows)

    def kernel(dual_far, coarse_far, right_far, *refs):
        out_refs, (dual_ref, coarse_ref, right_ref, sum_ref, sems) = refs[:-5], refs[-5:]
        wait = stream((dual_far, coarse_far, right_far), (dual_ref, coarse_ref, right_ref), sems)
        for t, here in enumerate(tiles):
            wait(t)
            left = split(dual_ref[here, :])
            for hand, columns in ((coarse_ref, slice(0, rank)), (right_ref, slice(rank, width))):
                part = dot3(left, split(hand[here, :]), ((0,), (0,)))
                sum_ref[:, columns] = part if t == 0 else sum_ref[:, columns] + part
        for low, high, out_ref in zip(cuts, cuts[1:], out_refs):
            out_ref[...] = sum_ref[low:high, :]

    return call(
        kernel,
        [dual, coarse, right],
        [(high - low, width) for low, high in zip(cuts, cuts[1:])],
        [dual.shape, coarse.shape, right.shape, (rank, width), pltpu.SemaphoreType.DMA((3, len(tiles)))],
        flops=6 * rows * rank * width,
        far_in=(0, 1, 2),
        limit=STREAM_LIMIT,
    )


def coarse_sent(core, inverse, gram, own, sib, part, total, flops):
    rank = gram.shape[0]
    half, width = rank // 2, total.shape[1]
    count = len(own)

    def kernel(core_ref, *refs):
        own_refs, sib_refs, fars = refs[:count], refs[count : 2 * count], refs[2 * count : 2 * count + 5]
        high_ref, low_ref, send_ref, own_ref, far_ref = refs[2 * count + 5 : 2 * count + 10]
        nears, sems = refs[2 * count + 10 : -1], refs[-1]
        gram_ref, inv_ref, part_high, part_low, total_ref = nears
        sent = pl.ds(pl.multiple_of((1 - core_ref[0]) * half, half), half)
        copies = [
            pltpu.make_async_copy(far if i < 2 else far.at[sent, :], near, sems.at[i])
            for i, (far, near) in enumerate(zip(fars, nears))
        ]
        for copy in copies:
            copy.start()
        gather_rows(own_refs, own_ref)
        gather_rows(sib_refs, far_ref)
        copies[0].wait()
        target = far_ref[...] - dot3(split(gram_ref[...]), split(own_ref[...]), ((1,), (0,)))
        copies[1].wait()
        coeffs = split(product(inv_ref[...], target))
        high_ref[...], low_ref[...] = coeffs
        for copy in copies[2:]:
            copy.wait()
        send_ref[...] = total_ref[...] - dot3((part_high[...], part_low[...]), coeffs, ((1,), (0,)))

    half_part = pltpu.VMEM((half, rank), jnp.bfloat16)
    return call(
        kernel,
        [core, *own, *sib, gram, inverse, *part, total],
        [*halves((rank, width)), (half, width)],
        [(rank, width)] * 2
        + [gram.shape, inverse.shape, half_part, half_part, (half, width), pltpu.SemaphoreType.DMA((5,))],
        scalars=1,
        flops=flops,
        far_in=range(1 + 2 * count, 6 + 2 * count),
    )


def coarse_kept(core, coeffs, part, total, flops):
    rank, width = total.shape
    half = rank // 2

    def kernel(core_ref, high_ref, low_ref, *refs):
        fars, keep_ref, nears, sems = refs[:3], refs[3], refs[4:7], refs[7]
        kept = pl.ds(pl.multiple_of(core_ref[0] * half, half), half)
        copies = [
            pltpu.make_async_copy(far.at[kept, :], near, sems.at[i]) for i, (far, near) in enumerate(zip(fars, nears))
        ]
        for copy in copies:
            copy.start()
        for copy in copies:
            copy.wait()
        coeffs = high_ref[...], low_ref[...]
        keep_ref[...] = nears[2][...] - dot3((nears[0][...], nears[1][...]), coeffs, ((1,), (0,)))

    half_part = pltpu.VMEM((half, rank), jnp.bfloat16)
    return call(
        kernel,
        [core, *coeffs, *part, total],
        [(half, width)],
        [half_part, half_part, (half, width), pltpu.SemaphoreType.DMA((3,))],
        scalars=1,
        flops=flops,
        far_in=(3, 4, 5),
    )[0]


def fine_update(pattern, basis, coarse, right, coeffs, flops):
    rows, rank = basis.shape
    nrhs = right.shape[1]

    def kernel(pattern_ref, basis_ref, coarse_ref, right_ref, *refs):
        coeff_refs, (new_ref, updated_ref) = refs[:-2], refs[-2:]
        for t, here in enumerate(row_tiles(rows)):
            masked = split(blocks_masked(pattern_ref, basis_ref[here, :], t * (TILE // BLK)))
            at = 0
            for high_ref, low_ref in zip(coeff_refs[::2], coeff_refs[1::2]):
                less = dot3(masked, (high_ref[...], low_ref[...]), ((1,), (0,)))
                for i in range(0, less.shape[1], BLK):
                    old_ref, to_ref, start = (
                        (coarse_ref, new_ref, at + i) if at + i < rank else (right_ref, updated_ref, at + i - rank)
                    )
                    to = slice(start, start + BLK)
                    to_ref[here, to] = old_ref[here, to] - less[:, i : i + BLK]
                at += less.shape[1]

    return call(
        kernel,
        [pattern, basis, coarse, right, *[half for pair in coeffs for half in pair]],
        [(rows, rank), (rows, nrhs)],
        scalars=1,
        flops=flops,
    )


def top_half(core, mine, other, far_mine, far_other, basis):
    count = len(mine)
    half, width = sum(piece.shape[0] for piece in mine), mine[0].shape[1]
    rank = 2 * half
    nrhs = width - rank
    rows = basis[0].shape[0]

    def kernel(core_ref, *refs):
        lists = [refs[count * i : count * (i + 1)] for i in range(4)]
        basis_refs = refs[4 * count : 4 * count + len(basis)]
        out_ref, whole_basis, own_ref, far_ref, c_ref, a_ref, t_ref, sems = refs[4 * count + len(basis) :]
        copies, at = [], 0
        for i, part in enumerate(basis_refs):
            there = whole_basis.at[:, at : at + part.shape[1]]
            copies.append(pltpu.make_async_copy(part, there, sems.at[i]))
            copies[-1].start()
            at += part.shape[1]
        for first, second, whole_ref in ((*lists[:2], own_ref), (*lists[2:], far_ref)):
            for side, pieces in ((core_ref[0], first), (1 - core_ref[0], second)):
                at = 0
                for part in pieces:
                    rows_here = pl.ds(pl.multiple_of(side * half + at, SUB), part.shape[0])
                    whole_ref[rows_here, :] = part[...]
                    at += part.shape[0]
        c_ref[...], scale = unit_rows(identity_less(product(far_ref[:, :rank], own_ref[:, :rank])))
        t_ref[...] = scale[:, :nrhs] * (far_ref[:, rank:] - product(far_ref[:, :rank], own_ref[:, rank:]))
        a_ref[...] = dot(c_ref[...], c_ref[...], ((1,), (1,)))
        eliminate(a_ref, t_ref, range(rank // LANE))
        here = pl.ds(pl.multiple_of(core_ref[0] * half, half), half)
        out_ref[...] = contract(c_ref[:, here], t_ref[...])
        for copy in copies:
            copy.wait()

    square, wide = (rank, rank), (rank, width)
    return call(
        kernel,
        [core, *mine, *other, *far_mine, *far_other, *basis],
        [(half, nrhs), (rows, rank)],
        [wide, wide, square, square, (rank, nrhs), pltpu.SemaphoreType.DMA((len(basis),))],
        scalars=1,
        flops=1 << 34,
        far_out=(1,),
    )


def final_update(core, mine, other, basis, updated):
    half, nrhs = mine.shape
    rows = updated.shape[0]
    tiles = row_tiles(rows)

    def kernel(core_ref, mine_ref, other_ref, *refs):
        basis_refs, (updated_ref, out_far, coeffs_ref, out_ref, sems) = refs[:-5], refs[-5:]
        for side, part in ((core_ref[0], mine_ref), (1 - core_ref[0], other_ref)):
            coeffs_ref[pl.ds(pl.multiple_of(side * half, half), half), :] = part[...]
        copies = []
        for t, here in enumerate(tiles):
            total, at = updated_ref[here, :], 0
            for part in basis_refs:
                coeffs = split(coeffs_ref[at : at + part.shape[1], :])
                total = total - dot3(split(part[here, :]), coeffs, ((1,), (0,)))
                at += part.shape[1]
            out_ref[here, :] = total
            copies.append(pltpu.make_async_copy(out_ref.at[here, :], out_far.at[here, :], sems.at[t]))
            copies[-1].start()
        for copy in copies:
            copy.wait()

    return call(
        kernel,
        [core, mine, other, *basis, updated],
        [(rows, nrhs)],
        [(2 * half, nrhs), (rows, nrhs), pltpu.SemaphoreType.DMA((len(tiles),))],
        scalars=1,
        flops=12 * rows * half * nrhs,
        far_out=(0,),
    )[0]


def swapped(value, axis, distance):
    mask = 2**distance
    pairs = [(source, source ^ mask) for source in range(lax.axis_size(axis))]
    return lax.ppermute(value, axis, pairs)


def after(value, *others):
    return lax.optimization_barrier((value, *others))[0]


def hop_count(axis):
    return 2 * (lax.axis_size(axis) // 2) - 1


def hop_pairs(axis, hop):
    size = lax.axis_size(axis)
    half = size // 2
    if hop == half - 1:
        return [(half - 1, half), (half, half - 1)]
    if hop < half - 1:
        return [(hop, hop + 1), (size - 1 - hop, size - 2 - hop)]
    t = 2 * half - 2 - hop
    return [(t + 1, t), (size - 2 - t, size - 1 - t)]


def leave(value, axis, hop):
    return lax.ppermute(value, axis, hop_pairs(axis, hop))


def arrive(value, arrived, axis, hop):
    size = lax.axis_size(axis)
    if hop < size // 2:
        return value + arrived
    here = lax.axis_index(axis)
    t = 2 * (size // 2) - 2 - hop
    return jnp.where((here == t) | (here == size - 1 - t), arrived, value)


def line_hops(values, axis, first, last, lag=None):
    values = list(values)
    for hop in range(first, last):
        moved = []
        for i, value in enumerate(values):
            if lag and i >= lag and hop == hop_count(axis) // 2:
                value = after(value, moved[i - lag])
            moved.append(arrive(value, leave(value, axis, hop), axis, hop))
        values = moved
    return values


def cross(value, hop):
    return arrive(value, leave(value, "row", hop), "row", hop)


def shards(basis_fine, dual_fine, basis_coarse, dual_coarse, right_side, pattern):
    rank, nrhs = basis_fine.shape[1], right_side.shape[1]
    half = rank // 2
    hops = hop_count("row")
    middle = hops // 2 + 1
    core = (lax.axis_index("sib") % 2)[None]

    gram = fine_gram(pattern, basis_fine, dual_fine)
    moment = fine_moment(after(dual_fine, gram[0]), basis_coarse, right_side, [0, rank * 9 // 16, rank])
    leaving = [leave(piece, "row", 0) for piece in gram]
    gram = lax.optimization_barrier((*gram, *moment))[: len(gram)]
    gram = [arrive(piece, arrived, "row", 0) for piece, arrived in zip(gram, leaving)]
    gram = line_hops(gram, "row", 1, middle)
    first, second = moment
    first, second = after(first, gram[2]), after(second, gram[2])
    second_flying = leave(second, "row", 0)
    for hop in range(middle - 1):
        first = cross(first, hop)
    gram = line_hops(gram, "row", middle, hops)
    gram_sib = [swapped(piece, "sib", 0) for piece in gram]
    first_flying = leave(first, "row", middle - 1)
    *gram, first = lax.optimization_barrier((*gram, first))
    normal, solved, scale, gram_sib = fine_open(gram, gram_sib, range(1), 1 << 24)

    first, second, normal = lax.optimization_barrier((first, second, normal))
    second = arrive(second, second_flying, "row", 0)
    for hop in range(1, middle - 1):
        second = cross(second, hop)
    first = arrive(first, first_flying, "row", middle - 1)
    normal, first, second = lax.optimization_barrier((normal, first, second))
    second_flying, first_flying = leave(second, "row", middle - 1), leave(first, "row", middle)
    normal, solved, scale, gram_sib = fine_steps(normal, solved, scale, gram_sib, range(1, 3), 1 << 24)

    first, second, normal = lax.optimization_barrier((first, second, normal))
    second = arrive(second, second_flying, "row", middle - 1)
    second, normal = lax.optimization_barrier((second, normal))
    second_flying = leave(second, "row", middle)
    inverse, gram_sib, *part, total = fine_close(
        pattern, normal, solved, scale, gram_sib, range(3, rank // LANE),
        [basis_fine, dual_coarse, basis_coarse, right_side], 1 << 24,
    )
    first, second, inverse = lax.optimization_barrier((first, second, inverse))
    first = arrive(first, first_flying, "row", middle)
    second = arrive(second, second_flying, "row", middle)
    moment = [first, second]
    for hop in range(middle + 1, hops):
        moment = [cross(value, hop) for value in moment]
    moment_sib = [swapped(piece, "sib", 0) for piece in moment]

    *coeffs, send = coarse_sent(core, inverse, gram_sib, moment, moment_sib, part, total, 1 << 28)
    keep = coarse_kept(core, coeffs, part, total, 1 << 24)
    whole = keep + swapped(send, "sib", 0)
    parts = lax.optimization_barrier([whole[piece, :] for piece in cuts(half, PIECES)])
    parts = line_hops(parts, "row", 0, middle, lag=2)
    coeffs[0] = after(coeffs[0], *parts)
    coeffs = [coeffs]
    new, updated = fine_update(pattern, basis_fine, basis_coarse, right_side, coeffs, 1 << 32)
    far = [after(swapped(value, "sib", 1), new) for value in parts]
    parts_other = [swapped(value, "sib", 0) for value in parts]
    far_other = [swapped(value, "sib", 0) for value in far]
    basis = [new]
    result, whole_basis = top_half(core, parts, parts_other, far, far_other, basis)
    result = line_hops([result], "row", middle, hops)[0]
    solution = final_update(core, result, swapped(result, "sib", 0), basis, updated)
    return (whole_basis, solution)


def solution(mesh):
    rows = P(("grp", "sib", "row"), None)
    return jax.shard_map(
        shards,
        mesh=mesh,
        in_specs=(rows,) * 6,
        out_specs=(rows, rows),
        check_vma=False,
    )
```

```python
import jax
import jax.numpy as jnp
from jax import lax
from jax.experimental import pallas as pl
from jax.experimental.pallas import tpu as pltpu
from jax.sharding import PartitionSpec as P

BLK = 128
SUB, LANE, PANEL = 8, 128, 32
PIECES = 3
TILE = 256
HIGH = lax.Precision.HIGHEST
WHOLE = pl.BlockSpec(memory_space=pltpu.VMEM)
FAR = pl.BlockSpec(memory_space=pltpu.HBM)
SCALARS = pl.BlockSpec(memory_space=pltpu.SMEM)
VMEM_LIMIT = 20 << 20
STREAM_LIMIT = 62 << 20


def dot(left, right, dims):
    return lax.dot_general(left, right, (dims, ((), ())), precision=HIGH, preferred_element_type=jnp.float32)


def product(left, right):
    return dot(left, right, ((1,), (0,)))


def contract(left, right):
    return dot(left, right, ((0,), (0,)))


def inverse_of(value):
    guess = pl.reciprocal(value, approx=True)
    guess = guess * (2.0 - value * guess)
    return guess * (2.0 - value * guess)


def sub_panel(panel, first, down, across, lane):
    rows = [down(panel, i) for i in range(SUB)]
    entry = {(i, j): across(rows[i], first + j) for i in range(SUB) for j in range(i + 1)}
    inside = (lane >= first) & (lane < first + SUB)
    rows = [jnp.where(inside, jnp.where(lane == first + i, 1.0, 0.0), row) for i, row in enumerate(rows)]
    lower, ends = {}, {}
    for s in range(0, SUB, 2):
        low, mid, high = entry[s, s], entry[s + 1, s], entry[s + 1, s + 1]
        scale = inverse_of(low * high - mid * mid)
        ends[s] = high * scale, -mid * scale, low * scale
        for i in range(s + 2, SUB):
            first_part, second_part = entry[i, s], entry[i, s + 1]
            lower[i, s] = first_part * ends[s][0] + second_part * ends[s][1]
            lower[i, s + 1] = first_part * ends[s][1] + second_part * ends[s][2]
        for i in range(s + 2, SUB):
            for j in range(s + 2, i + 1):
                entry[i, j] = entry[i, j] - (lower[i, s] * entry[j, s] + lower[i, s + 1] * entry[j, s + 1])
        for i in range(s + 2, SUB):
            rows[i] = rows[i] - (lower[i, s] * rows[s] + lower[i, s + 1] * rows[s + 1])
    for s in reversed(range(0, SUB, 2)):
        one, two = rows[s], rows[s + 1]
        rows[s] = ends[s][0] * one + ends[s][1] * two
        rows[s + 1] = ends[s][1] * one + ends[s][2] * two
        for at in (s, s + 1):
            for i in range(s + 2, SUB, 2):
                rows[at] = rows[at] - (lower[i, at] * rows[i] + lower[i + 1, at] * rows[i + 1])
    return rows


def block_inverse(block):
    size = block.shape[0]
    shape = (SUB, size)
    sub = lax.broadcasted_iota(jnp.int32, shape, 0)
    lane = lax.broadcasted_iota(jnp.int32, shape, 1)
    groups, tall = size // SUB, PANEL // SUB
    rows = [block[SUB * g : SUB * (g + 1), :] for g in range(groups)]
    down = lambda value, at: jnp.broadcast_to(value[at : at + 1, :], shape)
    across = lambda value, at: jnp.broadcast_to(value[:, at : at + 1], shape)
    for start in range(0, groups, tall):
        within = range(start, start + tall)
        ahead = range(start + tall, min(start + 2 * tall, groups))
        before = list(rows)
        for g in within:
            first = SUB * g
            tops = sub_panel(rows[g], first, down, across, lane)
            panel = tops[0]
            for i in range(1, SUB):
                panel = jnp.where(sub == i, tops[i], panel)
            rows[g] = panel
            inside = (lane >= first) & (lane < first + SUB)
            for h in [*within, *ahead]:
                if h != g:
                    terms = [across(rows[h], first + j) * tops[j] for j in range(SUB)]
                    while len(terms) > 1:
                        terms = [terms[i] + terms[i + 1] for i in range(0, len(terms), 2)]
                    rows[h] = jnp.where(inside, 0.0, rows[h]) - terms[0]
        inside = (lane >= SUB * start) & (lane < SUB * (start + tall))
        zero = jnp.zeros(shape, jnp.float32)
        others = [h for h in range(groups) if h not in within and h not in ahead]
        side = [jnp.where(inside, before[h], 0.0) for h in others]
        top = [rows[h] if h in within else zero for h in range(groups)]
        less = product(jnp.concatenate(side, axis=0), jnp.concatenate(top, axis=0))
        for i, h in enumerate(others):
            rows[h] = jnp.where(inside, 0.0, before[h]) - less[SUB * i : SUB * (i + 1), :]
    return jnp.concatenate(rows, axis=0)


def eliminate(a_ref, t_ref, steps):
    rank = a_ref.shape[0]
    blocks = rank // LANE
    at = lambda j: slice(LANE * j, LANE * (j + 1))
    block = a_ref[at(steps[0]), at(steps[0])]
    for j in steps:
        inv = block_inverse(block)
        others = [i for i in range(j + 1, blocks)] + [i for i in range(j)]
        sides = {i: a_ref[at(i), at(j)] for i in others}
        if j < blocks - 1:
            top = product(inv, a_ref[at(j), at(j + 1)])
            block = a_ref[at(j + 1), at(j + 1)] - product(sides[j + 1], top)
            a_ref[at(j), at(j + 1)] = top
            a_ref[at(j + 1), at(j + 1)] = block
            for i in others[1:]:
                a_ref[at(i), at(j + 1)] = a_ref[at(i), at(j + 1)] - product(sides[i], top)
        if j < blocks - 2:
            rest = slice(LANE * (j + 2), rank)
            top = product(inv, a_ref[at(j), rest])
            a_ref[at(j), rest] = top
            for i in others:
                a_ref[at(i), rest] = a_ref[at(i), rest] - product(sides[i], top)
        top = product(inv, t_ref[at(j), :])
        t_ref[at(j), :] = top
        for i in others:
            t_ref[at(i), :] = t_ref[at(i), :] - product(sides[i], top)


def unit_rows(value):
    scale = lax.rsqrt(jnp.sum(value * value, axis=1, keepdims=True))
    return value * scale, jnp.broadcast_to(scale, (value.shape[0], LANE))


def identity_less(value):
    row = lax.broadcasted_iota(jnp.int32, value.shape, 0)
    col = lax.broadcasted_iota(jnp.int32, value.shape, 1)
    return jnp.where(row == col, 1.0, 0.0) - value


def call(kernel, inputs, outputs, scratch=(), scalars=0, flops=0, far_in=(), far_out=(), limit=VMEM_LIMIT):
    return pl.pallas_call(
        kernel,
        out_shape=[
            jax.ShapeDtypeStruct(shape, jnp.float32) if isinstance(shape, tuple) else shape for shape in outputs
        ],
        in_specs=[SCALARS if i < scalars else FAR if i in far_in else WHOLE for i in range(len(inputs))],
        out_specs=[FAR if i in far_out else WHOLE for i in range(len(outputs))],
        scratch_shapes=[
            pltpu.VMEM(shape, jnp.float32) if isinstance(shape, tuple) else shape for shape in scratch
        ],
        cost_estimate=pl.CostEstimate(flops=flops, bytes_accessed=8 << 20, transcendentals=0),
        compiler_params=pltpu.CompilerParams(vmem_limit_bytes=limit),
    )(*inputs)


def cuts(rows, count):
    step = -(-rows // count // 16) * 16 if rows % (16 * count) else rows // count
    return [slice(low, min(low + step, rows)) for low in range(0, rows, step)]


def row_tiles(rows):
    return [slice(TILE * t, TILE * (t + 1)) for t in range(rows // TILE)]


def stream(far_refs, near_refs, sems):
    tiles = row_tiles(far_refs[0].shape[0])
    copies = [
        [pltpu.make_async_copy(far.at[here, :], near.at[here, :], sems.at[i, t])
         for i, (far, near) in enumerate(zip(far_refs, near_refs))]
        for t, here in enumerate(tiles)
    ]
    for tile in copies:
        for copy in tile:
            copy.start()

    def wait(t):
        for copy in copies[t]:
            copy.wait()

    return wait


def gather_rows(pieces, whole_ref):
    at = 0
    for piece in pieces:
        whole_ref[at : at + piece.shape[0], :] = piece[...]
        at += piece.shape[0]


def fine_open(own, sib, steps, flops):
    rank = own[0].shape[1]
    count = len(own)

    def kernel(*refs):
        own_refs, sib_refs = refs[:count], refs[count : 2 * count]
        a_ref, t_ref, scale_ref, far_ref, own_ref = refs[2 * count :]
        gather_rows(own_refs, own_ref)
        gather_rows(sib_refs, far_ref)
        t_ref[...], scale_ref[...] = unit_rows(identity_less(product(far_ref[...], own_ref[...])))
        a_ref[...] = dot(t_ref[...], t_ref[...], ((1,), (1,)))
        eliminate(a_ref, t_ref, steps)

    square = (rank, rank)
    return call(kernel, [*own, *sib], [square, square, (rank, LANE), square], [square], flops=flops)


def fine_steps(a, t, scale, gram, steps, flops):
    def kernel(a_in, t_in, scale_in, gram_in, a_ref, t_ref, scale_ref, gram_ref):
        a_ref[...] = a_in[...]
        t_ref[...] = t_in[...]
        scale_ref[...] = scale_in[...]
        gram_ref[...] = gram_in[...]
        eliminate(a_ref, t_ref, steps)

    arrays = [a, t, scale, gram]
    return call(kernel, arrays, [array.shape for array in arrays], flops=flops)


def fine_close(pattern, a, t, scale, gram, steps, arrays, flops):
    rank = a.shape[0]
    rows, nrhs = arrays[3].shape
    tiles = row_tiles(rows)

    def kernel(pattern_ref, a_in, t_in, scale_in, gram_in, *refs):
        far_refs, far_outs, near_refs = refs[:4], refs[4:9], refs[9:13]
        part_ref, a_ref, t_ref, sems, out_ref, high_ref, low_ref, sum_ref, out_sems = refs[13:]
        copies = [
            pltpu.make_async_copy(near, far, out_sems.at[i])
            for i, (near, far) in enumerate(zip((out_ref, gram_in, high_ref, low_ref, sum_ref), far_outs))
        ]
        copies[1].start()
        basis_ref, dual_ref, coarse_ref, right_ref = near_refs
        wait = stream(far_refs, near_refs, sems)
        a_ref[...] = a_in[...]
        t_ref[...] = t_in[...]
        eliminate(a_ref, t_ref, steps)
        for k, here in enumerate(tiles):
            wait(k)
            dual = split(dual_ref[here, :].T)
            masked = blocks_masked(pattern_ref, basis_ref[here, :], k * (TILE // BLK))
            for hand, to_ref, columns in (
                (masked, part_ref, slice(0, rank)),
                (coarse_ref[here, :], sum_ref, slice(0, rank)),
                (right_ref[here, :], sum_ref, slice(rank, rank + nrhs)),
            ):
                part = dot3(dual, split(hand), ((1,), (0,)))
                to_ref[:, columns] = part if k == 0 else to_ref[:, columns] + part
        high_ref[...], low_ref[...] = split(part_ref[...])
        for copy in copies[2:]:
            copy.start()
        for here in row_tiles(rank):
            for at in range(0, rank, LANE):
                to = slice(at, at + LANE)
                out_ref[to, here] = (t_ref[here, to] * scale_in[here, :]).T
        copies[0].start()
        for copy in copies:
            copy.wait()

    return call(
        kernel,
        [pattern, a, t, scale, gram, *arrays],
        [t.shape, gram.shape, *halves(a.shape), (rank, rank + nrhs)],
        [*(array.shape for array in arrays), *[a.shape] * 3, pltpu.SemaphoreType.DMA((4, len(tiles))), t.shape]
        + [pltpu.VMEM(a.shape, jnp.bfloat16)] * 2
        + [(rank, rank + nrhs), pltpu.SemaphoreType.DMA((5,))],
        flops=flops,
        far_in=range(5, 9),
        far_out=range(5),
    )


def halves(shape):
    return [jax.ShapeDtypeStruct(shape, jnp.bfloat16)] * 2


def split(value):
    high = value.astype(jnp.bfloat16)
    return high, (value - high.astype(jnp.float32)).astype(jnp.bfloat16)


def dot3(left, right, dims):
    part = lambda a, b: lax.dot_general(a, b, (dims, ((), ())), preferred_element_type=jnp.float32)
    return part(left[0], right[0]) + (part(left[0], right[1]) + part(left[1], right[0]))


def blocks_masked(pattern_ref, basis, at):
    present, rows = pattern_ref[...].astype(jnp.float32), []
    for i in range(basis.shape[0] // BLK):
        here = basis[BLK * i : BLK * (i + 1), :]
        row = [
            here[:, BLK * j : BLK * (j + 1)] * present[j : j + 1, at + i : at + i + 1]
            for j in range(basis.shape[1] // BLK)
        ]
        rows.append(jnp.concatenate(row, axis=1))
    return jnp.concatenate(rows, axis=0)


def fine_gram(pattern, basis, dual):
    rows, rank = basis.shape
    pieces = cuts(rank, PIECES)
    tiles = row_tiles(rows)

    def kernel(pattern_ref, basis_far, dual_far, *refs):
        out_refs, (basis_ref, dual_ref, sum_ref, sems) = refs[:-4], refs[-4:]
        wait = stream((basis_far, dual_far), (basis_ref, dual_ref), sems)
        for t, here in enumerate(tiles):
            wait(t)
            masked = blocks_masked(pattern_ref, basis_ref[here, :], t * (TILE // BLK))
            part = contract(dual_ref[here, :], masked)
            sum_ref[...] = part if t == 0 else sum_ref[...] + part
        for piece, out_ref in zip(pieces, out_refs):
            out_ref[...] = sum_ref[piece, :]

    return call(
        kernel,
        [pattern, basis, dual],
        [(piece.stop - piece.start, rank) for piece in pieces],
        [basis.shape, dual.shape, (rank, rank), pltpu.SemaphoreType.DMA((2, len(tiles)))],
        flops=12 * rows * rank * rank,
        far_in=(1, 2),
        limit=STREAM_LIMIT,
    )


def fine_moment(dual, coarse, right, cuts):
    rows, rank = dual.shape
    width = rank + right.shape[1]
    tiles = row_tiles(rows)

    def kernel(dual_far, coarse_far, right_far, *refs):
        out_refs, (dual_ref, coarse_ref, right_ref, sum_ref, sems) = refs[:-5], refs[-5:]
        wait = stream((dual_far, coarse_far, right_far), (dual_ref, coarse_ref, right_ref), sems)
        for t, here in enumerate(tiles):
            wait(t)
            left = split(dual_ref[here, :])
            for hand, columns in ((coarse_ref, slice(0, rank)), (right_ref, slice(rank, width))):
                part = dot3(left, split(hand[here, :]), ((0,), (0,)))
                sum_ref[:, columns] = part if t == 0 else sum_ref[:, columns] + part
        for low, high, out_ref in zip(cuts, cuts[1:], out_refs):
            out_ref[...] = sum_ref[low:high, :]

    return call(
        kernel,
        [dual, coarse, right],
        [(high - low, width) for low, high in zip(cuts, cuts[1:])],
        [dual.shape, coarse.shape, right.shape, (rank, width), pltpu.SemaphoreType.DMA((3, len(tiles)))],
        flops=6 * rows * rank * width,
        far_in=(0, 1, 2),
        limit=STREAM_LIMIT,
    )


def coarse_sent(core, inverse, gram, own, sib, part, total, flops):
    rank = gram.shape[0]
    half, width = rank // 2, total.shape[1]
    count = len(own)

    def kernel(core_ref, *refs):
        own_refs, sib_refs, fars = refs[:count], refs[count : 2 * count], refs[2 * count : 2 * count + 5]
        high_ref, low_ref, send_ref, own_ref, far_ref = refs[2 * count + 5 : 2 * count + 10]
        nears, sems = refs[2 * count + 10 : -1], refs[-1]
        gram_ref, inv_ref, part_high, part_low, total_ref = nears
        sent = pl.ds(pl.multiple_of((1 - core_ref[0]) * half, half), half)
        copies = [
            pltpu.make_async_copy(far if i < 2 else far.at[sent, :], near, sems.at[i])
            for i, (far, near) in enumerate(zip(fars, nears))
        ]
        for copy in copies:
            copy.start()
        gather_rows(own_refs, own_ref)
        gather_rows(sib_refs, far_ref)
        copies[0].wait()
        target = far_ref[...] - dot3(split(gram_ref[...]), split(own_ref[...]), ((1,), (0,)))
        copies[1].wait()
        coeffs = split(product(inv_ref[...], target))
        high_ref[...], low_ref[...] = coeffs
        for copy in copies[2:]:
            copy.wait()
        send_ref[...] = total_ref[...] - dot3((part_high[...], part_low[...]), coeffs, ((1,), (0,)))

    half_part = pltpu.VMEM((half, rank), jnp.bfloat16)
    return call(
        kernel,
        [core, *own, *sib, gram, inverse, *part, total],
        [*halves((rank, width)), (half, width)],
        [(rank, width)] * 2
        + [gram.shape, inverse.shape, half_part, half_part, (half, width), pltpu.SemaphoreType.DMA((5,))],
        scalars=1,
        flops=flops,
        far_in=range(1 + 2 * count, 6 + 2 * count),
    )


def coarse_kept(core, coeffs, part, total, flops):
    rank, width = total.shape
    half = rank // 2

    def kernel(core_ref, high_ref, low_ref, *refs):
        fars, keep_ref, nears, sems = refs[:3], refs[3], refs[4:7], refs[7]
        kept = pl.ds(pl.multiple_of(core_ref[0] * half, half), half)
        copies = [
            pltpu.make_async_copy(far.at[kept, :], near, sems.at[i]) for i, (far, near) in enumerate(zip(fars, nears))
        ]
        for copy in copies:
            copy.start()
        for copy in copies:
            copy.wait()
        coeffs = high_ref[...], low_ref[...]
        keep_ref[...] = nears[2][...] - dot3((nears[0][...], nears[1][...]), coeffs, ((1,), (0,)))

    half_part = pltpu.VMEM((half, rank), jnp.bfloat16)
    return call(
        kernel,
        [core, *coeffs, *part, total],
        [(half, width)],
        [half_part, half_part, (half, width), pltpu.SemaphoreType.DMA((3,))],
        scalars=1,
        flops=flops,
        far_in=(3, 4, 5),
    )[0]


def fine_update(pattern, basis, coarse, right, coeffs, flops):
    rows, rank = basis.shape
    nrhs = right.shape[1]

    def kernel(pattern_ref, basis_ref, coarse_ref, right_ref, *refs):
        coeff_refs, (new_ref, updated_ref) = refs[:-2], refs[-2:]
        for t, here in enumerate(row_tiles(rows)):
            masked = split(blocks_masked(pattern_ref, basis_ref[here, :], t * (TILE // BLK)))
            at = 0
            for high_ref, low_ref in zip(coeff_refs[::2], coeff_refs[1::2]):
                less = dot3(masked, (high_ref[...], low_ref[...]), ((1,), (0,)))
                for i in range(0, less.shape[1], BLK):
                    old_ref, to_ref, start = (
                        (coarse_ref, new_ref, at + i) if at + i < rank else (right_ref, updated_ref, at + i - rank)
                    )
                    to = slice(start, start + BLK)
                    to_ref[here, to] = old_ref[here, to] - less[:, i : i + BLK]
                at += less.shape[1]

    return call(
        kernel,
        [pattern, basis, coarse, right, *[half for pair in coeffs for half in pair]],
        [(rows, rank), (rows, nrhs)],
        flops=flops,
    )


def top_half(core, mine, other, far_mine, far_other, basis):
    count = len(mine)
    half, width = sum(piece.shape[0] for piece in mine), mine[0].shape[1]
    rank = 2 * half
    nrhs = width - rank
    rows = basis[0].shape[0]

    def kernel(core_ref, *refs):
        lists = [refs[count * i : count * (i + 1)] for i in range(4)]
        basis_refs = refs[4 * count : 4 * count + len(basis)]
        out_ref, whole_basis, own_ref, far_ref, c_ref, a_ref, t_ref, sems = refs[4 * count + len(basis) :]
        copies, at = [], 0
        for i, part in enumerate(basis_refs):
            there = whole_basis.at[:, at : at + part.shape[1]]
            copies.append(pltpu.make_async_copy(part, there, sems.at[i]))
            copies[-1].start()
            at += part.shape[1]
        for first, second, whole_ref in ((*lists[:2], own_ref), (*lists[2:], far_ref)):
            for side, pieces in ((core_ref[0], first), (1 - core_ref[0], second)):
                at = 0
                for part in pieces:
                    rows_here = pl.ds(pl.multiple_of(side * half + at, SUB), part.shape[0])
                    whole_ref[rows_here, :] = part[...]
                    at += part.shape[0]
        c_ref[...], scale = unit_rows(identity_less(product(far_ref[:, :rank], own_ref[:, :rank])))
        t_ref[...] = scale[:, :nrhs] * (far_ref[:, rank:] - product(far_ref[:, :rank], own_ref[:, rank:]))
        a_ref[...] = dot(c_ref[...], c_ref[...], ((1,), (1,)))
        eliminate(a_ref, t_ref, range(rank // LANE))
        here = pl.ds(pl.multiple_of(core_ref[0] * half, half), half)
        out_ref[...] = contract(c_ref[:, here], t_ref[...])
        for copy in copies:
            copy.wait()

    square, wide = (rank, rank), (rank, width)
    return call(
        kernel,
        [core, *mine, *other, *far_mine, *far_other, *basis],
        [(half, nrhs), (rows, rank)],
        [wide, wide, square, square, (rank, nrhs), pltpu.SemaphoreType.DMA((len(basis),))],
        scalars=1,
        flops=1 << 34,
        far_out=(1,),
    )


def final_update(core, mine, other, basis, updated):
    half, nrhs = mine.shape
    rows = updated.shape[0]
    tiles = row_tiles(rows)

    def kernel(core_ref, mine_ref, other_ref, *refs):
        basis_refs, (updated_ref, out_far, coeffs_ref, out_ref, sems) = refs[:-5], refs[-5:]
        for side, part in ((core_ref[0], mine_ref), (1 - core_ref[0], other_ref)):
            coeffs_ref[pl.ds(pl.multiple_of(side * half, half), half), :] = part[...]
        copies = []
        for t, here in enumerate(tiles):
            total, at = updated_ref[here, :], 0
            for part in basis_refs:
                coeffs = split(coeffs_ref[at : at + part.shape[1], :])
                total = total - dot3(split(part[here, :]), coeffs, ((1,), (0,)))
                at += part.shape[1]
            out_ref[here, :] = total
            copies.append(pltpu.make_async_copy(out_ref.at[here, :], out_far.at[here, :], sems.at[t]))
            copies[-1].start()
        for copy in copies:
            copy.wait()

    return call(
        kernel,
        [core, mine, other, *basis, updated],
        [(rows, nrhs)],
        [(2 * half, nrhs), (rows, nrhs), pltpu.SemaphoreType.DMA((len(tiles),))],
        scalars=1,
        flops=12 * rows * half * nrhs,
        far_out=(0,),
    )[0]


def swapped(value, axis, distance):
    mask = 2**distance
    pairs = [(source, source ^ mask) for source in range(lax.axis_size(axis))]
    return lax.ppermute(value, axis, pairs)


def after(value, *others):
    return lax.optimization_barrier((value, *others))[0]


def hop_count(axis):
    return 2 * (lax.axis_size(axis) // 2) - 1


def hop_pairs(axis, hop):
    size = lax.axis_size(axis)
    half = size // 2
    if hop == half - 1:
        return [(half - 1, half), (half, half - 1)]
    if hop < half - 1:
        return [(hop, hop + 1), (size - 1 - hop, size - 2 - hop)]
    t = 2 * half - 2 - hop
    return [(t + 1, t), (size - 2 - t, size - 1 - t)]


def leave(value, axis, hop):
    return lax.ppermute(value, axis, hop_pairs(axis, hop))


def arrive(value, arrived, axis, hop):
    size = lax.axis_size(axis)
    if hop < size // 2:
        return value + arrived
    here = lax.axis_index(axis)
    t = 2 * (size // 2) - 2 - hop
    return jnp.where((here == t) | (here == size - 1 - t), arrived, value)


def line_hops(values, axis, first, last, lag=None):
    values = list(values)
    for hop in range(first, last):
        moved = []
        for i, value in enumerate(values):
            if lag and i >= lag and hop == hop_count(axis) // 2:
                value = after(value, moved[i - lag])
            moved.append(arrive(value, leave(value, axis, hop), axis, hop))
        values = moved
    return values


def cross(value, hop):
    return arrive(value, leave(value, "row", hop), "row", hop)


def shards(basis_fine, dual_fine, basis_coarse, dual_coarse, right_side, pattern):
    rank, nrhs = basis_fine.shape[1], right_side.shape[1]
    half = rank // 2
    hops = hop_count("row")
    middle = hops // 2 + 1
    core = (lax.axis_index("sib") % 2)[None]
    pattern = pattern.T

    gram = fine_gram(pattern, basis_fine, dual_fine)
    moment = fine_moment(after(dual_fine, gram[0]), basis_coarse, right_side, [0, rank * 9 // 16, rank])
    leaving = [leave(piece, "row", 0) for piece in gram]
    gram = lax.optimization_barrier((*gram, *moment))[: len(gram)]
    gram = [arrive(piece, arrived, "row", 0) for piece, arrived in zip(gram, leaving)]
    gram = line_hops(gram, "row", 1, middle)
    first, second = moment
    first, second = after(first, gram[2]), after(second, gram[2])
    second_flying = leave(second, "row", 0)
    for hop in range(middle - 1):
        first = cross(first, hop)
    gram = line_hops(gram, "row", middle, hops)
    gram_sib = [swapped(piece, "sib", 0) for piece in gram]
    first_flying = leave(first, "row", middle - 1)
    *gram, first = lax.optimization_barrier((*gram, first))
    normal, solved, scale, gram_sib = fine_open(gram, gram_sib, range(1), 1 << 24)

    first, second, normal = lax.optimization_barrier((first, second, normal))
    second = arrive(second, second_flying, "row", 0)
    for hop in range(1, middle - 1):
        second = cross(second, hop)
    first = arrive(first, first_flying, "row", middle - 1)
    normal, first, second = lax.optimization_barrier((normal, first, second))
    second_flying, first_flying = leave(second, "row", middle - 1), leave(first, "row", middle)
    normal, solved, scale, gram_sib = fine_steps(normal, solved, scale, gram_sib, range(1, 3), 1 << 24)

    first, second, normal = lax.optimization_barrier((first, second, normal))
    second = arrive(second, second_flying, "row", middle - 1)
    second, normal = lax.optimization_barrier((second, normal))
    second_flying = leave(second, "row", middle)
    inverse, gram_sib, *part, total = fine_close(
        pattern, normal, solved, scale, gram_sib, range(3, rank // LANE),
        [basis_fine, dual_coarse, basis_coarse, right_side], 1 << 24,
    )
    first, second, inverse = lax.optimization_barrier((first, second, inverse))
    first = arrive(first, first_flying, "row", middle)
    second = arrive(second, second_flying, "row", middle)
    moment = [first, second]
    for hop in range(middle + 1, hops):
        moment = [cross(value, hop) for value in moment]
    moment_sib = [swapped(piece, "sib", 0) for piece in moment]

    *coeffs, send = coarse_sent(core, inverse, gram_sib, moment, moment_sib, part, total, 1 << 28)
    keep = coarse_kept(core, coeffs, part, total, 1 << 24)
    whole = keep + swapped(send, "sib", 0)
    parts = lax.optimization_barrier([whole[piece, :] for piece in cuts(half, PIECES)])
    parts = line_hops(parts, "row", 0, middle, lag=2)
    coeffs[0] = after(coeffs[0], *parts)
    coeffs = [coeffs]
    new, updated = fine_update(pattern, basis_fine, basis_coarse, right_side, coeffs, 1 << 32)
    far = [after(swapped(value, "sib", 1), new) for value in parts]
    parts_other = [swapped(value, "sib", 0) for value in parts]
    far_other = [swapped(value, "sib", 0) for value in far]
    basis = [new]
    result, whole_basis = top_half(core, parts, parts_other, far, far_other, basis)
    result = line_hops([result], "row", middle, hops)[0]
    solution = final_update(core, result, swapped(result, "sib", 0), basis, updated)
    return (whole_basis, solution)


def solution(mesh):
    rows = P(("grp", "sib", "row"), None)
    return jax.shard_map(
        shards,
        mesh=mesh,
        in_specs=(rows,) * 6,
        out_specs=(rows, rows),
        check_vma=False,
    )
```

```python
import jax
import jax.numpy as jnp
from jax import lax
from jax.experimental import pallas as pl
from jax.experimental.pallas import tpu as pltpu
from jax.sharding import PartitionSpec as P

BLK = 128
SUB, LANE, PANEL = 8, 128, 32
PIECES = 3
TILE = 256
HIGH = lax.Precision.HIGHEST
WHOLE = pl.BlockSpec(memory_space=pltpu.VMEM)
FAR = pl.BlockSpec(memory_space=pltpu.HBM)
SCALARS = pl.BlockSpec(memory_space=pltpu.SMEM)
VMEM_LIMIT = 14 << 20
STREAM_LIMIT = 62 << 20


def dot(left, right, dims):
    return lax.dot_general(left, right, (dims, ((), ())), precision=HIGH, preferred_element_type=jnp.float32)


def product(left, right):
    return dot(left, right, ((1,), (0,)))


def contract(left, right):
    return dot(left, right, ((0,), (0,)))


def block_inverse(block):
    size = block.shape[0]
    shape = (SUB, size)
    sub = lax.broadcasted_iota(jnp.int32, shape, 0)
    lane = lax.broadcasted_iota(jnp.int32, shape, 1)
    groups, tall = size // SUB, PANEL // SUB
    rows = [block[SUB * g : SUB * (g + 1), :] for g in range(groups)]
    down = lambda value, at: jnp.broadcast_to(value[at : at + 1, :], shape)
    across = lambda value, at: jnp.broadcast_to(value[:, at : at + 1], shape)
    for start in range(0, groups, tall):
        within = range(start, start + tall)
        for g in within:
            first = SUB * g
            panel = rows[g]
            heads = [across(panel, first + j) for j in range(SUB)]
            for s in range(0, SUB, 2):
                pair = heads[s], heads[s + 1]
                mid = down(pair[0], s + 1)
                low, high = down(pair[0], s), down(pair[1], s + 1)
                scale = 1.0 / (low * high - mid * mid)
                ends, cross = (high * scale, low * scale), -mid * scale
                solve = lambda first_row, second_row: (
                    ends[0] * first_row + cross * second_row,
                    cross * first_row + ends[1] * second_row,
                )
                place = lambda value, tops: jnp.where(
                    sub == s,
                    tops[0],
                    jnp.where(sub == s + 1, tops[1], value - pair[0] * tops[0] - pair[1] * tops[1]),
                )
                here = (lane == first + s) | (lane == first + s + 1)
                tops = solve(down(panel, s), down(panel, s + 1))
                tops = (
                    jnp.where(here, jnp.where(lane == first + s, ends[0], cross), tops[0]),
                    jnp.where(here, jnp.where(lane == first + s, cross, ends[1]), tops[1]),
                )
                panel = place(jnp.where(here, 0.0, panel), tops)
                for j in range(s + 2, SUB):
                    heads[j] = place(heads[j], solve(down(heads[j], s), down(heads[j], s + 1)))
            rows[g] = panel
            tops = [down(panel, j) for j in range(SUB)]
            inside = (lane >= first) & (lane < first + SUB)
            for h in within:
                if h != g:
                    terms = [across(rows[h], first + j) * tops[j] for j in range(SUB)]
                    while len(terms) > 1:
                        terms = [terms[i] + terms[i + 1] for i in range(0, len(terms), 2)]
                    rows[h] = jnp.where(inside, 0.0, rows[h]) - terms[0]
        inside = (lane >= SUB * start) & (lane < SUB * (start + tall))
        zero = jnp.zeros(shape, jnp.float32)
        side = [zero if h in within else jnp.where(inside, rows[h], 0.0) for h in range(groups)]
        top = [rows[h] if h in within else zero for h in range(groups)]
        less = product(jnp.concatenate(side, axis=0), jnp.concatenate(top, axis=0))
        for h in range(groups):
            if h not in within:
                rows[h] = jnp.where(inside, 0.0, rows[h]) - less[SUB * h : SUB * (h + 1), :]
    return jnp.concatenate(rows, axis=0)


def eliminate(a_ref, t_ref, steps):
    rank = a_ref.shape[0]
    blocks = rank // LANE
    at = lambda j: slice(LANE * j, LANE * (j + 1))
    for j in steps:
        rest = slice(LANE * (j + 1), rank)
        inv = block_inverse(a_ref[at(j), at(j)])
        others = [i for i in range(j + 1, blocks)] + [i for i in range(j)]
        if j < blocks - 1:
            top = product(inv, a_ref[at(j), rest])
            a_ref[at(j), rest] = top
            for i in others:
                a_ref[at(i), rest] = a_ref[at(i), rest] - product(a_ref[at(i), at(j)], top)
        top = product(inv, t_ref[at(j), :])
        t_ref[at(j), :] = top
        for i in others:
            t_ref[at(i), :] = t_ref[at(i), :] - product(a_ref[at(i), at(j)], top)


def unit_rows(value):
    scale = lax.rsqrt(jnp.sum(value * value, axis=1, keepdims=True))
    return value * scale, jnp.broadcast_to(scale, (value.shape[0], LANE))


def identity_less(value):
    row = lax.broadcasted_iota(jnp.int32, value.shape, 0)
    col = lax.broadcasted_iota(jnp.int32, value.shape, 1)
    return jnp.where(row == col, 1.0, 0.0) - value


def call(kernel, inputs, outputs, scratch=(), scalars=0, flops=0, far_in=(), far_out=(), limit=VMEM_LIMIT):
    return pl.pallas_call(
        kernel,
        out_shape=[
            jax.ShapeDtypeStruct(shape, jnp.float32) if isinstance(shape, tuple) else shape for shape in outputs
        ],
        in_specs=[SCALARS if i < scalars else FAR if i in far_in else WHOLE for i in range(len(inputs))],
        out_specs=[FAR if i in far_out else WHOLE for i in range(len(outputs))],
        scratch_shapes=[
            pltpu.VMEM(shape, jnp.float32) if isinstance(shape, tuple) else shape for shape in scratch
        ],
        cost_estimate=pl.CostEstimate(flops=flops, bytes_accessed=8 << 20, transcendentals=0),
        compiler_params=pltpu.CompilerParams(vmem_limit_bytes=limit),
    )(*inputs)


def cuts(rows, count):
    step = -(-rows // count // 16) * 16 if rows % (16 * count) else rows // count
    return [slice(low, min(low + step, rows)) for low in range(0, rows, step)]


def row_tiles(rows):
    return [slice(TILE * t, TILE * (t + 1)) for t in range(rows // TILE)]


def stream(far_refs, near_refs, sems):
    tiles = row_tiles(far_refs[0].shape[0])
    copies = [
        [pltpu.make_async_copy(far.at[here, :], near.at[here, :], sems.at[i, t])
         for i, (far, near) in enumerate(zip(far_refs, near_refs))]
        for t, here in enumerate(tiles)
    ]
    for tile in copies:
        for copy in tile:
            copy.start()

    def wait(t):
        for copy in copies[t]:
            copy.wait()

    return wait


def gather_rows(pieces, whole_ref):
    at = 0
    for piece in pieces:
        whole_ref[at : at + piece.shape[0], :] = piece[...]
        at += piece.shape[0]


def fine_open(own, sib, steps, flops):
    rank = own[0].shape[1]
    count = len(own)

    def kernel(*refs):
        own_refs, sib_refs = refs[:count], refs[count : 2 * count]
        a_ref, t_ref, scale_ref, far_ref, own_ref = refs[2 * count :]
        gather_rows(own_refs, own_ref)
        gather_rows(sib_refs, far_ref)
        t_ref[...], scale_ref[...] = unit_rows(identity_less(product(far_ref[...], own_ref[...])))
        a_ref[...] = dot(t_ref[...], t_ref[...], ((1,), (1,)))
        eliminate(a_ref, t_ref, steps)

    square = (rank, rank)
    return call(kernel, [*own, *sib], [square, square, (rank, LANE), square], [square], flops=flops)


def fine_steps(a, t, scale, gram, steps, flops):
    def kernel(a_in, t_in, scale_in, gram_in, a_ref, t_ref, scale_ref, gram_ref):
        a_ref[...] = a_in[...]
        t_ref[...] = t_in[...]
        scale_ref[...] = scale_in[...]
        gram_ref[...] = gram_in[...]
        eliminate(a_ref, t_ref, steps)

    arrays = [a, t, scale, gram]
    return call(kernel, arrays, [array.shape for array in arrays], flops=flops)


def fine_close(pattern, a, t, scale, gram, steps, arrays, flops):
    rank = a.shape[0]
    rows, nrhs = arrays[3].shape
    tiles = row_tiles(rows)

    def kernel(pattern_ref, a_in, t_in, scale_in, gram_in, *refs):
        (basis_ref, dual_ref, coarse_ref, right_ref), (out_ref, gram_ref, high_ref, low_ref, sum_ref) = refs[:4], refs[4:9]
        part_ref, a_ref, t_ref = refs[9:]
        gram_ref[...] = gram_in[...]
        a_ref[...] = a_in[...]
        t_ref[...] = t_in[...]
        eliminate(a_ref, t_ref, steps)
        for k, here in enumerate(tiles):
            dual = split(dual_ref[here, :].T)
            masked = blocks_masked(pattern_ref, basis_ref[here, :], k * (TILE // BLK))
            for hand, to_ref, columns in (
                (masked, part_ref, slice(0, rank)),
                (coarse_ref[here, :], sum_ref, slice(0, rank)),
                (right_ref[here, :], sum_ref, slice(rank, rank + nrhs)),
            ):
                part = dot3(dual, split(hand), ((1,), (0,)))
                to_ref[:, columns] = part if k == 0 else to_ref[:, columns] + part
        high_ref[...], low_ref[...] = split(part_ref[...])
        for here in row_tiles(rank):
            for at in range(0, rank, LANE):
                to = slice(at, at + LANE)
                out_ref[to, here] = (t_ref[here, to] * scale_in[here, :]).T

    return call(
        kernel,
        [pattern, a, t, scale, gram, *arrays],
        [t.shape, gram.shape, *halves(a.shape), (rank, rank + nrhs)],
        [a.shape] * 3,
        flops=flops,
    )


def halves(shape):
    return [jax.ShapeDtypeStruct(shape, jnp.bfloat16)] * 2


def split(value):
    high = value.astype(jnp.bfloat16)
    return high, (value - high.astype(jnp.float32)).astype(jnp.bfloat16)


def dot3(left, right, dims):
    part = lambda a, b: lax.dot_general(a, b, (dims, ((), ())), preferred_element_type=jnp.float32)
    return part(left[0], right[0]) + (part(left[0], right[1]) + part(left[1], right[0]))


def blocks_masked(pattern_ref, basis, at):
    present, rows = pattern_ref[...].astype(jnp.float32), []
    for i in range(basis.shape[0] // BLK):
        here = basis[BLK * i : BLK * (i + 1), :]
        row = [
            here[:, BLK * j : BLK * (j + 1)] * present[j : j + 1, at + i : at + i + 1]
            for j in range(basis.shape[1] // BLK)
        ]
        rows.append(jnp.concatenate(row, axis=1))
    return jnp.concatenate(rows, axis=0)


def fine_gram(pattern, basis, dual):
    rows, rank = basis.shape
    pieces = cuts(rank, PIECES)
    tiles = row_tiles(rows)

    def kernel(pattern_ref, basis_far, dual_far, *refs):
        out_refs, (basis_ref, dual_ref, sum_ref, sems) = refs[:-4], refs[-4:]
        wait = stream((basis_far, dual_far), (basis_ref, dual_ref), sems)
        for t, here in enumerate(tiles):
            wait(t)
            masked = blocks_masked(pattern_ref, basis_ref[here, :], t * (TILE // BLK))
            part = contract(dual_ref[here, :], masked)
            sum_ref[...] = part if t == 0 else sum_ref[...] + part
        for piece, out_ref in zip(pieces, out_refs):
            out_ref[...] = sum_ref[piece, :]

    return call(
        kernel,
        [pattern, basis, dual],
        [(piece.stop - piece.start, rank) for piece in pieces],
        [basis.shape, dual.shape, (rank, rank), pltpu.SemaphoreType.DMA((2, len(tiles)))],
        flops=12 * rows * rank * rank,
        far_in=(1, 2),
        limit=STREAM_LIMIT,
    )


def fine_moment(dual, coarse, right, cuts):
    rows, rank = dual.shape
    width = rank + right.shape[1]
    tiles = row_tiles(rows)

    def kernel(dual_far, coarse_far, right_far, *refs):
        out_refs, (dual_ref, coarse_ref, right_ref, sum_ref, sems) = refs[:-5], refs[-5:]
        wait = stream((dual_far, coarse_far, right_far), (dual_ref, coarse_ref, right_ref), sems)
        for t, here in enumerate(tiles):
            wait(t)
            left = split(dual_ref[here, :])
            for hand, columns in ((coarse_ref, slice(0, rank)), (right_ref, slice(rank, width))):
                part = dot3(left, split(hand[here, :]), ((0,), (0,)))
                sum_ref[:, columns] = part if t == 0 else sum_ref[:, columns] + part
        for low, high, out_ref in zip(cuts, cuts[1:], out_refs):
            out_ref[...] = sum_ref[low:high, :]

    return call(
        kernel,
        [dual, coarse, right],
        [(high - low, width) for low, high in zip(cuts, cuts[1:])],
        [dual.shape, coarse.shape, right.shape, (rank, width), pltpu.SemaphoreType.DMA((3, len(tiles)))],
        flops=6 * rows * rank * width,
        far_in=(0, 1, 2),
        limit=STREAM_LIMIT,
    )


def coarse_sent(core, inverse, gram, own, sib, part, total, flops):
    rank = gram.shape[0]
    half, width = rank // 2, total.shape[1]
    count = len(own)

    def kernel(core_ref, *refs):
        own_refs, sib_refs = refs[:count], refs[count : 2 * count]
        gram_ref, inv_ref, part_high, part_low, total_ref = refs[2 * count : 2 * count + 5]
        high_ref, low_ref, send_ref, own_ref, far_ref = refs[2 * count + 5 :]
        sent = pl.ds(pl.multiple_of((1 - core_ref[0]) * half, half), half)
        gather_rows(own_refs, own_ref)
        gather_rows(sib_refs, far_ref)
        target = far_ref[...] - dot3(split(gram_ref[...]), split(own_ref[...]), ((1,), (0,)))
        coeffs = split(product(inv_ref[...], target))
        high_ref[...], low_ref[...] = coeffs
        send_ref[...] = total_ref[sent, :] - dot3((part_high[sent, :], part_low[sent, :]), coeffs, ((1,), (0,)))

    return call(
        kernel,
        [core, *own, *sib, gram, inverse, *part, total],
        [*halves((rank, width)), (half, width)],
        [(rank, width)] * 2,
        scalars=1,
        flops=flops,
    )


def coarse_kept(core, coeffs, part, total, flops):
    rank, width = total.shape
    half = rank // 2

    def kernel(core_ref, high_ref, low_ref, part_high, part_low, total_ref, keep_ref):
        kept = pl.ds(pl.multiple_of(core_ref[0] * half, half), half)
        coeffs = high_ref[...], low_ref[...]
        keep_ref[...] = total_ref[kept, :] - dot3((part_high[kept, :], part_low[kept, :]), coeffs, ((1,), (0,)))

    return call(kernel, [core, *coeffs, *part, total], [(half, width)], scalars=1, flops=flops)[0]


def fine_update(pattern, basis, coarse, right, coeffs, flops):
    rows, rank = basis.shape
    nrhs = right.shape[1]

    def kernel(pattern_ref, basis_ref, coarse_ref, right_ref, *refs):
        coeff_refs, (new_ref, updated_ref) = refs[:-2], refs[-2:]
        for t, here in enumerate(row_tiles(rows)):
            masked = split(blocks_masked(pattern_ref, basis_ref[here, :], t * (TILE // BLK)))
            at = 0
            for high_ref, low_ref in zip(coeff_refs[::2], coeff_refs[1::2]):
                less = dot3(masked, (high_ref[...], low_ref[...]), ((1,), (0,)))
                for i in range(0, less.shape[1], BLK):
                    old_ref, to_ref, start = (
                        (coarse_ref, new_ref, at + i) if at + i < rank else (right_ref, updated_ref, at + i - rank)
                    )
                    to = slice(start, start + BLK)
                    to_ref[here, to] = old_ref[here, to] - less[:, i : i + BLK]
                at += less.shape[1]

    return call(
        kernel,
        [pattern, basis, coarse, right, *[half for pair in coeffs for half in pair]],
        [(rows, rank), (rows, nrhs)],
        flops=flops,
    )


def top_half(core, mine, other, far_mine, far_other, basis):
    count = len(mine)
    half, width = sum(piece.shape[0] for piece in mine), mine[0].shape[1]
    rank = 2 * half
    nrhs = width - rank
    rows = basis[0].shape[0]

    def kernel(core_ref, *refs):
        lists = [refs[count * i : count * (i + 1)] for i in range(4)]
        basis_refs = refs[4 * count : 4 * count + len(basis)]
        out_ref, whole_basis, own_ref, far_ref, c_ref, a_ref, t_ref, sems = refs[4 * count + len(basis) :]
        copies, at = [], 0
        for i, part in enumerate(basis_refs):
            there = whole_basis.at[:, at : at + part.shape[1]]
            copies.append(pltpu.make_async_copy(part, there, sems.at[i]))
            copies[-1].start()
            at += part.shape[1]
        for first, second, whole_ref in ((*lists[:2], own_ref), (*lists[2:], far_ref)):
            for side, pieces in ((core_ref[0], first), (1 - core_ref[0], second)):
                at = 0
                for part in pieces:
                    rows_here = pl.ds(pl.multiple_of(side * half + at, SUB), part.shape[0])
                    whole_ref[rows_here, :] = part[...]
                    at += part.shape[0]
        c_ref[...], scale = unit_rows(identity_less(product(far_ref[:, :rank], own_ref[:, :rank])))
        t_ref[...] = scale[:, :nrhs] * (far_ref[:, rank:] - product(far_ref[:, :rank], own_ref[:, rank:]))
        a_ref[...] = dot(c_ref[...], c_ref[...], ((1,), (1,)))
        eliminate(a_ref, t_ref, range(rank // LANE))
        here = pl.ds(pl.multiple_of(core_ref[0] * half, half), half)
        out_ref[...] = contract(c_ref[:, here], t_ref[...])
        for copy in copies:
            copy.wait()

    square, wide = (rank, rank), (rank, width)
    return call(
        kernel,
        [core, *mine, *other, *far_mine, *far_other, *basis],
        [(half, nrhs), (rows, rank)],
        [wide, wide, square, square, (rank, nrhs), pltpu.SemaphoreType.DMA((len(basis),))],
        scalars=1,
        flops=1 << 34,
        far_out=(1,),
    )


def final_update(core, mine, other, basis, updated):
    half, nrhs = mine.shape
    rows = updated.shape[0]
    tiles = row_tiles(rows)

    def kernel(core_ref, mine_ref, other_ref, *refs):
        basis_refs, (updated_ref, out_far, coeffs_ref, out_ref, sems) = refs[:-5], refs[-5:]
        for side, part in ((core_ref[0], mine_ref), (1 - core_ref[0], other_ref)):
            coeffs_ref[pl.ds(pl.multiple_of(side * half, half), half), :] = part[...]
        copies = []
        for t, here in enumerate(tiles):
            total, at = updated_ref[here, :], 0
            for part in basis_refs:
                coeffs = split(coeffs_ref[at : at + part.shape[1], :])
                total = total - dot3(split(part[here, :]), coeffs, ((1,), (0,)))
                at += part.shape[1]
            out_ref[here, :] = total
            copies.append(pltpu.make_async_copy(out_ref.at[here, :], out_far.at[here, :], sems.at[t]))
            copies[-1].start()
        for copy in copies:
            copy.wait()

    return call(
        kernel,
        [core, mine, other, *basis, updated],
        [(rows, nrhs)],
        [(2 * half, nrhs), (rows, nrhs), pltpu.SemaphoreType.DMA((len(tiles),))],
        scalars=1,
        flops=12 * rows * half * nrhs,
        far_out=(0,),
    )[0]


def swapped(value, axis, distance):
    mask = 2**distance
    pairs = [(source, source ^ mask) for source in range(lax.axis_size(axis))]
    return lax.ppermute(value, axis, pairs)


def after(value, *others):
    return lax.optimization_barrier((value, *others))[0]


def hop_count(axis):
    return 2 * (lax.axis_size(axis) // 2) - 1


def hop_pairs(axis, hop):
    size = lax.axis_size(axis)
    half = size // 2
    if hop == half - 1:
        return [(half - 1, half), (half, half - 1)]
    if hop < half - 1:
        return [(hop, hop + 1), (size - 1 - hop, size - 2 - hop)]
    t = 2 * half - 2 - hop
    return [(t + 1, t), (size - 2 - t, size - 1 - t)]


def leave(value, axis, hop):
    return lax.ppermute(value, axis, hop_pairs(axis, hop))


def arrive(value, arrived, axis, hop):
    size = lax.axis_size(axis)
    if hop < size // 2:
        return value + arrived
    here = lax.axis_index(axis)
    t = 2 * (size // 2) - 2 - hop
    return jnp.where((here == t) | (here == size - 1 - t), arrived, value)


def line_hops(values, axis, first, last, lag=None):
    values = list(values)
    for hop in range(first, last):
        moved = []
        for i, value in enumerate(values):
            if lag and i >= lag and hop == hop_count(axis) // 2:
                value = after(value, moved[i - lag])
            moved.append(arrive(value, leave(value, axis, hop), axis, hop))
        values = moved
    return values


def cross(value, hop):
    return arrive(value, leave(value, "row", hop), "row", hop)


def shards(basis_fine, dual_fine, basis_coarse, dual_coarse, right_side, pattern):
    rank, nrhs = basis_fine.shape[1], right_side.shape[1]
    half = rank // 2
    hops = hop_count("row")
    middle = hops // 2 + 1
    core = (lax.axis_index("sib") % 2)[None]
    pattern = pattern.T

    gram = fine_gram(pattern, basis_fine, dual_fine)
    moment = fine_moment(after(dual_fine, gram[0]), basis_coarse, right_side, [0, rank * 9 // 16, rank])
    leaving = [leave(piece, "row", 0) for piece in gram]
    gram = lax.optimization_barrier((*gram, *moment))[: len(gram)]
    gram = [arrive(piece, arrived, "row", 0) for piece, arrived in zip(gram, leaving)]
    gram = line_hops(gram, "row", 1, middle)
    over = gram
    gram = line_hops(gram, "row", middle, hops)
    first, second = after(moment[0], over[2]), after(moment[1], over[2])
    second_flying = leave(second, "row", 0)
    for hop in range(middle - 1):
        first = cross(first, hop)
    gram_sib = [swapped(piece, "sib", 0) for piece in gram]
    first_flying = leave(first, "row", middle - 1)
    *gram, first = lax.optimization_barrier((*gram, first))
    normal, solved, scale, gram_sib = fine_open(gram, gram_sib, range(1), 1 << 24)

    first, second, normal = lax.optimization_barrier((first, second, normal))
    second = arrive(second, second_flying, "row", 0)
    for hop in range(1, middle - 1):
        second = cross(second, hop)
    first = arrive(first, first_flying, "row", middle - 1)
    normal, first, second = lax.optimization_barrier((normal, first, second))
    second_flying, first_flying = leave(second, "row", middle - 1), leave(first, "row", middle)
    normal, solved, scale, gram_sib = fine_steps(normal, solved, scale, gram_sib, range(1, 3), 1 << 24)

    first, second, normal = lax.optimization_barrier((first, second, normal))
    second = arrive(second, second_flying, "row", middle - 1)
    second, normal = lax.optimization_barrier((second, normal))
    second_flying = leave(second, "row", middle)
    inverse, gram_sib, *part, total = fine_close(
        pattern, normal, solved, scale, gram_sib, range(3, rank // LANE),
        [basis_fine, dual_coarse, basis_coarse, right_side], 1 << 24,
    )
    first, second, inverse = lax.optimization_barrier((first, second, inverse))
    first = arrive(first, first_flying, "row", middle)
    second = arrive(second, second_flying, "row", middle)
    moment = [first, second]
    for hop in range(middle + 1, hops):
        moment = [cross(value, hop) for value in moment]
    moment_sib = [swapped(piece, "sib", 0) for piece in moment]

    *coeffs, send = coarse_sent(core, inverse, gram_sib, moment, moment_sib, part, total, 1 << 28)
    keep = coarse_kept(core, coeffs, part, total, 1 << 24)
    whole = keep + swapped(send, "sib", 0)
    parts = lax.optimization_barrier([whole[piece, :] for piece in cuts(half, PIECES)])
    parts = line_hops(parts, "row", 0, middle, lag=2)
    coeffs[0] = after(coeffs[0], *parts)
    coeffs = [coeffs]
    new, updated = fine_update(pattern, basis_fine, basis_coarse, right_side, coeffs, 1 << 32)
    far = [after(swapped(value, "sib", 1), new) for value in parts]
    parts_other = [swapped(value, "sib", 0) for value in parts]
    far_other = [swapped(value, "sib", 0) for value in far]
    basis = [new]
    result, whole_basis = top_half(core, parts, parts_other, far, far_other, basis)
    result = line_hops([result], "row", middle, hops)[0]
    solution = final_update(core, result, swapped(result, "sib", 0), basis, updated)
    return (whole_basis, solution)


def solution(mesh):
    rows = P(("grp", "sib", "row"), None)
    return jax.shard_map(
        shards,
        mesh=mesh,
        in_specs=(rows,) * 6,
        out_specs=(rows, rows),
        check_vma=False,
    )
```

```python
import jax
import jax.numpy as jnp
from jax import lax
from jax.experimental import pallas as pl
from jax.experimental.pallas import tpu as pltpu
from jax.sharding import PartitionSpec as P

BLK = 128
SUB, LANE, PANEL = 8, 128, 32
PIECES = 3
TILE = 256
HIGH = lax.Precision.HIGHEST
WHOLE = pl.BlockSpec(memory_space=pltpu.VMEM)
FAR = pl.BlockSpec(memory_space=pltpu.HBM)
SCALARS = pl.BlockSpec(memory_space=pltpu.SMEM)
VMEM_LIMIT = 14 << 20
STREAM_LIMIT = 62 << 20


def dot(left, right, dims):
    return lax.dot_general(left, right, (dims, ((), ())), precision=HIGH, preferred_element_type=jnp.float32)


def product(left, right):
    return dot(left, right, ((1,), (0,)))


def contract(left, right):
    return dot(left, right, ((0,), (0,)))


def block_inverse(block):
    size = block.shape[0]
    shape = (SUB, size)
    sub = lax.broadcasted_iota(jnp.int32, shape, 0)
    lane = lax.broadcasted_iota(jnp.int32, shape, 1)
    groups, tall = size // SUB, PANEL // SUB
    rows = [block[SUB * g : SUB * (g + 1), :] for g in range(groups)]
    down = lambda value, at: jnp.broadcast_to(value[at : at + 1, :], shape)
    across = lambda value, at: jnp.broadcast_to(value[:, at : at + 1], shape)
    for start in range(0, groups, tall):
        within = range(start, start + tall)
        for g in within:
            first = SUB * g
            panel = rows[g]
            heads = [across(panel, first + j) for j in range(SUB)]
            for s in range(0, SUB, 2):
                pair = heads[s], heads[s + 1]
                mid = down(pair[0], s + 1)
                low, high = down(pair[0], s), down(pair[1], s + 1)
                scale = 1.0 / (low * high - mid * mid)
                ends, cross = (high * scale, low * scale), -mid * scale
                solve = lambda first_row, second_row: (
                    ends[0] * first_row + cross * second_row,
                    cross * first_row + ends[1] * second_row,
                )
                place = lambda value, tops: jnp.where(
                    sub == s,
                    tops[0],
                    jnp.where(sub == s + 1, tops[1], value - pair[0] * tops[0] - pair[1] * tops[1]),
                )
                here = (lane == first + s) | (lane == first + s + 1)
                tops = solve(down(panel, s), down(panel, s + 1))
                tops = (
                    jnp.where(here, jnp.where(lane == first + s, ends[0], cross), tops[0]),
                    jnp.where(here, jnp.where(lane == first + s, cross, ends[1]), tops[1]),
                )
                panel = place(jnp.where(here, 0.0, panel), tops)
                for j in range(s + 2, SUB):
                    heads[j] = place(heads[j], solve(down(heads[j], s), down(heads[j], s + 1)))
            rows[g] = panel
            tops = [down(panel, j) for j in range(SUB)]
            inside = (lane >= first) & (lane < first + SUB)
            for h in within:
                if h != g:
                    terms = [across(rows[h], first + j) * tops[j] for j in range(SUB)]
                    while len(terms) > 1:
                        terms = [terms[i] + terms[i + 1] for i in range(0, len(terms), 2)]
                    rows[h] = jnp.where(inside, 0.0, rows[h]) - terms[0]
        inside = (lane >= SUB * start) & (lane < SUB * (start + tall))
        zero = jnp.zeros(shape, jnp.float32)
        side = [zero if h in within else jnp.where(inside, rows[h], 0.0) for h in range(groups)]
        top = [rows[h] if h in within else zero for h in range(groups)]
        less = product(jnp.concatenate(side, axis=0), jnp.concatenate(top, axis=0))
        for h in range(groups):
            if h not in within:
                rows[h] = jnp.where(inside, 0.0, rows[h]) - less[SUB * h : SUB * (h + 1), :]
    return jnp.concatenate(rows, axis=0)


def eliminate(a_ref, t_ref, steps):
    rank = a_ref.shape[0]
    blocks = rank // LANE
    at = lambda j: slice(LANE * j, LANE * (j + 1))
    for j in steps:
        rest = slice(LANE * (j + 1), rank)
        inv = block_inverse(a_ref[at(j), at(j)])
        others = [i for i in range(j + 1, blocks)] + [i for i in range(j)]
        if j < blocks - 1:
            top = product(inv, a_ref[at(j), rest])
            a_ref[at(j), rest] = top
            for i in others:
                a_ref[at(i), rest] = a_ref[at(i), rest] - product(a_ref[at(i), at(j)], top)
        top = product(inv, t_ref[at(j), :])
        t_ref[at(j), :] = top
        for i in others:
            t_ref[at(i), :] = t_ref[at(i), :] - product(a_ref[at(i), at(j)], top)


def unit_rows(value):
    scale = lax.rsqrt(jnp.sum(value * value, axis=1, keepdims=True))
    return value * scale, jnp.broadcast_to(scale, (value.shape[0], LANE))


def identity_less(value):
    row = lax.broadcasted_iota(jnp.int32, value.shape, 0)
    col = lax.broadcasted_iota(jnp.int32, value.shape, 1)
    return jnp.where(row == col, 1.0, 0.0) - value


def call(kernel, inputs, outputs, scratch=(), scalars=0, flops=0, far_in=(), far_out=(), limit=VMEM_LIMIT):
    return pl.pallas_call(
        kernel,
        out_shape=[
            jax.ShapeDtypeStruct(shape, jnp.float32) if isinstance(shape, tuple) else shape for shape in outputs
        ],
        in_specs=[SCALARS if i < scalars else FAR if i in far_in else WHOLE for i in range(len(inputs))],
        out_specs=[FAR if i in far_out else WHOLE for i in range(len(outputs))],
        scratch_shapes=[
            pltpu.VMEM(shape, jnp.float32) if isinstance(shape, tuple) else shape for shape in scratch
        ],
        cost_estimate=pl.CostEstimate(flops=flops, bytes_accessed=8 << 20, transcendentals=0),
        compiler_params=pltpu.CompilerParams(vmem_limit_bytes=limit),
    )(*inputs)


def cuts(rows, count):
    step = -(-rows // count // 16) * 16 if rows % (16 * count) else rows // count
    return [slice(low, min(low + step, rows)) for low in range(0, rows, step)]


def row_tiles(rows):
    return [slice(TILE * t, TILE * (t + 1)) for t in range(rows // TILE)]


def stream(far_refs, near_refs, sems):
    tiles = row_tiles(far_refs[0].shape[0])
    copies = [
        [pltpu.make_async_copy(far.at[here, :], near.at[here, :], sems.at[i, t])
         for i, (far, near) in enumerate(zip(far_refs, near_refs))]
        for t, here in enumerate(tiles)
    ]
    for tile in copies:
        for copy in tile:
            copy.start()

    def wait(t):
        for copy in copies[t]:
            copy.wait()

    return wait


def gather_rows(pieces, whole_ref):
    at = 0
    for piece in pieces:
        whole_ref[at : at + piece.shape[0], :] = piece[...]
        at += piece.shape[0]


def fine_open(own, sib, steps, flops):
    rank = own[0].shape[1]
    count = len(own)

    def kernel(*refs):
        own_refs, sib_refs = refs[:count], refs[count : 2 * count]
        a_ref, t_ref, scale_ref, far_ref, own_ref = refs[2 * count :]
        gather_rows(own_refs, own_ref)
        gather_rows(sib_refs, far_ref)
        t_ref[...], scale_ref[...] = unit_rows(identity_less(product(far_ref[...], own_ref[...])))
        a_ref[...] = dot(t_ref[...], t_ref[...], ((1,), (1,)))
        eliminate(a_ref, t_ref, steps)

    square = (rank, rank)
    return call(kernel, [*own, *sib], [square, square, (rank, LANE), square], [square], flops=flops)


def fine_steps(a, t, scale, gram, steps, flops):
    def kernel(a_in, t_in, scale_in, gram_in, a_ref, t_ref, scale_ref, gram_ref):
        a_ref[...] = a_in[...]
        t_ref[...] = t_in[...]
        scale_ref[...] = scale_in[...]
        gram_ref[...] = gram_in[...]
        eliminate(a_ref, t_ref, steps)

    arrays = [a, t, scale, gram]
    return call(kernel, arrays, [array.shape for array in arrays], flops=flops)


def fine_close(pattern, a, t, scale, gram, steps, arrays, flops):
    rank = a.shape[0]
    rows, nrhs = arrays[3].shape
    tiles = row_tiles(rows)

    def kernel(pattern_ref, a_in, t_in, scale_in, gram_in, *refs):
        (basis_ref, dual_ref, coarse_ref, right_ref), (out_ref, gram_ref, high_ref, low_ref, sum_ref) = refs[:4], refs[4:9]
        part_ref, a_ref, t_ref = refs[9:]
        gram_ref[...] = gram_in[...]
        a_ref[...] = a_in[...]
        t_ref[...] = t_in[...]
        eliminate(a_ref, t_ref, steps)
        for k, here in enumerate(tiles):
            dual = split(dual_ref[here, :].T)
            masked = blocks_masked(pattern_ref, basis_ref[here, :], k * (TILE // BLK))
            for hand, to_ref, columns in (
                (masked, part_ref, slice(0, rank)),
                (coarse_ref[here, :], sum_ref, slice(0, rank)),
                (right_ref[here, :], sum_ref, slice(rank, rank + nrhs)),
            ):
                part = dot3(dual, split(hand), ((1,), (0,)))
                to_ref[:, columns] = part if k == 0 else to_ref[:, columns] + part
        high_ref[...], low_ref[...] = split(part_ref[...])
        for here in row_tiles(rank):
            for at in range(0, rank, LANE):
                to = slice(at, at + LANE)
                out_ref[to, here] = (t_ref[here, to] * scale_in[here, :]).T

    return call(
        kernel,
        [pattern, a, t, scale, gram, *arrays],
        [t.shape, gram.shape, *halves(a.shape), (rank, rank + nrhs)],
        [a.shape] * 3,
        flops=flops,
    )


def halves(shape):
    return [jax.ShapeDtypeStruct(shape, jnp.bfloat16)] * 2


def split(value):
    high = value.astype(jnp.bfloat16)
    return high, (value - high.astype(jnp.float32)).astype(jnp.bfloat16)


def dot3(left, right, dims):
    part = lambda a, b: lax.dot_general(a, b, (dims, ((), ())), preferred_element_type=jnp.float32)
    return part(left[0], right[0]) + (part(left[0], right[1]) + part(left[1], right[0]))


def blocks_masked(pattern_ref, basis, at):
    present, rows = pattern_ref[...].astype(jnp.float32), []
    for i in range(basis.shape[0] // BLK):
        here = basis[BLK * i : BLK * (i + 1), :]
        row = [
            here[:, BLK * j : BLK * (j + 1)] * present[j : j + 1, at + i : at + i + 1]
            for j in range(basis.shape[1] // BLK)
        ]
        rows.append(jnp.concatenate(row, axis=1))
    return jnp.concatenate(rows, axis=0)


def fine_gram(pattern, basis, dual):
    rows, rank = basis.shape
    pieces = cuts(rank, PIECES)
    tiles = row_tiles(rows)

    def kernel(pattern_ref, basis_far, dual_far, *refs):
        out_refs, (basis_ref, dual_ref, sum_ref, sems) = refs[:-4], refs[-4:]
        wait = stream((basis_far, dual_far), (basis_ref, dual_ref), sems)
        for t, here in enumerate(tiles):
            wait(t)
            masked = blocks_masked(pattern_ref, basis_ref[here, :], t * (TILE // BLK))
            part = contract(dual_ref[here, :], masked)
            sum_ref[...] = part if t == 0 else sum_ref[...] + part
        for piece, out_ref in zip(pieces, out_refs):
            out_ref[...] = sum_ref[piece, :]

    return call(
        kernel,
        [pattern, basis, dual],
        [(piece.stop - piece.start, rank) for piece in pieces],
        [basis.shape, dual.shape, (rank, rank), pltpu.SemaphoreType.DMA((2, len(tiles)))],
        flops=12 * rows * rank * rank,
        far_in=(1, 2),
        limit=STREAM_LIMIT,
    )


def fine_moment(dual, coarse, right, cuts):
    rows, rank = dual.shape
    width = rank + right.shape[1]
    tiles = row_tiles(rows)

    def kernel(dual_far, coarse_far, right_far, *refs):
        out_refs, (dual_ref, coarse_ref, right_ref, sum_ref, sems) = refs[:-5], refs[-5:]
        wait = stream((dual_far, coarse_far, right_far), (dual_ref, coarse_ref, right_ref), sems)
        for t, here in enumerate(tiles):
            wait(t)
            left = split(dual_ref[here, :])
            for hand, columns in ((coarse_ref, slice(0, rank)), (right_ref, slice(rank, width))):
                part = dot3(left, split(hand[here, :]), ((0,), (0,)))
                sum_ref[:, columns] = part if t == 0 else sum_ref[:, columns] + part
        for low, high, out_ref in zip(cuts, cuts[1:], out_refs):
            out_ref[...] = sum_ref[low:high, :]

    return call(
        kernel,
        [dual, coarse, right],
        [(high - low, width) for low, high in zip(cuts, cuts[1:])],
        [dual.shape, coarse.shape, right.shape, (rank, width), pltpu.SemaphoreType.DMA((3, len(tiles)))],
        flops=6 * rows * rank * width,
        far_in=(0, 1, 2),
        limit=STREAM_LIMIT,
    )


def coarse_sent(core, inverse, gram, own, sib, part, total, flops):
    rank = gram.shape[0]
    half, width = rank // 2, total.shape[1]
    count = len(own)

    def kernel(core_ref, *refs):
        own_refs, sib_refs = refs[:count], refs[count : 2 * count]
        gram_ref, inv_ref, part_high, part_low, total_ref = refs[2 * count : 2 * count + 5]
        high_ref, low_ref, send_ref, own_ref, far_ref = refs[2 * count + 5 :]
        sent = pl.ds(pl.multiple_of((1 - core_ref[0]) * half, half), half)
        gather_rows(own_refs, own_ref)
        gather_rows(sib_refs, far_ref)
        target = far_ref[...] - dot3(split(gram_ref[...]), split(own_ref[...]), ((1,), (0,)))
        coeffs = split(dot3(split(inv_ref[...]), split(target), ((1,), (0,))))
        high_ref[...], low_ref[...] = coeffs
        send_ref[...] = total_ref[sent, :] - dot3((part_high[sent, :], part_low[sent, :]), coeffs, ((1,), (0,)))

    return call(
        kernel,
        [core, *own, *sib, gram, inverse, *part, total],
        [*halves((rank, width)), (half, width)],
        [(rank, width)] * 2,
        scalars=1,
        flops=flops,
    )


def coarse_kept(core, coeffs, part, total, flops):
    rank, width = total.shape
    half = rank // 2

    def kernel(core_ref, high_ref, low_ref, part_high, part_low, total_ref, keep_ref):
        kept = pl.ds(pl.multiple_of(core_ref[0] * half, half), half)
        coeffs = high_ref[...], low_ref[...]
        keep_ref[...] = total_ref[kept, :] - dot3((part_high[kept, :], part_low[kept, :]), coeffs, ((1,), (0,)))

    return call(kernel, [core, *coeffs, *part, total], [(half, width)], scalars=1, flops=flops)[0]


def fine_update(pattern, basis, coarse, right, coeffs, flops):
    rows, rank = basis.shape
    nrhs = right.shape[1]

    def kernel(pattern_ref, basis_ref, coarse_ref, right_ref, *refs):
        coeff_refs, (new_ref, updated_ref) = refs[:-2], refs[-2:]
        for t, here in enumerate(row_tiles(rows)):
            masked = split(blocks_masked(pattern_ref, basis_ref[here, :], t * (TILE // BLK)))
            at = 0
            for high_ref, low_ref in zip(coeff_refs[::2], coeff_refs[1::2]):
                less = dot3(masked, (high_ref[...], low_ref[...]), ((1,), (0,)))
                for i in range(0, less.shape[1], BLK):
                    old_ref, to_ref, start = (
                        (coarse_ref, new_ref, at + i) if at + i < rank else (right_ref, updated_ref, at + i - rank)
                    )
                    to = slice(start, start + BLK)
                    to_ref[here, to] = old_ref[here, to] - less[:, i : i + BLK]
                at += less.shape[1]

    return call(
        kernel,
        [pattern, basis, coarse, right, *[half for pair in coeffs for half in pair]],
        [(rows, rank), (rows, nrhs)],
        flops=flops,
    )


def top_half(core, mine, other, far_mine, far_other, basis):
    count = len(mine)
    half, width = sum(piece.shape[0] for piece in mine), mine[0].shape[1]
    rank = 2 * half
    nrhs = width - rank
    rows = basis[0].shape[0]

    def kernel(core_ref, *refs):
        lists = [refs[count * i : count * (i + 1)] for i in range(4)]
        basis_refs = refs[4 * count : 4 * count + len(basis)]
        out_ref, whole_basis, own_ref, far_ref, c_ref, a_ref, t_ref, sems = refs[4 * count + len(basis) :]
        copies, at = [], 0
        for i, part in enumerate(basis_refs):
            there = whole_basis.at[:, at : at + part.shape[1]]
            copies.append(pltpu.make_async_copy(part, there, sems.at[i]))
            copies[-1].start()
            at += part.shape[1]
        for first, second, whole_ref in ((*lists[:2], own_ref), (*lists[2:], far_ref)):
            for side, pieces in ((core_ref[0], first), (1 - core_ref[0], second)):
                at = 0
                for part in pieces:
                    rows_here = pl.ds(pl.multiple_of(side * half + at, SUB), part.shape[0])
                    whole_ref[rows_here, :] = part[...]
                    at += part.shape[0]
        c_ref[...], scale = unit_rows(identity_less(product(far_ref[:, :rank], own_ref[:, :rank])))
        t_ref[...] = scale[:, :nrhs] * (far_ref[:, rank:] - product(far_ref[:, :rank], own_ref[:, rank:]))
        a_ref[...] = dot(c_ref[...], c_ref[...], ((1,), (1,)))
        eliminate(a_ref, t_ref, range(rank // LANE))
        here = pl.ds(pl.multiple_of(core_ref[0] * half, half), half)
        out_ref[...] = contract(c_ref[:, here], t_ref[...])
        for copy in copies:
            copy.wait()

    square, wide = (rank, rank), (rank, width)
    return call(
        kernel,
        [core, *mine, *other, *far_mine, *far_other, *basis],
        [(half, nrhs), (rows, rank)],
        [wide, wide, square, square, (rank, nrhs), pltpu.SemaphoreType.DMA((len(basis),))],
        scalars=1,
        flops=1 << 34,
        far_out=(1,),
    )


def final_update(core, mine, other, basis, updated):
    half, nrhs = mine.shape
    rows = updated.shape[0]
    tiles = row_tiles(rows)

    def kernel(core_ref, mine_ref, other_ref, *refs):
        basis_refs, (updated_ref, out_far, coeffs_ref, out_ref, sems) = refs[:-5], refs[-5:]
        for side, part in ((core_ref[0], mine_ref), (1 - core_ref[0], other_ref)):
            coeffs_ref[pl.ds(pl.multiple_of(side * half, half), half), :] = part[...]
        copies = []
        for t, here in enumerate(tiles):
            total, at = updated_ref[here, :], 0
            for part in basis_refs:
                coeffs = split(coeffs_ref[at : at + part.shape[1], :])
                total = total - dot3(split(part[here, :]), coeffs, ((1,), (0,)))
                at += part.shape[1]
            out_ref[here, :] = total
            copies.append(pltpu.make_async_copy(out_ref.at[here, :], out_far.at[here, :], sems.at[t]))
            copies[-1].start()
        for copy in copies:
            copy.wait()

    return call(
        kernel,
        [core, mine, other, *basis, updated],
        [(rows, nrhs)],
        [(2 * half, nrhs), (rows, nrhs), pltpu.SemaphoreType.DMA((len(tiles),))],
        scalars=1,
        flops=12 * rows * half * nrhs,
        far_out=(0,),
    )[0]


def swapped(value, axis, distance):
    mask = 2**distance
    pairs = [(source, source ^ mask) for source in range(lax.axis_size(axis))]
    return lax.ppermute(value, axis, pairs)


def after(value, *others):
    return lax.optimization_barrier((value, *others))[0]


def hop_count(axis):
    return 2 * (lax.axis_size(axis) // 2) - 1


def hop_pairs(axis, hop):
    size = lax.axis_size(axis)
    half = size // 2
    if hop == half - 1:
        return [(half - 1, half), (half, half - 1)]
    if hop < half - 1:
        return [(hop, hop + 1), (size - 1 - hop, size - 2 - hop)]
    t = 2 * half - 2 - hop
    return [(t + 1, t), (size - 2 - t, size - 1 - t)]


def leave(value, axis, hop):
    return lax.ppermute(value, axis, hop_pairs(axis, hop))


def arrive(value, arrived, axis, hop):
    size = lax.axis_size(axis)
    if hop < size // 2:
        return value + arrived
    here = lax.axis_index(axis)
    t = 2 * (size // 2) - 2 - hop
    return jnp.where((here == t) | (here == size - 1 - t), arrived, value)


def line_hops(values, axis, first, last, lag=None):
    values = list(values)
    for hop in range(first, last):
        moved = []
        for i, value in enumerate(values):
            if lag and i >= lag and hop == hop_count(axis) // 2:
                value = after(value, moved[i - lag])
            moved.append(arrive(value, leave(value, axis, hop), axis, hop))
        values = moved
    return values


def cross(value, hop):
    return arrive(value, leave(value, "row", hop), "row", hop)


def shards(basis_fine, dual_fine, basis_coarse, dual_coarse, right_side, pattern):
    rank, nrhs = basis_fine.shape[1], right_side.shape[1]
    half = rank // 2
    hops = hop_count("row")
    middle = hops // 2 + 1
    core = (lax.axis_index("sib") % 2)[None]
    pattern = pattern.T

    gram = fine_gram(pattern, basis_fine, dual_fine)
    moment = fine_moment(after(dual_fine, gram[0]), basis_coarse, right_side, [0, rank * 9 // 16, rank])
    leaving = [leave(piece, "row", 0) for piece in gram]
    gram = lax.optimization_barrier((*gram, *moment))[: len(gram)]
    gram = [arrive(piece, arrived, "row", 0) for piece, arrived in zip(gram, leaving)]
    gram = line_hops(gram, "row", 1, middle)
    over = gram
    gram = line_hops(gram, "row", middle, hops)
    first, second = after(moment[0], over[2]), after(moment[1], over[2])
    second_flying = leave(second, "row", 0)
    for hop in range(middle - 1):
        first = cross(first, hop)
    gram_sib = [swapped(piece, "sib", 0) for piece in gram]
    first_flying = leave(first, "row", middle - 1)
    *gram, first = lax.optimization_barrier((*gram, first))
    normal, solved, scale, gram_sib = fine_open(gram, gram_sib, range(0), 1 << 24)

    first, second, normal = lax.optimization_barrier((first, second, normal))
    second = arrive(second, second_flying, "row", 0)
    for hop in range(1, middle - 1):
        second = cross(second, hop)
    first = arrive(first, first_flying, "row", middle - 1)
    normal, first, second = lax.optimization_barrier((normal, first, second))
    second_flying, first_flying = leave(second, "row", middle - 1), leave(first, "row", middle)
    normal, solved, scale, gram_sib = fine_steps(normal, solved, scale, gram_sib, range(0, 2), 1 << 24)

    first, second, normal = lax.optimization_barrier((first, second, normal))
    second = arrive(second, second_flying, "row", middle - 1)
    second, normal = lax.optimization_barrier((second, normal))
    second_flying = leave(second, "row", middle)
    normal, solved, scale, gram_sib = fine_steps(normal, solved, scale, gram_sib, range(2, 3), 1 << 24)
    inverse, gram_sib, *part, total = fine_close(
        pattern, normal, solved, scale, gram_sib, range(3, rank // LANE),
        [basis_fine, dual_coarse, basis_coarse, right_side], 1 << 24,
    )
    first, second, inverse = lax.optimization_barrier((first, second, inverse))
    first = arrive(first, first_flying, "row", middle)
    second = arrive(second, second_flying, "row", middle)
    moment = [first, second]
    for hop in range(middle + 1, hops):
        moment = [cross(value, hop) for value in moment]
    moment_sib = [swapped(piece, "sib", 0) for piece in moment]

    *coeffs, send = coarse_sent(core, inverse, gram_sib, moment, moment_sib, part, total, 1 << 28)
    keep = coarse_kept(core, coeffs, part, total, 1 << 24)
    whole = keep + swapped(send, "sib", 0)
    parts = lax.optimization_barrier([whole[piece, :] for piece in cuts(half, PIECES)])
    parts = line_hops(parts, "row", 0, middle, lag=2)
    coeffs[0] = after(coeffs[0], *parts)
    coeffs = [coeffs]
    new, updated = fine_update(pattern, basis_fine, basis_coarse, right_side, coeffs, 1 << 32)
    far = [after(swapped(value, "sib", 1), new) for value in parts]
    parts_other = [swapped(value, "sib", 0) for value in parts]
    far_other = [swapped(value, "sib", 0) for value in far]
    basis = [new]
    result, whole_basis = top_half(core, parts, parts_other, far, far_other, basis)
    result = line_hops([result], "row", middle, hops)[0]
    solution = final_update(core, result, swapped(result, "sib", 0), basis, updated)
    return (whole_basis, solution)


def solution(mesh):
    rows = P(("grp", "sib", "row"), None)
    return jax.shard_map(
        shards,
        mesh=mesh,
        in_specs=(rows,) * 6,
        out_specs=(rows, rows),
        check_vma=False,
    )
```
